32 devices in a mesh: groups: 2 (over y), tm: 16 (over z, x, core).
Axes of the slice: x: 2, y: 2, z: 4, core: 2. Of those that a mesh axis runs over, the one named last changes fastest.
Arguments:
- start_frames: float32 [6, 4, 8, 256], P('groups'), parts along dimension 0, may hold values from -6 to 6
- plan: int32 [32], P(('groups', 'tm')), parts along dimension 0, may hold values from 0 to 999
- noise: float32 [16, 6, 4, 8, 256], P('tm', 'groups'), parts along dimension 1, may hold values from -6 to 6
- w_lift: float32 [3, 128], replicated, may hold values from -3.5 to 3.5
- w_time: float32 [128, 128], replicated, may hold values from -0.75 to 0.75
- spatial: float32 [2, 128, 9], replicated, may hold values from -2 to 2
- temporal: float32 [2, 128, 3], replicated, may hold values from -3.5 to 3.5
- w_point: bfloat16 [2, 128, 128], replicated, may hold values from -0.5 to 0.5
- w_out: float32 [128, 3], replicated, may hold values from -0.5 to 0.5
Outputs:
- trajectory: float32 [16, 6, 4, 8, 256], P('tm', 'groups'), parts along dimension 1
The draws below stay inside these ranges and needn't reach their ends.
There are 2 independent parts, one for each index of `groups`. The reference program is written for one: setup_inputs(seed, part) draws one part's arguments, and reference() takes and returns one part's arrays. A program takes and returns all parts, laid end to end along the dimension named above; an argument that names none is the same for every part. Nothing has to cross between parts.
All inputs are finite; a program needn't handle non-finite values.
Results may differ from the reference program's by a relative error of at most 0.0023.
Values sent between devices are 32-bit elements; how exact they have to be, the bound alone decides.
No kernel may reach another device: no remote copies, remote signals or barrier semaphores. Data moves between devices by JAX's collectives and lax.ppermute only.
A program may use at most 64 MiB of HBM per device.

```python
import math
import jax
import jax.numpy as jnp
from jax import lax

C = 3
HID = 128
F = 4
H = 8
W = 256
ITERS = 2
BLOCKS = 2
TIMES = 16


def touch_ends(entries, key, smallest, high):
    longest = entries.shape.index(max(entries.shape))
    spots = []
    for shift in (0, 1):
        where = [jax.random.randint(jax.random.fold_in(key, axis), (), 0, length) for axis, length in enumerate(entries.shape)]
        where[longest] = (where[longest] + shift) % entries.shape[longest]
        spots.append(tuple(where))
    return entries.at[spots[0]].set(smallest).at[spots[1]].set(high)


def block_scale(own_key, extent, cuts, least, largest):
    def one(position, parts):
        draws = jax.random.uniform(jax.random.fold_in(jax.random.fold_in(own_key, 6), position), (parts,), jnp.float32, least / len(cuts), largest / len(cuts))
        return jnp.repeat(jnp.exp(draws), extent[position] // parts).reshape((-1,) + (1,) * (len(extent) - position - 1))

    gain = one(*cuts[0])
    for cut in cuts[1:]:
        gain = gain * one(*cut)
    return gain


def normal_values(rng, extent, scale, limit, cuts=(), held_as=jnp.bfloat16):
    values = scale * jax.random.normal(rng, extent, jnp.float32)
    if cuts:
        values = values * block_scale(rng, extent, cuts, -0.22, 0.18)
    return jnp.clip(values, -limit, limit).astype(held_as)


def setup_inputs(seed: int = 0, part: int = 0) -> dict:
    seeds = jax.random.split(jax.random.key(seed), 10)
    part_splits = jax.random.split(jax.random.fold_in(seeds[9], part), 10)
    start_frames = normal_values(part_splits[0], (C, F, H, W), 1.0, 6.0, (), jnp.float32)
    plan = touch_ends(jax.random.randint(part_splits[1], (TIMES,), 0, 1000), jax.random.fold_in(part_splits[1], 1), 0, 999).astype(jnp.int32)
    noise = normal_values(part_splits[2], (TIMES, C, F, H, W), 1.0, 6.0, ((0, 16),), jnp.float32)
    w_lift = normal_values(seeds[3], (C, HID), C ** -0.5, 3.5, (), jnp.float32)
    w_time = normal_values(seeds[4], (HID, HID), (HID // 2) ** -0.5, 0.75, (), jnp.float32)
    spatial = normal_values(seeds[5], (BLOCKS, HID, 9), 9 ** -0.5, 2.0, (), jnp.float32)
    temporal = normal_values(seeds[6], (BLOCKS, HID, 3), 3 ** -0.5, 3.5, (), jnp.float32)
    w_point = normal_values(seeds[7], (BLOCKS, HID, HID), HID ** -0.5, 0.5)
    w_out = normal_values(seeds[8], (HID, C), HID ** -0.5, 0.5, (), jnp.float32)
    return {"start_frames": start_frames, "plan": plan, "noise": noise, "w_lift": w_lift, "w_time": w_time, "spatial": spatial, "temporal": temporal, "w_point": w_point, "w_out": w_out}


noise_scale = 2.0

def embedding(step_index, width):
    half_width = width // 2
    column = jnp.arange(half_width, dtype=jnp.float32)
    freqs = jnp.exp(-math.log(1000.0) * column / half_width)
    angles = step_index.astype(jnp.float32) * freqs
    return jnp.concatenate([jnp.sin(angles), jnp.cos(angles)])

def convolve(values, kernel_space, kernel_time):
    frames, rows, columns = (values.shape[1], values.shape[2], values.shape[3])
    padded = jnp.pad(values, ((0, 0), (0, 0), (1, 1), (1, 1)))
    spatial_sum = jnp.zeros_like(values)
    for row_tap in range(3):
        for col_tap in range(3):
            spatial_sum = spatial_sum + kernel_space[:, 3 * row_tap + col_tap, None, None, None] * padded[:, :, row_tap:row_tap + rows, col_tap:col_tap + columns]
    framed = jnp.pad(spatial_sum, ((0, 0), (1, 1), (0, 0), (0, 0)))
    result = jnp.zeros_like(values)
    for frame_tap in range(3):
        result = result + kernel_time[:, frame_tap, None, None, None] * framed[:, frame_tap:frame_tap + frames]
    return result

def network(states, step_index, w_lift, w_time, spatial, temporal, w_point, w_out):
    width = w_time.shape[0]
    shape_cells = states.shape[1:]
    bias = jnp.dot(embedding(step_index, width), w_time, precision=lax.Precision.HIGHEST)
    flat_states = states.reshape(states.shape[0], -1)
    lifted = jnp.dot(w_lift.T, flat_states, precision=lax.Precision.HIGHEST) + bias[:, None]
    features = lifted.astype(jnp.bfloat16)
    for block in range(spatial.shape[0]):
        mixed = convolve(features.astype(jnp.float32).reshape((width,) + shape_cells), spatial[block], temporal[block]).reshape(width, -1)
        root_mean = jnp.sqrt(lax.optimization_barrier(jnp.mean(mixed * mixed, axis=0, keepdims=True)) + 1e-06)
        normed = jax.nn.silu(mixed / root_mean).astype(jnp.bfloat16)
        update = jnp.dot(w_point[block].T, normed, preferred_element_type=jnp.float32)
        features = (features.astype(jnp.float32) + update).astype(jnp.bfloat16)
    output = jnp.dot(w_out.T, features.astype(jnp.float32), precision=lax.Precision.HIGHEST)
    return output.reshape(states.shape)

def reference(start_frames, plan, noise, w_lift, w_time, spatial, temporal, w_point, w_out):
    step_size = 1.0 / TIMES

    def drift_of(items):
        states, step_index, noise_now = items
        value = network(states, step_index, w_lift, w_time, spatial, temporal, w_point, w_out)
        return step_size * value + noise_scale * math.sqrt(step_size) * noise_now
    states_all = jnp.broadcast_to(start_frames[None], noise.shape)
    result = states_all
    for iteration in range(ITERS):
        drifts = lax.map(drift_of, (states_all, plan, noise))
        running = jnp.cumsum(drifts, axis=0)
        if iteration + 1 < ITERS:
            before = jnp.concatenate([jnp.zeros_like(drifts[:1]), running[:-1]], axis=0)
            states_all = start_frames[None] + before
        else:
            result = start_frames[None] + running
    return result
```

```python
import functools
import math

import jax
import jax.numpy as jnp
from jax import lax
from jax.experimental import pallas as pl
from jax.experimental.pallas import tpu as pltpu
from jax.sharding import PartitionSpec as P

ITERS = 2
LANES = 128
SUB = 8
HALO = 2
NOISE_SCALE = 2.0
EPS = 1e-06
F32 = jnp.float32
BF16 = jnp.bfloat16
VMEM_LIMIT = 50 * 1024 * 1024


def round_up(value, multiple):
    return (value + multiple - 1) // multiple * multiple


def whole(memory_space=pltpu.VMEM):
    return pl.BlockSpec(memory_space=memory_space)


def columns_as_rows(image, extra):
    channels, frames, rows, columns = image.shape
    parts = [image[c, f] for f in range(frames) for c in range(channels)]
    left = LANES - channels * frames * rows
    parts.append(jnp.full((left, columns), extra, F32))
    return jnp.transpose(jnp.concatenate(parts, axis=0))


def pack_kernel(shares, share, block, plan_ref, noise_ref, out_ref, padded):
    columns = noise_ref.shape[-1]
    edge = jnp.zeros((SUB, LANES), F32)
    padded[0:SUB, :] = edge
    padded[SUB + columns : 2 * SUB + columns, :] = edge
    padded[SUB : SUB + columns, :] = columns_as_rows(
        noise_ref[0], plan_ref[0].astype(F32)
    )
    for dest in range(shares):
        first = SUB - HALO + dest * share
        out_ref[dest, 0 : share + 2 * HALO, :] = padded[first : first + share + 2 * HALO, :]
        if block > share + 2 * HALO:
            out_ref[dest, share + 2 * HALO : block, :] = jnp.zeros(
                (block - share - 2 * HALO, LANES), F32
            )


def window_of(frame, frames):
    return min(max(frame - 1, 0), frames - 3)


def stack_taps(state, window, group):
    width = 3 * group
    before, here, after = [
        pltpu.roll(s, (LANES - window * group + k * width) % LANES, 1)
        for k, s in enumerate(state)
    ]
    lane = lax.broadcasted_iota(jnp.int32, before.shape, 1)
    first = jnp.where(lane < width, before, here)
    spill = 2 * width - LANES
    second = jnp.where(
        lane < spill, here, jnp.where(lane < spill + width, after, 0.0)
    )
    return jnp.concatenate([first.astype(BF16), second.astype(BF16)], axis=-1)


def prep_kernel(
    share, sizes, index_ref, start_ref, lift_ref, spatial_ref, temporal_ref, out_w_ref,
    mix_ref, taps_ref, lin_ref, edge_ref, own_ref, proj_ref, padded,
):
    channels, frames, rows, columns = sizes
    group = channels * rows
    index = index_ref[0]
    row = lax.broadcasted_iota(jnp.int32, (SUB, LANES), 0)

    zero = jnp.zeros((SUB, LANES), F32)
    sp = [spatial_ref[k : k + 1, :] for k in range(9)]
    tm = [temporal_ref[k : k + 1, :] for k in range(3)]
    lift = [lift_ref[c : c + 1, :] for c in range(channels)]
    for h in range(rows):
        by_tap = []
        for tap in range(3):
            total = zero
            for a in range(3):
                total = jnp.where(row == h + a - 1, sp[3 * a + tap], total)
            by_tap.append(total)
        lifted = [[t * l for l in lift] for t in by_tap]
        only = [jnp.where(row == h, l, 0.0) for l in lift]
        for f in range(frames):
            window = window_of(f, frames)
            mixes, ups = [], []
            for tap in range(3):
                for local in range(3):
                    k = window + local - f + 1
                    for c in range(channels):
                        inside = 0 <= k < 3
                        mixes.append(lifted[tap][c] * tm[k] if inside else zero)
                        ups.append(only[c] if k == 1 and tap == 1 else zero)
            mixes += [zero] * (2 * LANES // SUB - len(mixes))
            ups += [zero] * (2 * LANES // SUB - len(ups))
            at = h * 2 * LANES
            mix_ref[f, :, at : at + LANES] = jnp.concatenate(mixes, axis=0).astype(BF16)
            mix_ref[f, :, at + LANES : at + 2 * LANES] = jnp.concatenate(ups, axis=0).astype(BF16)

    lane = lax.broadcasted_iota(jnp.int32, (LANES, LANES), 1)
    for h in range(rows):
        for f in range(frames):
            hi = jnp.zeros((LANES, LANES), F32)
            for c in range(channels):
                hi = jnp.where(lane == f * group + c * rows + h, out_w_ref[:, c : c + 1], hi)
            top = hi.astype(BF16)
            at = (h * frames + f) * LANES
            proj_ref[at : at + LANES, 0:LANES] = top
            proj_ref[at : at + LANES, LANES : 2 * LANES] = (hi - top.astype(F32)).astype(BF16)

    for k in range(12):
        line = spatial_ref[9 + k : 10 + k, :] if k < 9 else temporal_ref[k - 6 : k - 5, :]
        taps_ref[k] = jnp.broadcast_to(line, (16, LANES)).astype(BF16)

    wide = round_up(share + 4 * HALO, SUB)
    lead = 2 * HALO + SUB
    padded[...] = jnp.zeros_like(padded)
    padded[lead : lead + columns, :] = columns_as_rows(start_ref[...], 0.0)
    own_ref[...] = padded[pl.ds(SUB + index * share, wide), :]
    around = [
        padded[pl.ds(SUB + index * share + k, wide), :] for k in range(3)
    ]
    for f in range(frames):
        left = stack_taps(around, window_of(f, frames), group)
        lin_ref[f] = jnp.dot(left, mix_ref[f], preferred_element_type=F32)
    col = lax.broadcasted_iota(jnp.int32, (wide, LANES), 0) + index * share - (2 * HALO - 1)
    inside = [
        jnp.where((col + d >= 0) & (col + d < columns), 1.0, 0.0) for d in (-1, 0, 1)
    ]
    for h in range(rows):
        by_tap = [
            functools.reduce(
                jnp.add, [sp[3 * a + tap] for a in range(3) if 0 <= h + a - 1 < rows]
            )
            for tap in range(3)
        ]
        total = functools.reduce(jnp.add, [i * t for i, t in zip(inside, by_tap)])
        for f in range(frames):
            over = functools.reduce(
                jnp.add, [tm[k] for k in range(3) if 0 <= f + k - 1 < frames]
            )
            edge_ref[f, h] = total * over


def main_kernel(
    share, sizes, times, block, index_ref, noise_ref, freq_ref, time_ref, mix_ref, taps_ref,
    lin_ref, edge_ref, own_ref, proj_ref, point_ref, out_ref, feats, diag, acc, state,
):
    channels, frames, rows, columns = sizes
    group = channels * rows
    index = index_ref[0]
    step = 1.0 / times

    zero = jnp.zeros((LANES, LANES), BF16)
    for b in range(2):
        diag[b, 0:LANES, 0:LANES] = point_ref[b]
        diag[b, LANES:, LANES:] = point_ref[b]
        diag[b, 0:LANES, LANES:] = zero
        diag[b, LANES:, 0:LANES] = zero
    ones = jnp.full((LANES, LANES), 4.0 / LANES, BF16)
    diag[2, 0:LANES, 0:LANES] = ones
    diag[2, LANES:, LANES:] = ones
    diag[2, 0:LANES, LANES:] = zero
    diag[2, LANES:, 0:LANES] = zero

    planned = noise_ref[pl.ds(HALO, times, stride=block), :][:, LANES - 1 : LANES]
    angles = planned * freq_ref[0:1, :]
    lane = lax.broadcasted_iota(jnp.int32, angles.shape, 1)
    embedded = jnp.where(lane < LANES // 2, jnp.sin(angles), jnp.cos(angles))
    bias = jnp.dot(embedded, time_ref[...], precision=lax.Precision.HIGHEST,
                   preferred_element_type=F32)

    feats[:, 0] = jnp.zeros(feats.shape[:1] + feats.shape[2:], BF16)
    feats[:, rows + 1] = jnp.zeros(feats.shape[:1] + feats.shape[2:], BF16)

    def normalise(mixed):
        pair = jnp.concatenate(mixed, axis=1)
        mean = jnp.dot(pair * pair, diag[2], preferred_element_type=F32)
        half = pair * lax.rsqrt(mean + 4.0 * EPS).astype(BF16)
        return half + half * jnp.tanh(half)

    def block_one(cols, offset, linear):
        def one(h, carry):
            for f in range(0, frames, 2):
                mixed, lifted = [], []
                for g in (f, f + 1):
                    m, up = linear(g, h)
                    edges = edge_ref[g, h, offset : offset + cols, :]
                    m = m + edges[:, None, :] * bias[None]
                    mixed.append(m.reshape(cols * times, LANES).astype(BF16))
                    lifted.append((up + bias[None]).reshape(cols * times, LANES))
                update = jnp.dot(normalise(mixed), diag[0], preferred_element_type=F32)
                for k, g in enumerate((f, f + 1)):
                    new = lifted[k] + update[:, k * LANES : (k + 1) * LANES]
                    feats[g, h + 1, 0:cols] = new.astype(BF16).reshape(cols, times, LANES)
            return carry

        lax.fori_loop(0, rows, one, 0)
        margin = (cols - share) // 2
        for j in list(range(margin)) + list(range(cols - margin, cols)):
            col = index * share + j - margin

            @pl.when((col < 0) | (col >= columns))
            def _():
                feats[:, :, j] = jnp.zeros(feats.shape[:2] + feats.shape[3:], BF16)

    def block_two(cols):
        acc[0 : cols * times, :] = jnp.zeros((cols * times, 2 * LANES), F32)

        def one(h, carry):
            taps = [taps_ref[k][None] if times == 16 else jnp.concatenate(
                [taps_ref[k]] * (times // 16), axis=0)[None] for k in range(12)]
            spread = []
            for f in range(frames):
                total = None
                for a in range(3):
                    line = feats[f, h + a, 0 : cols + 2]
                    for c in range(3):
                        term = line[c : c + cols] * taps[3 * a + c]
                        total = term if total is None else total + term
                spread.append(total)
            outs = []
            for f in range(0, frames, 2):
                mixed = []
                for g in (f, f + 1):
                    total = None
                    for k in range(3):
                        if 0 <= g + k - 1 < frames:
                            term = spread[g + k - 1] * taps[9 + k]
                            total = term if total is None else total + term
                    mixed.append(total.reshape(cols * times, LANES))
                update = jnp.dot(normalise(mixed), diag[1], preferred_element_type=F32)
                for k, g in enumerate((f, f + 1)):
                    old = feats[g, h + 1, 1 : cols + 1].reshape(cols * times, LANES)
                    new = old.astype(F32) + update[:, k * LANES : (k + 1) * LANES]
                    outs.append(new.astype(BF16))
            at = pl.multiple_of(h * frames * LANES, frames * LANES)
            acc[0 : cols * times, :] += jnp.dot(
                jnp.concatenate(outs, axis=1), proj_ref[pl.ds(at, frames * LANES), :],
                preferred_element_type=F32,
            )
            return carry

        lax.fori_loop(0, rows, one, 0)

    def drift(cols, skip):
        f = acc[0 : cols * times, 0:LANES] + acc[0 : cols * times, LANES : 2 * LANES]
        noise = jnp.stack(
            [noise_ref[pl.ds(skip + j, times, stride=block), :] for j in range(cols)]
        )
        return step * f.reshape(cols, times, LANES) + (NOISE_SCALE * math.sqrt(step)) * noise

    def running(values):
        when = lax.broadcasted_iota(jnp.int32, values.shape, 1)
        reach = 1
        while reach < times:
            values = values + jnp.where(when >= reach, pltpu.roll(values, reach, 1), 0.0)
            reach *= 2
        return values

    def from_start(f, h):
        at = pl.multiple_of(h * 2 * LANES, 2 * LANES)
        cols = share + 2 * HALO + 2
        both = lin_ref[f, 0:cols, pl.ds(at, 2 * LANES)]
        return both[:, None, 0:LANES], both[:, None, LANES : 2 * LANES]

    block_one(share + 2 * HALO + 2, 0, from_start)
    block_two(share + 2 * HALO)
    cols = share + 2 * HALO
    moved = drift(cols, 0)
    col = lax.broadcasted_iota(jnp.int32, moved.shape, 0) + (index * share - HALO)
    inside = (col >= 0) & (col < columns)
    begin = own_ref[HALO : HALO + cols, :][:, None, :]
    state[...] = begin + jnp.where(inside, running(moved) - moved, 0.0)

    inner = share + 2
    around = [state[k : k + inner].reshape(inner * times, LANES) for k in range(3)]
    left = [stack_taps(around, window, group) for window in range(frames - 2)]

    def from_state(f, h):
        at = pl.multiple_of(h * 2 * LANES, 2 * LANES)
        both = jnp.dot(
            left[window_of(f, frames)], mix_ref[f, :, pl.ds(at, 2 * LANES)],
            preferred_element_type=F32,
        ).reshape(inner, times, 2 * LANES)
        return both[:, :, 0:LANES], both[:, :, LANES : 2 * LANES]

    block_one(inner, HALO, from_state)
    block_two(share)
    ended = own_ref[2 * HALO : 2 * HALO + share, :][:, None, :] + running(drift(share, HALO))
    for j in range(share):
        out_ref[pl.ds(j, times, stride=share), :] = ended[j]


def unpack_kernel(sizes, in_ref, out_ref):
    channels, frames, rows, _ = sizes
    image = jnp.transpose(in_ref[...])
    for f in range(frames):
        for c in range(channels):
            at = (f * channels + c) * rows
            out_ref[0, c, f] = image[at : at + rows, :]


def shards(start_frames, plan, noise, w_lift, w_time, spatial, temporal, w_point, w_out):
    times = lax.axis_size("tm")
    sizes = start_frames.shape
    channels, frames, rows, columns = sizes
    share = columns // times
    block = round_up(share + 2 * HALO, SUB)
    wide = round_up(share + 4 * HALO, SUB)
    params = pltpu.CompilerParams(vmem_limit_bytes=VMEM_LIMIT)
    index = lax.axis_index("tm").astype(jnp.int32).reshape(1)

    packed = pl.pallas_call(
        functools.partial(pack_kernel, times, share, block),
        out_shape=jax.ShapeDtypeStruct((times, block, LANES), F32),
        in_specs=[whole(pltpu.SMEM), whole()],
        out_specs=whole(),
        scratch_shapes=[pltpu.VMEM((columns + 2 * SUB, LANES), F32)],
        compiler_params=params,
        name="pack",
    )(plan, noise)
    arrived = lax.all_to_all(packed, "tm", split_axis=0, concat_axis=0, tiled=True)

    mix, taps, lin, edge, own, proj = pl.pallas_call(
        functools.partial(prep_kernel, share, sizes),
        out_shape=[
            jax.ShapeDtypeStruct((frames, 2 * LANES, rows * 2 * LANES), BF16),
            jax.ShapeDtypeStruct((12, 16, LANES), BF16),
            jax.ShapeDtypeStruct((frames, wide, rows * 2 * LANES), F32),
            jax.ShapeDtypeStruct((frames, rows, wide, LANES), F32),
            jax.ShapeDtypeStruct((wide, LANES), F32),
            jax.ShapeDtypeStruct((rows * frames * LANES, 2 * LANES), BF16),
        ],
        in_specs=[whole(pltpu.SMEM)] + [whole()] * 5,
        out_specs=[whole()] * 6,
        scratch_shapes=[pltpu.VMEM((columns + 4 * SUB + wide, LANES), F32)],
        compiler_params=params,
        cost_estimate=pl.CostEstimate(flops=10**9, bytes_accessed=10**7, transcendentals=0),
        name="prep",
    )(
        index, start_frames, w_lift,
        jnp.transpose(spatial, (0, 2, 1)).reshape(-1, LANES),
        jnp.transpose(temporal, (0, 2, 1)).reshape(-1, LANES), w_out,
    )

    half = LANES // 2
    freqs = jnp.exp(-math.log(1000.0) * jnp.arange(half, dtype=F32) / half)
    result = pl.pallas_call(
        functools.partial(main_kernel, share, sizes, times, block),
        out_shape=jax.ShapeDtypeStruct((times * share, LANES), F32),
        in_specs=[whole(pltpu.SMEM)] + [whole()] * 10,
        out_specs=whole(),
        scratch_shapes=[
            pltpu.VMEM((frames, rows + 2, share + 2 * HALO + 2, times, LANES), BF16),
            pltpu.VMEM((3, 2 * LANES, 2 * LANES), BF16),
            pltpu.VMEM(((share + 2 * HALO) * times, 2 * LANES), F32),
            pltpu.VMEM((share + 2 * HALO, times, LANES), F32),
        ],
        compiler_params=params,
        name="sampler",
    )(
        index, arrived.reshape(times * block, LANES), jnp.concatenate([freqs, freqs])[None],
        w_time, mix, taps, lin, edge, own, proj, w_point,
    )
    back = lax.all_to_all(
        result.reshape(times, share, LANES), "tm", split_axis=0, concat_axis=0, tiled=True
    )
    return pl.pallas_call(
        functools.partial(unpack_kernel, sizes),
        out_shape=jax.ShapeDtypeStruct((1,) + sizes, F32),
        in_specs=[whole()],
        out_specs=whole(),
        compiler_params=params,
        name="unpack",
    )(back.reshape(columns, LANES))


def solution(mesh):
    in_specs = (
        P("groups", None, None, None),
        P(("groups", "tm")),
        P("tm", "groups", None, None, None),
        P(),
        P(),
        P(),
        P(),
        P(),
        P(),
    )
    out_specs = P("tm", "groups", None, None, None)
    return jax.shard_map(shards, mesh=mesh, in_specs=in_specs, out_specs=out_specs, check_vma=False)
```

```python
import functools
import math

import jax
import jax.numpy as jnp
from jax import lax
from jax.experimental import pallas as pl
from jax.experimental.pallas import tpu as pltpu
from jax.sharding import PartitionSpec as P

ITERS = 2
LANES = 128
SUB = 8
HALO = 2
NOISE_SCALE = 2.0
EPS = 1e-06
F32 = jnp.float32
BF16 = jnp.bfloat16
VMEM_LIMIT = 40 * 1024 * 1024


def in_hbm(value):
    return pltpu.with_memory_space_constraint(value, pltpu.HBM)


def round_up(value, multiple):
    return (value + multiple - 1) // multiple * multiple


def whole(memory_space=pltpu.VMEM):
    return pl.BlockSpec(memory_space=memory_space)


def columns_as_rows(image, extra):
    channels, frames, rows, columns = image.shape
    parts = [image[c, f] for f in range(frames) for c in range(channels)]
    left = LANES - channels * frames * rows
    parts.append(jnp.full((left, columns), extra, F32))
    return jnp.transpose(jnp.concatenate(parts, axis=0))


def pack_kernel(shares, share, block, plan_ref, noise_ref, out_ref, padded):
    columns = noise_ref.shape[-1]
    edge = jnp.zeros((SUB, LANES), F32)
    padded[0:SUB, :] = edge
    padded[SUB + columns : 2 * SUB + columns, :] = edge
    padded[SUB : SUB + columns, :] = columns_as_rows(
        noise_ref[0], plan_ref[0].astype(F32)
    )
    for dest in range(shares):
        first = SUB - HALO + dest * share
        out_ref[dest, 0 : share + 2 * HALO, :] = padded[first : first + share + 2 * HALO, :]
        if block > share + 2 * HALO:
            out_ref[dest, share + 2 * HALO : block, :] = jnp.zeros(
                (block - share - 2 * HALO, LANES), F32
            )


def window_of(frame, frames):
    return min(max(frame - 1, 0), frames - 3)


def stack_taps(state, window, group):
    width = 3 * group
    before, here, after = [
        pltpu.roll(s, (LANES - window * group + k * width) % LANES, 1)
        for k, s in enumerate(state)
    ]
    lane = lax.broadcasted_iota(jnp.int32, before.shape, 1)
    first = jnp.where(lane < width, before, here)
    spill = 2 * width - LANES
    second = jnp.where(
        lane < spill, here, jnp.where(lane < spill + width, after, 0.0)
    )
    return jnp.concatenate([first.astype(BF16), second.astype(BF16)], axis=-1)


class Table:
    def __init__(self, share, sizes):
        _, frames, rows, _ = sizes
        self.wide = round_up(share + 4 * HALO, SUB)
        self.taps = 0
        self.edges = 12 * SUB
        self.own = self.edges + round_up(3 * frames * rows, SUB)
        self.direct = self.own + self.wide
        self.out = self.direct + self.wide
        self.size = self.out + LANES


def weight_rows(frames):
    proj = 2 * frames * LANES
    return proj, proj + 2 * LANES, proj + 4 * LANES, proj + 6 * LANES


def exact(a, b):
    return jnp.dot(a, b, precision=lax.Precision.HIGHEST, preferred_element_type=F32)


def split(value):
    top = value.astype(BF16)
    return top, (value - top.astype(F32)).astype(BF16)


def prep_kernel(
    share, sizes, index_ref, start_hbm, lift_hbm, spatial_hbm, temporal_hbm, point_hbm, out_hbm,
    mix_hbm, lin_ref, table_ref, weight_ref,
    mix_ref, start_ref, lift_ref, spatial_ref, temporal_ref, point_ref, out_w_ref, padded, sems,
):
    channels, frames, rows, columns = sizes
    group = channels * rows
    index = index_ref[0]
    table = Table(share, sizes)
    copies = [
        pltpu.make_async_copy(source, target, sems.at[k])
        for k, (source, target) in enumerate([
            (start_hbm, start_ref), (lift_hbm, lift_ref), (spatial_hbm, spatial_ref),
            (temporal_hbm, temporal_ref), (point_hbm, point_ref), (out_hbm, out_w_ref),
        ])
    ]
    for copy in copies:
        copy.start()
    padded[...] = jnp.zeros_like(padded)
    for copy in copies:
        copy.wait()
    row = lax.broadcasted_iota(jnp.int32, (SUB, LANES), 0)

    zero = jnp.zeros((SUB, LANES), F32)
    sp = [spatial_ref[k, 0:1, :] for k in range(9)]
    tm = [temporal_ref[k, 0:1, :] for k in range(3)]
    lift = [lift_ref[c : c + 1, :] for c in range(channels)]
    timed = [[l * t for t in tm] for l in lift]
    for h in range(rows):
        by_tap = []
        for tap in range(3):
            total = zero
            for a in range(3):
                if 0 <= h + a - 1 < rows:
                    total = jnp.where(row == h + a - 1, sp[3 * a + tap], total)
            by_tap.append(total)
        made = [[[t * timed[c][k] for k in range(3)] for c in range(channels)] for t in by_tap]
        only = [jnp.where(row == h, l, 0.0) for l in lift]
        for f in range(frames):
            window = window_of(f, frames)
            mixes, ups = [], []
            for tap in range(3):
                for local in range(3):
                    k = window + local - f + 1
                    for c in range(channels):
                        mixes.append(made[tap][c][k] if 0 <= k < 3 else zero)
                        ups.append(only[c] if k == 1 and tap == 1 else zero)
            mixes += [zero] * (2 * LANES // SUB - len(mixes))
            ups += [zero] * (2 * LANES // SUB - len(ups))
            at = h * 2 * LANES
            mix_ref[f, :, at : at + LANES] = jnp.concatenate(mixes, axis=0).astype(BF16)
            mix_ref[f, :, at + LANES : at + 2 * LANES] = jnp.concatenate(ups, axis=0).astype(BF16)

    leaving = pltpu.make_async_copy(mix_ref, mix_hbm, sems.at[6])
    leaving.start()

    for k in range(12):
        line = spatial_ref[k, 1:2, :] if k < 9 else temporal_ref[k - 9, 1:2, :]
        table_ref[table.taps + k * SUB : table.taps + (k + 1) * SUB, :] = jnp.broadcast_to(
            line, (SUB, LANES)
        )
    for tap in range(3):
        lines = []
        for f in range(frames):
            over = functools.reduce(
                jnp.add, [tm[k] for k in range(3) if 0 <= f + k - 1 < frames]
            )
            for h in range(rows):
                lines.append(over * functools.reduce(
                    jnp.add, [sp[3 * a + tap] for a in range(3) if 0 <= h + a - 1 < rows]
                ))
        at = table.edges + tap * frames * rows
        table_ref[at : at + frames * rows, :] = jnp.concatenate(lines, axis=0)

    left = jnp.zeros((LANES - frames * group, LANES), F32)
    spread = [jnp.broadcast_to(out_w_ref[c : c + 1, :], (rows, LANES)) for c in range(channels)]
    out_lanes = jnp.transpose(jnp.concatenate(spread * frames + [left], axis=0))
    table_ref[table.out : table.out + LANES, :] = out_lanes
    lane = lax.broadcasted_iota(jnp.int32, (LANES, LANES), 1)
    line = lax.broadcasted_iota(jnp.int32, (LANES, LANES), 0)
    first = jnp.where(lax.rem(lane, rows) == 0, out_lanes, 0.0)
    for slot, b in enumerate((1, 0)):
        folded = exact(point_ref[b].astype(F32), first)
        for f in range(frames):
            here = jnp.where((lane >= f * group) & (lane < (f + 1) * group), folded, 0.0)
            at = (slot * frames + f) * LANES
            weight_ref[at : at + LANES, 0:LANES], weight_ref[at : at + LANES, LANES:] = split(here)
    lift_rows = [jnp.broadcast_to(l, (rows, LANES)) for l in lift]
    both = exact(jnp.concatenate(lift_rows * frames + [left], axis=0), out_lanes)
    same = (lax.div(lane, group) == lax.div(line, group)) & (
        lax.rem(lane, rows) == lax.rem(line, rows)
    )
    both = jnp.where(same, both, 0.0)
    proj, direct, mixing, _ = weight_rows(frames)
    hi, lo = split(both)
    nothing = jnp.zeros((LANES, LANES), BF16)
    weight_ref[proj : proj + LANES, 0:LANES] = hi
    weight_ref[proj : proj + LANES, LANES:] = lo
    weight_ref[proj + LANES : direct, 0:LANES] = hi
    weight_ref[proj + LANES : direct, LANES:] = nothing
    for at, value in ((direct, point_ref[0]), (mixing, jnp.full((LANES, LANES), 4.0 / LANES, BF16))):
        weight_ref[at : at + LANES, 0:LANES] = value
        weight_ref[at + LANES : at + 2 * LANES, LANES:] = value
        weight_ref[at : at + LANES, LANES:] = nothing
        weight_ref[at + LANES : at + 2 * LANES, 0:LANES] = nothing

    lead = 2 * HALO + SUB
    padded[lead : lead + columns, :] = columns_as_rows(start_ref[...], 0.0)
    around = [padded[pl.ds(SUB + index * share + k, table.wide), :] for k in range(3)]
    own = around[0]
    table_ref[table.own : table.own + table.wide, :] = own
    table_ref[table.direct : table.direct + table.wide, :] = exact(own, both)
    for f in range(frames):
        lin_ref[f] = jnp.dot(
            stack_taps(around, window_of(f, frames), group), mix_ref[f], preferred_element_type=F32
        )
    leaving.wait()


def main_kernel(
    share, sizes, times, block, index_ref, noise_ref, time_ref, mix_hbm, lin_ref, table_ref,
    weight_ref, out_ref, feats, mixed_buf, normed_buf, acc, state, mix_ref, sem,
):
    channels, frames, rows, columns = sizes
    group = channels * rows
    index = index_ref[0]
    step = 1.0 / times
    table = Table(share, sizes)
    halves = times // SUB
    proj, direct, mixing, mean_end = weight_rows(frames)
    copy = pltpu.make_async_copy(mix_hbm, mix_ref, sem)
    copy.start()
    for h in (0, rows + 1):
        feats[:, h] = jnp.zeros(feats.shape[:1] + feats.shape[2:], F32)

    half = LANES // 2
    planned = noise_ref[pl.ds(HALO, times, stride=block), :][:, LANES - 1 : LANES]
    lane = lax.broadcasted_iota(jnp.int32, (1, LANES), 1)
    place = jnp.where(lane < half, lane, lane - half).astype(F32)
    angles = planned * jnp.exp(place * (-math.log(1000.0) / half))
    embedded = jnp.where(lane < half, jnp.sin(angles), jnp.cos(angles))
    bias = exact(embedded, time_ref[...])
    bias_out = exact(bias, table_ref[table.out : table.out + LANES, :])
    bias = bias.reshape(halves, SUB, LANES)

    def normalise(pair):
        mean = jnp.dot(
            (pair * pair).astype(BF16), weight_ref[mixing:mean_end, :], preferred_element_type=F32
        )
        value = pair * lax.rsqrt(mean + 4.0 * EPS)
        return (value + value * jnp.tanh(value)).astype(BF16)

    def in_pairs(values):
        return jnp.concatenate(
            [jnp.concatenate(values[f : f + 2], axis=1) for f in range(0, frames, 2)], axis=0
        )

    def by_frame(pairs, cells):
        return jnp.concatenate(
            [pairs[k * cells : (k + 1) * cells] for k in range(frames // 2)], axis=1
        )

    def run_network(cols, linear):
        wide = cols + 2
        cells = cols * times
        margin = (wide - share) // 2
        flags = {}
        for j in list(range(margin)) + list(range(wide - margin, wide)):
            col = index * share + j - margin
            flags[j] = jnp.where((col >= 0) & (col < columns), 1.0, 0.0).astype(F32)
        taps = [table_ref[table.taps + k * SUB : table.taps + (k + 1) * SUB, :] for k in range(12)]

        def block_one(h):
            mixed, lifted = [], []
            for f in range(frames):
                m, up = linear(f, h)
                at = table.edges + f * rows + h
                by_tap = [
                    bias * table_ref[pl.ds(at + k * frames * rows, 1), :][None] for k in range(3)
                ]
                over = by_tap[0] + by_tap[1] + by_tap[2]
                parts = []
                for j in range(wide):
                    value = m[j] + over
                    if j == margin:
                        value = value - by_tap[0] * jnp.where(index == 0, 1.0, 0.0)
                    if j == wide - margin - 1:
                        value = value - by_tap[2] * jnp.where((index + 1) * share == columns, 1.0, 0.0)
                    parts.append(value.reshape(times, LANES))
                mixed.append(jnp.concatenate(parts, axis=0))
                lifted.append(up)
            normed = normalise(in_pairs(mixed))
            update = jnp.dot(normed, weight_ref[direct:mixing, :], preferred_element_type=F32)
            normed_buf[h + 1, 0:cells, :] = by_frame(normed, wide * times)[times : times + cells]
            for f in range(frames):
                at = (f // 2) * wide * times
                lanes = (f % 2) * LANES
                for j in range(wide):
                    new = update[at + j * times : at + (j + 1) * times, lanes : lanes + LANES]
                    new = new.reshape(halves, SUB, LANES) + (lifted[f][j] + bias)
                    feats[f, h + 1, j] = new * flags[j] if j in flags else new

        def convolve(h):
            for j in range(cols):
                spread = []
                for f in range(frames):
                    total = None
                    for a in range(3):
                        for c in range(3):
                            term = feats[f, h + a, j + c] * taps[3 * a + c]
                            total = term if total is None else total + term
                    spread.append(total)
                for f in range(frames):
                    total = None
                    for k in range(3):
                        if 0 <= f + k - 1 < frames:
                            term = spread[f + k - 1] * taps[9 + k]
                            total = term if total is None else total + term
                    mixed_buf[lax.rem(h, 2), f, j * times : (j + 1) * times, :] = total.reshape(
                        times, LANES
                    )

        def finish(h, slot):
            values = [mixed_buf[slot, f, 0:cells, :] for f in range(frames)]
            normed = by_frame(normalise(in_pairs(values)), cells)
            left = jnp.concatenate([normed, normed_buf[h + 1, 0:cells, :]], axis=1)
            out = jnp.dot(left, weight_ref[0:proj, :], preferred_element_type=F32)
            out = out[:, 0:LANES] + out[:, LANES:]
            acc[0:cells, :] += pltpu.roll(out, lax.rem(h + LANES, LANES), 1)

        acc[0:cells, :] = jnp.zeros((cells, LANES), F32)
        mixed_buf[1] = jnp.zeros(mixed_buf.shape[1:], F32)
        normed_buf[0] = jnp.zeros(normed_buf.shape[1:], BF16)

        def lead_in(h, carry):
            block_one(h)
            return carry

        def steady(h, carry):
            finish(h - 1, lax.rem(h + 1, 2))
            convolve(h)
            block_one(h + 2)
            return carry

        def tail(h, carry):
            finish(h - 1, lax.rem(h + 1, 2))
            convolve(h)
            return carry

        lax.fori_loop(0, 2, lead_in, 0)
        lax.fori_loop(0, rows - 2, steady, 0)
        lax.fori_loop(rows - 2, rows, tail, 0)
        finish(rows - 1, (rows - 1) % 2)

    def drift(cols, skip, through):
        f = acc[0 : cols * times, :].reshape(cols, times, LANES) + through + bias_out[None]
        noise = jnp.stack(
            [noise_ref[pl.ds(skip + j, times, stride=block), :] for j in range(cols)]
        )
        return step * f + (NOISE_SCALE * math.sqrt(step)) * noise

    def running(values):
        when = lax.broadcasted_iota(jnp.int32, values.shape, 1)
        reach = 1
        while reach < times:
            values = values + jnp.where(when >= reach, pltpu.roll(values, reach, 1), 0.0)
            reach *= 2
        return values

    def from_start(f, h):
        at = pl.multiple_of(h * 2 * LANES, 2 * LANES)
        cols = share + 2 * HALO + 2
        both = [lin_ref[f, pl.ds(j, 1), pl.ds(at, 2 * LANES)] for j in range(cols)]
        return [b[None, :, 0:LANES] for b in both], [b[None, :, LANES:] for b in both]

    cols = share + 2 * HALO
    run_network(cols, from_start)
    begin = table_ref[table.own + HALO : table.own + HALO + cols, :][:, None, :]
    through = table_ref[table.direct + HALO : table.direct + HALO + cols, :][:, None, :]
    moved = drift(cols, 0, through)
    col = lax.broadcasted_iota(jnp.int32, moved.shape, 0) + (index * share - HALO)
    inside = (col >= 0) & (col < columns)
    state[...] = begin + jnp.where(inside, running(moved) - moved, 0.0)

    copy.wait()
    inner = share + 2
    around = [state[k : k + inner].reshape(inner * times, LANES) for k in range(3)]
    left = [stack_taps(around, window, group) for window in range(frames - 2)]

    def from_state(f, h):
        at = pl.multiple_of(h * 2 * LANES, 2 * LANES)
        both = jnp.dot(
            left[window_of(f, frames)], mix_ref[f, :, pl.ds(at, 2 * LANES)],
            preferred_element_type=F32,
        ).reshape(inner, halves, SUB, 2 * LANES)
        return (
            [both[j, :, :, 0:LANES] for j in range(inner)],
            [both[j, :, :, LANES:] for j in range(inner)],
        )

    run_network(share, from_state)
    hi, lo = split(state[HALO : HALO + share].reshape(share * times, LANES))
    through = jnp.dot(
        jnp.concatenate([hi, lo], axis=1), weight_ref[proj:direct, :], preferred_element_type=F32
    )
    through = (through[:, 0:LANES] + through[:, LANES:]).reshape(share, times, LANES)
    own = table.own + 2 * HALO
    ended = table_ref[own : own + share, :][:, None, :] + running(drift(share, HALO, through))
    for j in range(share):
        out_ref[pl.ds(j, times, stride=share), :] = ended[j]


def unpack_kernel(sizes, in_ref, out_ref):
    channels, frames, rows, _ = sizes
    image = jnp.transpose(in_ref[...])
    for f in range(frames):
        for c in range(channels):
            at = (f * channels + c) * rows
            out_ref[0, c, f] = image[at : at + rows, :]


def shards(start_frames, plan, noise, w_lift, w_time, spatial, temporal, w_point, w_out):
    times = lax.axis_size("tm")
    sizes = start_frames.shape
    channels, frames, rows, columns = sizes
    share = columns // times
    block = round_up(share + 2 * HALO, SUB)
    table = Table(share, sizes)
    params = pltpu.CompilerParams(vmem_limit_bytes=VMEM_LIMIT)
    index = lax.axis_index("tm").astype(jnp.int32).reshape(1)
    hbm = whole(pltpu.HBM)

    packed = pl.pallas_call(
        functools.partial(pack_kernel, times, share, block),
        out_shape=pltpu.VMEM((times, block, LANES), F32),
        in_specs=[whole(pltpu.SMEM), whole()],
        out_specs=whole(),
        scratch_shapes=[pltpu.VMEM((columns + 2 * SUB, LANES), F32)],
        compiler_params=params,
        name="pack",
    )(plan, noise)
    arrived = lax.all_to_all(packed, "tm", split_axis=0, concat_axis=0, tiled=True)

    by_tap = (
        w_lift, jnp.transpose(spatial, (2, 0, 1)), jnp.transpose(temporal, (2, 0, 1)), w_point,
        jnp.transpose(w_out),
    )
    mix, lin, lines, weights = pl.pallas_call(
        functools.partial(prep_kernel, share, sizes),
        out_shape=[
            pltpu.HBM((frames, 2 * LANES, rows * 2 * LANES), BF16),
            pltpu.VMEM((frames, table.wide, rows * 2 * LANES), F32),
            pltpu.VMEM((table.size, LANES), F32),
            pltpu.VMEM((weight_rows(frames)[-1], 2 * LANES), BF16),
        ],
        in_specs=[whole(pltpu.SMEM)] + [hbm] * 6,
        out_specs=[hbm] + [whole()] * 3,
        scratch_shapes=[pltpu.VMEM((frames, 2 * LANES, rows * 2 * LANES), BF16)]
        + [pltpu.VMEM(sizes, F32)]
        + [pltpu.VMEM(a.shape, a.dtype) for a in by_tap]
        + [
            pltpu.VMEM((columns + 4 * SUB + table.wide, LANES), F32),
            pltpu.SemaphoreType.DMA((7,)),
        ],
        compiler_params=params,
        cost_estimate=pl.CostEstimate(flops=10**9, bytes_accessed=10**7, transcendentals=0),
        name="prep",
    )(index, *[in_hbm(a) for a in (start_frames,) + by_tap])

    result = pl.pallas_call(
        functools.partial(main_kernel, share, sizes, times, block),
        out_shape=jax.ShapeDtypeStruct((times * share, LANES), F32),
        in_specs=[whole(pltpu.SMEM), whole(), whole(), hbm] + [whole()] * 3,
        out_specs=whole(),
        scratch_shapes=[
            pltpu.VMEM(
                (frames, rows + 2, share + 2 * HALO + 2, times // SUB, SUB, LANES), F32
            ),
            pltpu.VMEM((2, frames, (share + 2 * HALO) * times, LANES), F32),
            pltpu.VMEM((rows + 1, (share + 2 * HALO) * times, frames * LANES), BF16),
            pltpu.VMEM(((share + 2 * HALO) * times, LANES), F32),
            pltpu.VMEM((share + 2 * HALO, times, LANES), F32),
            pltpu.VMEM(mix.shape, BF16),
            pltpu.SemaphoreType.DMA,
        ],
        compiler_params=params,
        name="sampler",
    )(index, arrived.reshape(times * block, LANES), w_time, in_hbm(mix), lin, lines, weights)
    back = lax.all_to_all(
        result.reshape(times, share, LANES), "tm", split_axis=0, concat_axis=0, tiled=True
    )
    return pl.pallas_call(
        functools.partial(unpack_kernel, sizes),
        out_shape=jax.ShapeDtypeStruct((1,) + sizes, F32),
        in_specs=[whole()],
        out_specs=whole(),
        compiler_params=params,
        name="unpack",
    )(back.reshape(columns, LANES))


def solution(mesh):
    in_specs = (
        P("groups", None, None, None),
        P(("groups", "tm")),
        P("tm", "groups", None, None, None),
        P(),
        P(),
        P(),
        P(),
        P(),
        P(),
    )
    out_specs = P("tm", "groups", None, None, None)
    return jax.shard_map(shards, mesh=mesh, in_specs=in_specs, out_specs=out_specs, check_vma=False)
```

```python
import functools
import math

import jax
import jax.numpy as jnp
from jax import lax
from jax.experimental import pallas as pl
from jax.experimental.pallas import tpu as pltpu
from jax.sharding import PartitionSpec as P

ITERS = 2
LANES = 128
SUB = 8
HALO = 2
NOISE_SCALE = 2.0
EPS = 1e-06
F32 = jnp.float32
BF16 = jnp.bfloat16
VMEM_LIMIT = 60 * 1024 * 1024


def in_hbm(value):
    return pltpu.with_memory_space_constraint(value, pltpu.HBM)


def round_up(value, multiple):
    return (value + multiple - 1) // multiple * multiple


def whole(memory_space=pltpu.VMEM):
    return pl.BlockSpec(memory_space=memory_space)


def columns_as_rows(image, extra):
    channels, frames, rows, columns = image.shape
    parts = [image[c, f] for f in range(frames) for c in range(channels)]
    left = LANES - channels * frames * rows
    parts.append(jnp.full((left, columns), extra, F32))
    return jnp.transpose(jnp.concatenate(parts, axis=0))


def pack_kernel(shares, share, block, plan_ref, noise_ref, out_ref, padded):
    columns = noise_ref.shape[-1]
    edge = jnp.zeros((SUB, LANES), F32)
    padded[0:SUB, :] = edge
    padded[SUB + columns : 2 * SUB + columns, :] = edge
    padded[SUB : SUB + columns, :] = columns_as_rows(
        noise_ref[0], plan_ref[0].astype(F32)
    )
    for dest in range(shares):
        first = SUB - HALO + dest * share
        out_ref[dest, 0 : share + 2 * HALO, :] = padded[first : first + share + 2 * HALO, :]
        if block > share + 2 * HALO:
            out_ref[dest, share + 2 * HALO : block, :] = jnp.zeros(
                (block - share - 2 * HALO, LANES), F32
            )


def window_of(frame, frames):
    return min(max(frame - 1, 0), frames - 3)


def one_hot_fits(times, group):
    return 9 * group + 2 * times <= 2 * LANES and (2 * LANES - 2 * times) % 16 == 0


def stack_taps(state, window, group, times):
    width = 3 * group
    before, here, after = [
        pltpu.roll(s, (LANES - window * group + k * width) % LANES, 1)
        for k, s in enumerate(state)
    ]
    lane = lax.broadcasted_iota(jnp.int32, before.shape, 1)
    first = jnp.where(lane < width, before, here)
    spill = 2 * width - LANES
    code = jnp.zeros_like(before)
    if one_hot_fits(times, group):
        when = lax.rem(lax.broadcasted_iota(jnp.int32, before.shape, 0), times)
        at = lane - (LANES - 2 * times)
        code = jnp.where((at >= 0) & (lax.rem(at + times, times) == when), 1.0, 0.0)
    second = jnp.where(
        lane < spill, here, jnp.where(lane < spill + width, after, code)
    )
    return jnp.concatenate([first.astype(BF16), second.astype(BF16)], axis=-1)


class Table:
    def __init__(self, share, sizes):
        _, frames, rows, _ = sizes
        self.wide = round_up(share + 4 * HALO, SUB)
        self.taps = 0
        self.edges = 15 * SUB
        self.own = self.edges + round_up(3 * frames * rows, SUB)
        self.direct = self.own + self.wide
        self.out = self.direct + self.wide
        self.size = self.out + LANES


def weight_rows(frames):
    proj = 2 * frames * LANES
    return proj, proj + 2 * LANES, proj + 4 * LANES, proj + 6 * LANES


def exact(a, b):
    return jnp.dot(a, b, precision=lax.Precision.HIGHEST, preferred_element_type=F32)


def split(value):
    top = value.astype(BF16)
    return top, (value - top.astype(F32)).astype(BF16)


def prep_kernel(
    share, sizes, index_ref, start_hbm, lift_hbm, spatial_hbm, temporal_hbm, point_hbm, out_hbm,
    mix_hbm, table_ref, weight_ref,
    mix_ref, start_ref, lift_ref, spatial_ref, temporal_ref, point_ref, out_w_ref, padded, sems,
):
    channels, frames, rows, columns = sizes
    group = channels * rows
    index = index_ref[0]
    table = Table(share, sizes)
    copies = [
        pltpu.make_async_copy(source, target, sems.at[k])
        for k, (source, target) in enumerate([
            (start_hbm, start_ref), (lift_hbm, lift_ref), (spatial_hbm, spatial_ref),
            (temporal_hbm, temporal_ref), (point_hbm, point_ref), (out_hbm, out_w_ref),
        ])
    ]
    for copy in copies:
        copy.start()
    padded[...] = jnp.zeros_like(padded)
    for copy in copies:
        copy.wait()
    row = lax.broadcasted_iota(jnp.int32, (SUB, LANES), 0)

    zero = jnp.zeros((SUB, LANES), F32)
    sp = [spatial_ref[k, 0:1, :] for k in range(9)]
    tm = [temporal_ref[k, 0:1, :] for k in range(3)]
    lift = [lift_ref[c : c + 1, :] for c in range(channels)]
    timed = [[l * t for t in tm] for l in lift]
    for h in range(rows):
        by_tap = []
        for tap in range(3):
            total = zero
            for a in range(3):
                if 0 <= h + a - 1 < rows:
                    total = jnp.where(row == h + a - 1, sp[3 * a + tap], total)
            by_tap.append(total)
        made = [[[t * timed[c][k] for k in range(3)] for c in range(channels)] for t in by_tap]
        only = [jnp.where(row == h, l, 0.0) for l in lift]
        for f in range(frames):
            window = window_of(f, frames)
            mixes, ups = [], []
            for tap in range(3):
                for local in range(3):
                    k = window + local - f + 1
                    for c in range(channels):
                        mixes.append(made[tap][c][k] if 0 <= k < 3 else zero)
                        ups.append(only[c] if k == 1 and tap == 1 else zero)
            mixes += [zero] * (2 * LANES // SUB - len(mixes))
            ups += [zero] * (2 * LANES // SUB - len(ups))
            at = f % 2 * LANES
            mix_ref[h, f // 2, :, at : at + LANES] = jnp.concatenate(mixes, axis=0).astype(BF16)
            at += 2 * LANES
            mix_ref[h, f // 2, :, at : at + LANES] = jnp.concatenate(ups, axis=0).astype(BF16)
    leaving = pltpu.make_async_copy(mix_ref, mix_hbm, sems.at[6])
    leaving.start()

    lines = []
    for a in range(3):
        g = [spatial_ref[3 * a + c, 1:2, :] for c in range(3)]
        lines += [g[0], 0.5 * (g[0] + g[1] + g[2]), 0.5 * (g[0] - g[1] + g[2]), g[2]]
    lines += [temporal_ref[k, 1:2, :] for k in range(3)]
    for k, line in enumerate(lines):
        at = table.taps + k * SUB
        table_ref[at : at + SUB, :] = jnp.broadcast_to(line, (SUB, LANES))
    for tap in range(3):
        lines = []
        for f in range(frames):
            over = functools.reduce(
                jnp.add, [tm[k] for k in range(3) if 0 <= f + k - 1 < frames]
            )
            for h in range(rows):
                lines.append(over * functools.reduce(
                    jnp.add, [sp[3 * a + tap] for a in range(3) if 0 <= h + a - 1 < rows]
                ))
        at = table.edges + tap * frames * rows
        table_ref[at : at + frames * rows, :] = jnp.concatenate(lines, axis=0)

    left = jnp.zeros((LANES - frames * group, LANES), F32)
    spread = [jnp.broadcast_to(out_w_ref[c : c + 1, :], (rows, LANES)) for c in range(channels)]
    out_lanes = jnp.transpose(jnp.concatenate(spread * frames + [left], axis=0))
    table_ref[table.out : table.out + LANES, :] = out_lanes
    lane = lax.broadcasted_iota(jnp.int32, (LANES, LANES), 1)
    line = lax.broadcasted_iota(jnp.int32, (LANES, LANES), 0)
    first = jnp.where(lax.rem(lane, rows) == 0, out_lanes, 0.0)
    for slot, b in enumerate((1, 0)):
        folded = exact(point_ref[b].astype(F32), first)
        for f in range(frames):
            here = jnp.where((lane >= f * group) & (lane < (f + 1) * group), folded, 0.0)
            at = (slot * frames + f) * LANES
            weight_ref[at : at + LANES, 0:LANES], weight_ref[at : at + LANES, LANES:] = split(here)
    lift_rows = [jnp.broadcast_to(l, (rows, LANES)) for l in lift]
    both = exact(jnp.concatenate(lift_rows * frames + [left], axis=0), out_lanes)
    same = (lax.div(lane, group) == lax.div(line, group)) & (
        lax.rem(lane, rows) == lax.rem(line, rows)
    )
    both = jnp.where(same, both, 0.0)
    proj, direct, mixing, _ = weight_rows(frames)
    hi, lo = split(both)
    nothing = jnp.zeros((LANES, LANES), BF16)
    weight_ref[proj : proj + LANES, 0:LANES] = hi
    weight_ref[proj : proj + LANES, LANES:] = lo
    weight_ref[proj + LANES : direct, 0:LANES] = hi
    weight_ref[proj + LANES : direct, LANES:] = nothing
    for at, value in ((direct, point_ref[0]), (mixing, jnp.full((LANES, LANES), 4.0 / LANES, BF16))):
        weight_ref[at : at + LANES, 0:LANES] = value
        weight_ref[at + LANES : at + 2 * LANES, LANES:] = value
        weight_ref[at : at + LANES, LANES:] = nothing
        weight_ref[at + LANES : at + 2 * LANES, 0:LANES] = nothing

    lead = 2 * HALO + SUB
    padded[lead : lead + columns, :] = columns_as_rows(start_ref[...], 0.0)
    own = padded[pl.ds(SUB + index * share, table.wide), :]
    table_ref[table.own : table.own + table.wide, :] = own
    table_ref[table.direct : table.direct + table.wide, :] = exact(own, both)
    leaving.wait()


def main_kernel(
    share, sizes, times, block, index_ref, noise_ref, time_ref, mix_hbm, table_ref, weight_ref,
    out_ref, feats, fresh, mixed_buf, normed_buf, acc, state, left_buf, mix_ref, sems,
):
    channels, frames, rows, columns = sizes
    group = channels * rows
    index = index_ref[0]
    step = 1.0 / times
    table = Table(share, sizes)
    halves = times // SUB
    proj, direct, mixing, mean_end = weight_rows(frames)
    hot = one_hot_fits(times, group)

    def arrival(h):
        return pltpu.make_async_copy(mix_hbm.at[h], mix_ref.at[h], sems.at[h])

    for h in range(rows):
        arrival(h).start()
    for h in (0, rows + 1):
        feats[:, h] = jnp.zeros(feats.shape[:1] + feats.shape[2:], F32)

    half = LANES // 2
    planned = noise_ref[pl.ds(HALO, times, stride=block), :][:, LANES - 1 : LANES]
    lane = lax.broadcasted_iota(jnp.int32, (1, LANES), 1)
    place = jnp.where(lane < half, lane, lane - half).astype(F32)
    angles = planned * jnp.exp(place * (-math.log(1000.0) / half))
    embedded = jnp.where(lane < half, jnp.sin(angles), jnp.cos(angles))
    bias = exact(embedded, time_ref[...])
    bias_out = exact(bias, table_ref[table.out : table.out + LANES, :])

    def mean_square(pair):
        return jnp.dot(
            (pair * pair).astype(BF16), weight_ref[mixing:mean_end, :], preferred_element_type=F32
        )

    def normalise(pair, mean):
        value = pair * lax.rsqrt(mean + 4.0 * EPS)
        return (value + value * jnp.tanh(value)).astype(BF16)

    def in_pairs(values):
        return jnp.concatenate(
            [jnp.concatenate(values[f : f + 2], axis=1) for f in range(0, frames, 2)], axis=0
        )

    def by_frame(pairs, cells):
        return jnp.concatenate(
            [pairs[k * cells : (k + 1) * cells] for k in range(frames // 2)], axis=1
        )

    def bias_taps(h):
        return [
            jnp.concatenate(
                [
                    bias * table_ref[pl.ds(table.edges + (k * frames + f) * rows + h, 1), :]
                    for f in range(frames)
                ],
                axis=1,
            )
            for k in range(3)
        ]

    def receive(h):
        arrival(h).wait()
        if hot:
            by_tap = bias_taps(h)
            every = by_tap[0] + by_tap[1] + by_tap[2]
            at = 2 * LANES - 2 * times
            for p in range(frames // 2):
                here = every[:, 2 * p * LANES : 2 * (p + 1) * LANES]
                terms = jnp.concatenate([here, bias, bias], axis=1)
                mix_ref[h, p, at : at + times, :], mix_ref[h, p, at + times :, :] = split(terms)

    def run_network(cols, first_time):
        wide = cols + 2
        cells = cols * times
        many = wide * times
        margin = (wide - share) // 2
        flags = {}
        for j in list(range(margin)) + list(range(wide - margin, wide)):
            col = index * share + j - margin
            flags[j] = jnp.where((col >= 0) & (col < columns), 1.0, 0.0).astype(F32)
        at_left = jnp.where(index == 0, 1.0, 0.0).astype(F32)
        at_right = jnp.where((index + 1) * share == columns, 1.0, 0.0).astype(F32)
        taps = [table_ref[table.taps + k * SUB : table.taps + (k + 1) * SUB, :] for k in range(15)]
        around = [state[k : k + wide].reshape(many, LANES) for k in range(3)]
        for p in range(frames // 2):
            left_buf[p, 0:many, :] = stack_taps(around, p, group, times)

        def block_one(h):
            linear = [
                jnp.dot(
                    left_buf[p, 0:many, :], mix_ref[h, p, :, 0 : 2 * LANES],
                    preferred_element_type=F32,
                )
                for p in range(frames // 2)
            ]
            yield
            by_tap = bias_taps(h)
            parts = []
            for p in range(frames // 2):
                lanes = slice(2 * p * LANES, 2 * (p + 1) * LANES)
                mixed = linear[p]
                if not hot:
                    every = by_tap[0] + by_tap[1] + by_tap[2]
                    mixed = mixed + jnp.concatenate([every[:, lanes]] * wide, axis=0)
                one, two = margin * times, (wide - margin - 1) * times
                if one == two:
                    edge = by_tap[0][:, lanes] * at_left + by_tap[2][:, lanes] * at_right
                    middle = [mixed[one : one + times] - edge]
                else:
                    middle = [
                        mixed[one : one + times] - by_tap[0][:, lanes] * at_left,
                        mixed[one + times : two],
                        mixed[two : two + times] - by_tap[2][:, lanes] * at_right,
                    ]
                parts += [mixed[:one]] + middle + [mixed[two + times :]]
            pair = jnp.concatenate([x for x in parts if x.shape[0]], axis=0)
            mean = mean_square(pair)
            yield
            normed = normalise(pair, mean)
            normed_buf[h, 0:cells, :] = by_frame(normed, many)[times : times + cells]
            updates = []
            for p in range(frames // 2):
                both = jnp.concatenate([normed[p * many : (p + 1) * many], left_buf[p, 0:many, :]], axis=1)
                onto = jnp.concatenate(
                    [weight_ref[direct:mixing, :], mix_ref[h, p, :, 2 * LANES :]], axis=0
                )
                updates.append(jnp.dot(both, onto, preferred_element_type=F32))
            yield
            for p in range(frames // 2):
                fresh[p, 0:many, :] = updates[p]
            yield

        def settle(lines, line):
            for f in range(frames):
                lanes = slice(f % 2 * LANES, (f % 2 + 1) * LANES)
                new = []
                for j in range(wide):
                    value = fresh[f // 2, j * times : (j + 1) * times, lanes]
                    if not hot:
                        value = value + bias
                    value = value.reshape(halves, SUB, LANES)
                    new.append(value * flags[j] if j in flags else value)
                for q in range(cols // 2):
                    d = new[2 * q : 2 * q + 4]
                    lines[f, line, q, 0] = d[0] - d[2]
                    lines[f, line, q, 1] = d[1] + d[2]
                    lines[f, line, q, 2] = d[2] - d[1]
                    lines[f, line, q, 3] = d[1] - d[3]

        def convolve(h, lines, begin, end):
            for q in range(begin, end):
                spread = []
                for f in range(frames):
                    m = []
                    for i in range(4):
                        terms = [lines[f, a, q, i] * taps[4 * a + i] for a in range(3)]
                        m.append(terms[0] + terms[1] + terms[2])
                    spread.append((m[0] + m[1] + m[2], m[1] - m[2] - m[3]))
                for f in range(frames):
                    for side in range(2):
                        total = None
                        for k in range(3):
                            if 0 <= f + k - 1 < frames:
                                term = spread[f + k - 1][side] * taps[12 + k]
                                total = term if total is None else total + term
                        at = (2 * q + side) * times
                        mixed_buf[lax.rem(h, 2), f, at : at + times, :] = total.reshape(times, LANES)

        def finish(h, slot):
            pair = in_pairs([mixed_buf[slot, f, 0:cells, :] for f in range(frames)])
            mean = mean_square(pair)
            yield
            normed = by_frame(normalise(pair, mean), cells)
            left = jnp.concatenate([normed, normed_buf[h, 0:cells, :]], axis=1)
            out = jnp.dot(left, weight_ref[0:proj, :], preferred_element_type=F32)
            yield
            out = out[:, 0:LANES] + out[:, LANES:]
            acc[0:cells, :] += pltpu.roll(out, h, 1)
            yield

        acc[0:cells, :] = jnp.zeros((cells, LANES), F32)
        pairs = cols // 2

        def receive_next(h):
            if first_time and isinstance(h, int):
                receive(h)
            elif first_time:

                @pl.when(h < rows)
                def _():
                    receive(h)

        def steady(h, carry):
            lines = feats.at[:, pl.ds(h, 3)]
            ending, starting = finish(h - 1, lax.rem(h + 1, 2)), block_one(h + 2)
            settle(lines, 2)
            next(starting)
            next(ending)
            next(starting)
            convolve(h, lines, 0, pairs)
            next(ending)
            next(starting)
            next(ending)
            next(starting)
            receive_next(h + 3)
            return carry

        if first_time:
            receive(0)
            receive(1)
        ahead = block_one(0)
        for _ in ahead:
            pass
        settle(feats, 1)
        for _ in block_one(1):
            pass
        receive_next(2)
        settle(feats, 2)
        starting = block_one(2)
        next(starting)
        convolve(0, feats, 0, pairs)
        for _ in starting:
            pass
        receive_next(3)
        lax.fori_loop(1, rows - 2, steady, 0)
        lines = feats.at[:, pl.ds(rows - 2, 3)]
        settle(lines, 2)
        ending = finish(rows - 3, (rows - 3) % 2)
        next(ending)
        convolve(rows - 2, lines, 0, pairs)
        for _ in ending:
            pass
        ending = finish(rows - 2, (rows - 2) % 2)
        next(ending)
        convolve(rows - 1, feats.at[:, pl.ds(rows - 1, 3)], 0, pairs)
        for _ in ending:
            pass
        for _ in finish(rows - 1, (rows - 1) % 2):
            pass

    def drift(cols, skip, through):
        f = acc[0 : cols * times, :].reshape(cols, times, LANES) + through + bias_out[None]
        noise = jnp.stack(
            [noise_ref[pl.ds(skip + j, times, stride=block), :] for j in range(cols)]
        )
        return step * f + (NOISE_SCALE * math.sqrt(step)) * noise

    def running(values):
        when = lax.broadcasted_iota(jnp.int32, values.shape, 1)
        reach = 1
        while reach < times:
            values = values + jnp.where(when >= reach, pltpu.roll(values, reach, 1), 0.0)
            reach *= 2
        return values

    cols = share + 2 * HALO
    for j in range(cols + 4):
        at = table.own + j
        state[j] = jnp.broadcast_to(table_ref[at : at + 1, :], (times, LANES))
    run_network(cols, True)
    begin = table_ref[table.own + HALO : table.own + HALO + cols, :][:, None, :]
    through = table_ref[table.direct + HALO : table.direct + HALO + cols, :][:, None, :]
    moved = drift(cols, 0, through)
    col = lax.broadcasted_iota(jnp.int32, moved.shape, 0) + (index * share - HALO)
    inside = (col >= 0) & (col < columns)
    state[0:cols] = begin + jnp.where(inside, running(moved) - moved, 0.0)

    run_network(share, False)
    hi, lo = split(state[HALO : HALO + share].reshape(share * times, LANES))
    through = jnp.dot(
        jnp.concatenate([hi, lo], axis=1), weight_ref[proj:direct, :], preferred_element_type=F32
    )
    through = (through[:, 0:LANES] + through[:, LANES:]).reshape(share, times, LANES)
    own = table.own + 2 * HALO
    ended = table_ref[own : own + share, :][:, None, :] + running(drift(share, HALO, through))
    for j in range(share):
        out_ref[pl.ds(j, times, stride=share), :] = ended[j]


def unpack_kernel(sizes, in_ref, out_ref):
    channels, frames, rows, _ = sizes
    image = jnp.transpose(in_ref[...])
    for f in range(frames):
        for c in range(channels):
            at = (f * channels + c) * rows
            out_ref[0, c, f] = image[at : at + rows, :]


def shards(start_frames, plan, noise, w_lift, w_time, spatial, temporal, w_point, w_out):
    times = lax.axis_size("tm")
    sizes = start_frames.shape
    channels, frames, rows, columns = sizes
    share = columns // times
    block = round_up(share + 2 * HALO, SUB)
    cols = share + 2 * HALO
    table = Table(share, sizes)
    params = pltpu.CompilerParams(vmem_limit_bytes=VMEM_LIMIT)
    index = lax.axis_index("tm").astype(jnp.int32).reshape(1)
    hbm = whole(pltpu.HBM)

    packed = pl.pallas_call(
        functools.partial(pack_kernel, times, share, block),
        out_shape=pltpu.VMEM((times, block, LANES), F32),
        in_specs=[whole(pltpu.SMEM), whole()],
        out_specs=whole(),
        scratch_shapes=[pltpu.VMEM((columns + 2 * SUB, LANES), F32)],
        compiler_params=params,
        name="pack",
    )(plan, noise)
    arrived = lax.all_to_all(packed, "tm", split_axis=0, concat_axis=0, tiled=True)

    by_tap = (
        w_lift, jnp.transpose(spatial, (2, 0, 1)), jnp.transpose(temporal, (2, 0, 1)), w_point,
        jnp.transpose(w_out),
    )
    mix, lines, weights = pl.pallas_call(
        functools.partial(prep_kernel, share, sizes),
        out_shape=[
            pltpu.HBM((rows, frames // 2, 2 * LANES, 4 * LANES), BF16),
            pltpu.VMEM((table.size, LANES), F32),
            pltpu.VMEM((weight_rows(frames)[-1], 2 * LANES), BF16),
        ],
        in_specs=[whole(pltpu.SMEM)] + [hbm] * 6,
        out_specs=[hbm] + [whole()] * 2,
        scratch_shapes=[pltpu.VMEM((rows, frames // 2, 2 * LANES, 4 * LANES), BF16)]
        + [pltpu.VMEM(sizes, F32)]
        + [pltpu.VMEM(a.shape, a.dtype) for a in by_tap]
        + [
            pltpu.VMEM((columns + 4 * SUB + table.wide, LANES), F32),
            pltpu.SemaphoreType.DMA((7,)),
        ],
        compiler_params=params,
        cost_estimate=pl.CostEstimate(flops=10**9, bytes_accessed=10**7, transcendentals=0),
        name="prep",
    )(index, *[in_hbm(a) for a in (start_frames,) + by_tap])

    result = pl.pallas_call(
        functools.partial(main_kernel, share, sizes, times, block),
        out_shape=jax.ShapeDtypeStruct((times * share, LANES), F32),
        in_specs=[whole(pltpu.SMEM), whole(), whole(), hbm, whole(), whole()],
        out_specs=whole(),
        scratch_shapes=[
            pltpu.VMEM((frames, rows + 2, cols // 2, 4, times // SUB, SUB, LANES), F32),
            pltpu.VMEM((frames // 2, (cols + 2) * times, 2 * LANES), F32),
            pltpu.VMEM((2, frames, cols * times, LANES), F32),
            pltpu.VMEM((rows, cols * times, frames * LANES), BF16),
            pltpu.VMEM((cols * times, LANES), F32),
            pltpu.VMEM((cols + 4, times, LANES), F32),
            pltpu.VMEM((frames // 2, (cols + 2) * times, 2 * LANES), BF16),
            pltpu.VMEM(mix.shape, BF16),
            pltpu.SemaphoreType.DMA((rows,)),
        ],
        compiler_params=params,
        name="sampler",
    )(index, arrived.reshape(times * block, LANES), w_time, in_hbm(mix), lines, weights)
    back = lax.all_to_all(
        result.reshape(times, share, LANES), "tm", split_axis=0, concat_axis=0, tiled=True
    )
    return pl.pallas_call(
        functools.partial(unpack_kernel, sizes),
        out_shape=jax.ShapeDtypeStruct((1,) + sizes, F32),
        in_specs=[whole()],
        out_specs=whole(),
        compiler_params=params,
        name="unpack",
    )(back.reshape(columns, LANES))


def solution(mesh):
    in_specs = (
        P("groups", None, None, None),
        P(("groups", "tm")),
        P("tm", "groups", None, None, None),
        P(),
        P(),
        P(),
        P(),
        P(),
        P(),
    )
    out_specs = P("tm", "groups", None, None, None)
    return jax.shard_map(shards, mesh=mesh, in_specs=in_specs, out_specs=out_specs, check_vma=False)
```

```python
import functools
import math

import jax
import jax.numpy as jnp
from jax import lax
from jax.experimental import pallas as pl
from jax.experimental.pallas import tpu as pltpu
from jax.sharding import PartitionSpec as P

ITERS = 2
LANES = 128
SUB = 8
HALO = 2
NOISE_SCALE = 2.0
EPS = 1e-06
F32 = jnp.float32
BF16 = jnp.bfloat16
VMEM_ROOM = 10 * 1024 * 1024


def in_hbm(value):
    return pltpu.with_memory_space_constraint(value, pltpu.HBM)


def limit(scratch):
    held = [s for s in scratch if hasattr(s, "shape") and jnp.issubdtype(s.dtype, jnp.number)]
    size = sum(math.prod(s.shape) * jnp.dtype(s.dtype).itemsize for s in held)
    return pltpu.CompilerParams(vmem_limit_bytes=size + VMEM_ROOM)


def round_up(value, multiple):
    return (value + multiple - 1) // multiple * multiple


def whole(memory_space=pltpu.VMEM):
    return pl.BlockSpec(memory_space=memory_space)


def columns_as_rows(image, extra):
    channels, frames, rows, columns = image.shape
    parts = [image[c, f] for f in range(frames) for c in range(channels)]
    left = LANES - channels * frames * rows
    parts.append(jnp.full((left, columns), extra, F32))
    return jnp.transpose(jnp.concatenate(parts, axis=0))


def pack_kernel(shares, share, block, plan_ref, noise_ref, out_ref, padded):
    columns = noise_ref.shape[-1]
    edge = jnp.zeros((SUB, LANES), F32)
    padded[0:SUB, :] = edge
    padded[SUB + columns : 2 * SUB + columns, :] = edge
    padded[SUB : SUB + columns, :] = columns_as_rows(
        noise_ref[0], plan_ref[0].astype(F32)
    )
    for dest in range(shares):
        first = SUB - HALO + dest * share
        out_ref[dest, 0 : share + 2 * HALO, :] = padded[first : first + share + 2 * HALO, :]
        if block > share + 2 * HALO:
            out_ref[dest, share + 2 * HALO : block, :] = jnp.zeros(
                (block - share - 2 * HALO, LANES), F32
            )


def window_of(frame, frames):
    return min(max(frame - 1, 0), frames - 3)


def one_hot_fits(times, group):
    return 9 * group + 2 * times <= 2 * LANES and (2 * LANES - 2 * times) % 16 == 0


def stack_taps(state, window, group, times):
    width = 3 * group
    before, here, after = [
        pltpu.roll(s, (LANES - window * group + k * width) % LANES, 1)
        for k, s in enumerate(state)
    ]
    lane = lax.broadcasted_iota(jnp.int32, before.shape, 1)
    first = jnp.where(lane < width, before, here)
    spill = 2 * width - LANES
    code = jnp.zeros_like(before)
    if one_hot_fits(times, group):
        when = lax.rem(lax.broadcasted_iota(jnp.int32, before.shape, 0), times)
        at = lane - (LANES - 2 * times)
        code = jnp.where((at >= 0) & (lax.rem(at + times, times) == when), 1.0, 0.0)
    second = jnp.where(
        lane < spill, here, jnp.where(lane < spill + width, after, code)
    )
    return jnp.concatenate([first.astype(BF16), second.astype(BF16)], axis=-1)


class Table:
    def __init__(self, share, sizes):
        _, frames, rows, _ = sizes
        self.wide = round_up(share + 4 * HALO, SUB)
        self.taps = 0
        self.edges = 15 * SUB
        self.own = self.edges + round_up(3 * frames * rows, SUB)
        self.direct = self.own + self.wide
        self.out = self.direct + self.wide
        self.size = self.out + LANES


def weight_rows(frames):
    proj = 2 * frames * LANES
    return proj, proj + 2 * LANES, proj + 4 * LANES, proj + 6 * LANES


def exact(a, b):
    return jnp.dot(a, b, precision=lax.Precision.HIGHEST, preferred_element_type=F32)


def split(value):
    top = value.astype(BF16)
    return top, (value - top.astype(F32)).astype(BF16)


def prep_kernel(
    share, sizes, index_ref, start_hbm, lift_hbm, spatial_hbm, temporal_hbm, point_hbm, out_hbm,
    mix_hbm, table_ref, weight_ref,
    mix_ref, start_ref, lift_ref, spatial_ref, temporal_ref, point_ref, out_w_ref, padded, sems,
):
    channels, frames, rows, columns = sizes
    group = channels * rows
    index = index_ref[0]
    table = Table(share, sizes)
    copies = [
        pltpu.make_async_copy(source, target, sems.at[k])
        for k, (source, target) in enumerate([
            (start_hbm, start_ref), (lift_hbm, lift_ref), (spatial_hbm, spatial_ref),
            (temporal_hbm, temporal_ref), (point_hbm, point_ref), (out_hbm, out_w_ref),
        ])
    ]
    for copy in copies:
        copy.start()
    padded[...] = jnp.zeros_like(padded)
    for copy in copies:
        copy.wait()
    row = lax.broadcasted_iota(jnp.int32, (SUB, LANES), 0)

    zero = jnp.zeros((SUB, LANES), F32)
    sp = [spatial_ref[k, 0:1, :] for k in range(9)]
    tm = [temporal_ref[k, 0:1, :] for k in range(3)]
    lift = [lift_ref[c : c + 1, :] for c in range(channels)]
    timed = [[l * t for t in tm] for l in lift]
    for h in range(rows):
        by_tap = []
        for tap in range(3):
            total = zero
            for a in range(3):
                if 0 <= h + a - 1 < rows:
                    total = jnp.where(row == h + a - 1, sp[3 * a + tap], total)
            by_tap.append(total)
        made = [[[t * timed[c][k] for k in range(3)] for c in range(channels)] for t in by_tap]
        only = [jnp.where(row == h, l, 0.0) for l in lift]
        for f in range(frames):
            window = window_of(f, frames)
            mixes, ups = [], []
            for tap in range(3):
                for local in range(3):
                    k = window + local - f + 1
                    for c in range(channels):
                        mixes.append(made[tap][c][k] if 0 <= k < 3 else zero)
                        ups.append(only[c] if k == 1 and tap == 1 else zero)
            mixes += [zero] * (2 * LANES // SUB - len(mixes))
            ups += [zero] * (2 * LANES // SUB - len(ups))
            at = f % 2 * LANES
            mix_ref[h, f // 2, :, at : at + LANES] = jnp.concatenate(mixes, axis=0).astype(BF16)
            at += 2 * LANES
            mix_ref[h, f // 2, :, at : at + LANES] = jnp.concatenate(ups, axis=0).astype(BF16)
    leaving = pltpu.make_async_copy(mix_ref, mix_hbm, sems.at[6])
    leaving.start()

    lines = []
    for a in range(3):
        g = [spatial_ref[3 * a + c, 1:2, :] for c in range(3)]
        lines += [g[0], 0.5 * (g[0] + g[1] + g[2]), 0.5 * (g[0] - g[1] + g[2]), g[2]]
    lines += [temporal_ref[k, 1:2, :] for k in range(3)]
    for k, line in enumerate(lines):
        at = table.taps + k * SUB
        table_ref[at : at + SUB, :] = jnp.broadcast_to(line, (SUB, LANES))
    for tap in range(3):
        lines = []
        for f in range(frames):
            over = functools.reduce(
                jnp.add, [tm[k] for k in range(3) if 0 <= f + k - 1 < frames]
            )
            for h in range(rows):
                lines.append(over * functools.reduce(
                    jnp.add, [sp[3 * a + tap] for a in range(3) if 0 <= h + a - 1 < rows]
                ))
        at = table.edges + tap * frames * rows
        table_ref[at : at + frames * rows, :] = jnp.concatenate(lines, axis=0)

    left = jnp.zeros((LANES - frames * group, LANES), F32)
    spread = [jnp.broadcast_to(out_w_ref[c : c + 1, :], (rows, LANES)) for c in range(channels)]
    out_lanes = jnp.transpose(jnp.concatenate(spread * frames + [left], axis=0))
    table_ref[table.out : table.out + LANES, :] = out_lanes
    lane = lax.broadcasted_iota(jnp.int32, (LANES, LANES), 1)
    line = lax.broadcasted_iota(jnp.int32, (LANES, LANES), 0)
    first = jnp.where(lax.rem(lane, rows) == 0, out_lanes, 0.0)
    for slot, b in enumerate((1, 0)):
        folded = exact(point_ref[b].astype(F32), first)
        for f in range(frames):
            here = jnp.where((lane >= f * group) & (lane < (f + 1) * group), folded, 0.0)
            at = (slot * frames + f) * LANES
            weight_ref[at : at + LANES, 0:LANES], weight_ref[at : at + LANES, LANES:] = split(here)
    lift_rows = [jnp.broadcast_to(l, (rows, LANES)) for l in lift]
    both = exact(jnp.concatenate(lift_rows * frames + [left], axis=0), out_lanes)
    same = (lax.div(lane, group) == lax.div(line, group)) & (
        lax.rem(lane, rows) == lax.rem(line, rows)
    )
    both = jnp.where(same, both, 0.0)
    proj, direct, mixing, _ = weight_rows(frames)
    hi, lo = split(both)
    nothing = jnp.zeros((LANES, LANES), BF16)
    weight_ref[proj : proj + LANES, 0:LANES] = hi
    weight_ref[proj : proj + LANES, LANES:] = lo
    weight_ref[proj + LANES : direct, 0:LANES] = hi
    weight_ref[proj + LANES : direct, LANES:] = nothing
    for at, value in ((direct, point_ref[0]), (mixing, jnp.full((LANES, LANES), 4.0 / LANES, BF16))):
        weight_ref[at : at + LANES, 0:LANES] = value
        weight_ref[at + LANES : at + 2 * LANES, LANES:] = value
        weight_ref[at : at + LANES, LANES:] = nothing
        weight_ref[at + LANES : at + 2 * LANES, 0:LANES] = nothing

    lead = 2 * HALO + SUB
    padded[lead : lead + columns, :] = columns_as_rows(start_ref[...], 0.0)
    own = padded[pl.ds(SUB + index * share, table.wide), :]
    table_ref[table.own : table.own + table.wide, :] = own
    table_ref[table.direct : table.direct + table.wide, :] = exact(own, both)
    leaving.wait()


def main_kernel(
    share, sizes, times, block, index_ref, noise_ref, time_ref, mix_hbm, table_ref, weight_ref,
    out_ref, feats, fresh, mixed_buf, normed_buf, acc, state, left_buf, mix_ref, sems,
):
    channels, frames, rows, columns = sizes
    group = channels * rows
    index = index_ref[0]
    step = 1.0 / times
    table = Table(share, sizes)
    halves = times // SUB
    proj, direct, mixing, mean_end = weight_rows(frames)
    hot = one_hot_fits(times, group)

    def arrival(h):
        return pltpu.make_async_copy(mix_hbm.at[h], mix_ref.at[h], sems.at[h])

    for h in range(3):
        arrival(h).start()
    for h in (0, rows + 1):
        feats[:, h] = jnp.zeros(feats.shape[:1] + feats.shape[2:], F32)

    half = LANES // 2
    planned = noise_ref[pl.ds(HALO, times, stride=block), :][:, LANES - 1 : LANES]
    lane = lax.broadcasted_iota(jnp.int32, (1, LANES), 1)
    place = jnp.where(lane < half, lane, lane - half).astype(F32)
    angles = planned * jnp.exp(place * (-math.log(1000.0) / half))
    embedded = jnp.where(lane < half, jnp.sin(angles), jnp.cos(angles))
    bias = exact(embedded, time_ref[...])
    bias_out = exact(bias, table_ref[table.out : table.out + LANES, :])

    def mean_square(pair):
        return jnp.dot(
            (pair * pair).astype(BF16), weight_ref[mixing:mean_end, :], preferred_element_type=F32
        )

    def normalise(pair, mean):
        value = pair * lax.rsqrt(mean + 4.0 * EPS)
        return (value + value * jnp.tanh(value)).astype(BF16)

    def in_pairs(values):
        return jnp.concatenate(
            [jnp.concatenate(values[f : f + 2], axis=1) for f in range(0, frames, 2)], axis=0
        )

    def by_frame(pairs, cells):
        return jnp.concatenate(
            [pairs[k * cells : (k + 1) * cells] for k in range(frames // 2)], axis=1
        )

    def bias_taps(h):
        return [
            jnp.concatenate(
                [
                    bias * table_ref[pl.ds(table.edges + (k * frames + f) * rows + h, 1), :]
                    for f in range(frames)
                ],
                axis=1,
            )
            for k in range(3)
        ]

    def receive(h):
        arrival(h).wait()
        if hot:
            by_tap = bias_taps(h)
            every = by_tap[0] + by_tap[1] + by_tap[2]
            at = 2 * LANES - 2 * times
            for p in range(frames // 2):
                here = every[:, 2 * p * LANES : 2 * (p + 1) * LANES]
                terms = jnp.concatenate([here, bias, bias], axis=1)
                mix_ref[h, p, at : at + times, :], mix_ref[h, p, at + times :, :] = split(terms)

    def run_network(cols, first_time):
        wide = cols + 2
        cells = cols * times
        many = wide * times
        margin = (wide - share) // 2
        flags = {}
        for j in list(range(margin)) + list(range(wide - margin, wide)):
            col = index * share + j - margin
            flags[j] = jnp.where((col >= 0) & (col < columns), 1.0, 0.0).astype(F32)
        at_left = jnp.where(index == 0, 1.0, 0.0).astype(F32)
        at_right = jnp.where((index + 1) * share == columns, 1.0, 0.0).astype(F32)
        taps = [table_ref[table.taps + k * SUB : table.taps + (k + 1) * SUB, :] for k in range(15)]
        around = [state[k : k + wide].reshape(many, LANES) for k in range(3)]
        for p in range(frames // 2):
            left_buf[p, 0:many, :] = stack_taps(around, p, group, times)

        def block_one(h):
            linear = [
                jnp.dot(
                    left_buf[p, 0:many, :], mix_ref[h, p, :, 0 : 2 * LANES],
                    preferred_element_type=F32,
                )
                for p in range(frames // 2)
            ]
            yield
            by_tap = bias_taps(h)
            parts = []
            for p in range(frames // 2):
                lanes = slice(2 * p * LANES, 2 * (p + 1) * LANES)
                mixed = linear[p]
                if not hot:
                    every = by_tap[0] + by_tap[1] + by_tap[2]
                    mixed = mixed + jnp.concatenate([every[:, lanes]] * wide, axis=0)
                one, two = margin * times, (wide - margin - 1) * times
                if one == two:
                    edge = by_tap[0][:, lanes] * at_left + by_tap[2][:, lanes] * at_right
                    middle = [mixed[one : one + times] - edge]
                else:
                    middle = [
                        mixed[one : one + times] - by_tap[0][:, lanes] * at_left,
                        mixed[one + times : two],
                        mixed[two : two + times] - by_tap[2][:, lanes] * at_right,
                    ]
                parts += [mixed[:one]] + middle + [mixed[two + times :]]
            pair = jnp.concatenate([x for x in parts if x.shape[0]], axis=0)
            mean = mean_square(pair)
            yield
            normed = normalise(pair, mean)
            normed_buf[h, 0:cells, :] = by_frame(normed, many)[times : times + cells]
            updates = []
            for p in range(frames // 2):
                both = jnp.concatenate([normed[p * many : (p + 1) * many], left_buf[p, 0:many, :]], axis=1)
                onto = jnp.concatenate(
                    [weight_ref[direct:mixing, :], mix_ref[h, p, :, 2 * LANES :]], axis=0
                )
                updates.append(jnp.dot(both, onto, preferred_element_type=F32))
            yield
            for p in range(frames // 2):
                fresh[p, 0:many, :] = updates[p]
            yield

        def settle(lines, line):
            for f in range(frames):
                lanes = slice(f % 2 * LANES, (f % 2 + 1) * LANES)
                new = []
                for j in range(wide):
                    value = fresh[f // 2, j * times : (j + 1) * times, lanes]
                    if not hot:
                        value = value + bias
                    value = value.reshape(halves, SUB, LANES)
                    new.append(value * flags[j] if j in flags else value)
                for q in range(cols // 2):
                    d = new[2 * q : 2 * q + 4]
                    lines[f, line, q, 0] = d[0] - d[2]
                    lines[f, line, q, 1] = d[1] + d[2]
                    lines[f, line, q, 2] = d[2] - d[1]
                    lines[f, line, q, 3] = d[1] - d[3]

        def convolve(h, lines, begin, end):
            for q in range(begin, end):
                spread = []
                for f in range(frames):
                    m = []
                    for i in range(4):
                        terms = [lines[f, a, q, i] * taps[4 * a + i] for a in range(3)]
                        m.append(terms[0] + terms[1] + terms[2])
                    spread.append((m[0] + m[1] + m[2], m[1] - m[2] - m[3]))
                for f in range(frames):
                    for side in range(2):
                        total = None
                        for k in range(3):
                            if 0 <= f + k - 1 < frames:
                                term = spread[f + k - 1][side] * taps[12 + k]
                                total = term if total is None else total + term
                        at = (2 * q + side) * times
                        mixed_buf[lax.rem(h, 2), f, at : at + times, :] = total.reshape(times, LANES)

        def finish(h, slot):
            pair = in_pairs([mixed_buf[slot, f, 0:cells, :] for f in range(frames)])
            mean = mean_square(pair)
            yield
            normed = by_frame(normalise(pair, mean), cells)
            left = jnp.concatenate([normed, normed_buf[h, 0:cells, :]], axis=1)
            out = jnp.dot(left, weight_ref[0:proj, :], preferred_element_type=F32)
            yield
            out = out[:, 0:LANES] + out[:, LANES:]
            acc[0:cells, :] += pltpu.roll(out, h, 1)
            yield

        acc[0:cells, :] = jnp.zeros((cells, LANES), F32)
        pairs = cols // 2

        def receive_next(h):
            if first_time and isinstance(h, int):
                receive(h)
            elif first_time:

                @pl.when(h < rows)
                def _():
                    receive(h)

        def steady(h, carry):
            lines = feats.at[:, pl.ds(h, 3)]
            ending, starting = finish(h - 1, lax.rem(h + 1, 2)), block_one(h + 2)
            settle(lines, 2)
            next(starting)
            next(ending)
            next(starting)
            convolve(h, lines, 0, pairs)
            next(ending)
            next(starting)
            next(ending)
            next(starting)
            receive_next(h + 3)
            return carry

        if first_time:
            receive(0)
            receive(1)
            for h in range(3, rows):
                arrival(h).start()
        ahead = block_one(0)
        for _ in ahead:
            pass
        settle(feats, 1)
        for _ in block_one(1):
            pass
        receive_next(2)
        settle(feats, 2)
        starting = block_one(2)
        next(starting)
        convolve(0, feats, 0, pairs)
        for _ in starting:
            pass
        receive_next(3)
        lax.fori_loop(1, rows - 2, steady, 0)
        lines = feats.at[:, pl.ds(rows - 2, 3)]
        settle(lines, 2)
        ending = finish(rows - 3, (rows - 3) % 2)
        next(ending)
        convolve(rows - 2, lines, 0, pairs)
        for _ in ending:
            pass
        ending = finish(rows - 2, (rows - 2) % 2)
        next(ending)
        convolve(rows - 1, feats.at[:, pl.ds(rows - 1, 3)], 0, pairs)
        for _ in ending:
            pass
        for _ in finish(rows - 1, (rows - 1) % 2):
            pass

    def drift(cols, skip, through):
        f = acc[0 : cols * times, :].reshape(cols, times, LANES) + through + bias_out[None]
        noise = jnp.stack(
            [noise_ref[pl.ds(skip + j, times, stride=block), :] for j in range(cols)]
        )
        return step * f + (NOISE_SCALE * math.sqrt(step)) * noise

    def running(values):
        when = lax.broadcasted_iota(jnp.int32, values.shape, 1)
        reach = 1
        while reach < times:
            values = values + jnp.where(when >= reach, pltpu.roll(values, reach, 1), 0.0)
            reach *= 2
        return values

    cols = share + 2 * HALO
    for j in range(cols + 4):
        at = table.own + j
        state[j] = jnp.broadcast_to(table_ref[at : at + 1, :], (times, LANES))
    run_network(cols, True)
    begin = table_ref[table.own + HALO : table.own + HALO + cols, :][:, None, :]
    through = table_ref[table.direct + HALO : table.direct + HALO + cols, :][:, None, :]
    moved = drift(cols, 0, through)
    col = lax.broadcasted_iota(jnp.int32, moved.shape, 0) + (index * share - HALO)
    inside = (col >= 0) & (col < columns)
    state[0:cols] = begin + jnp.where(inside, running(moved) - moved, 0.0)

    run_network(share, False)
    hi, lo = split(state[HALO : HALO + share].reshape(share * times, LANES))
    through = jnp.dot(
        jnp.concatenate([hi, lo], axis=1), weight_ref[proj:direct, :], preferred_element_type=F32
    )
    through = (through[:, 0:LANES] + through[:, LANES:]).reshape(share, times, LANES)
    own = table.own + 2 * HALO
    ended = table_ref[own : own + share, :][:, None, :] + running(drift(share, HALO, through))
    for j in range(share):
        out_ref[pl.ds(j, times, stride=share), :] = ended[j]


def unpack_kernel(sizes, in_ref, out_ref):
    channels, frames, rows, _ = sizes
    image = jnp.transpose(in_ref[...])
    for f in range(frames):
        for c in range(channels):
            at = (f * channels + c) * rows
            out_ref[0, c, f] = image[at : at + rows, :]


def shards(start_frames, plan, noise, w_lift, w_time, spatial, temporal, w_point, w_out):
    times = lax.axis_size("tm")
    sizes = start_frames.shape
    channels, frames, rows, columns = sizes
    share = columns // times
    block = round_up(share + 2 * HALO, SUB)
    cols = share + 2 * HALO
    table = Table(share, sizes)
    params = limit([])
    prep_scratch = [pltpu.VMEM((rows, frames // 2, 2 * LANES, 4 * LANES), BF16), pltpu.VMEM(sizes, F32)]
    main_scratch = [
        pltpu.VMEM((frames, rows + 2, cols // 2, 4, times // SUB, SUB, LANES), F32),
        pltpu.VMEM((frames // 2, (cols + 2) * times, 2 * LANES), F32),
        pltpu.VMEM((2, frames, cols * times, LANES), F32),
        pltpu.VMEM((rows, cols * times, frames * LANES), BF16),
        pltpu.VMEM((cols * times, LANES), F32),
        pltpu.VMEM((cols + 4, times, LANES), F32),
        pltpu.VMEM((frames // 2, (cols + 2) * times, 2 * LANES), BF16),
        pltpu.VMEM((rows, frames // 2, 2 * LANES, 4 * LANES), BF16),
    ]
    index = lax.axis_index("tm").astype(jnp.int32).reshape(1)
    hbm = whole(pltpu.HBM)

    packed = pl.pallas_call(
        functools.partial(pack_kernel, times, share, block),
        out_shape=pltpu.VMEM((times, block, LANES), F32),
        in_specs=[whole(pltpu.SMEM), whole()],
        out_specs=whole(),
        scratch_shapes=[pltpu.VMEM((columns + 2 * SUB, LANES), F32)],
        compiler_params=params,
        name="pack",
    )(plan, noise)
    arrived = lax.all_to_all(packed, "tm", split_axis=0, concat_axis=0, tiled=True)

    by_tap = (
        w_lift, jnp.transpose(spatial, (2, 0, 1)), jnp.transpose(temporal, (2, 0, 1)), w_point,
        jnp.transpose(w_out),
    )
    mix, lines, weights = pl.pallas_call(
        functools.partial(prep_kernel, share, sizes),
        out_shape=[
            pltpu.HBM((rows, frames // 2, 2 * LANES, 4 * LANES), BF16),
            pltpu.VMEM((table.size, LANES), F32),
            pltpu.VMEM((weight_rows(frames)[-1], 2 * LANES), BF16),
        ],
        in_specs=[whole(pltpu.SMEM)] + [hbm] * 6,
        out_specs=[hbm] + [whole()] * 2,
        scratch_shapes=prep_scratch
        + [pltpu.VMEM(a.shape, a.dtype) for a in by_tap]
        + [
            pltpu.VMEM((columns + 4 * SUB + table.wide, LANES), F32),
            pltpu.SemaphoreType.DMA((7,)),
        ],
        compiler_params=limit(prep_scratch),
        cost_estimate=pl.CostEstimate(flops=10**9, bytes_accessed=10**7, transcendentals=0),
        name="prep",
    )(index, *[in_hbm(a) for a in (start_frames,) + by_tap])

    result = pl.pallas_call(
        functools.partial(main_kernel, share, sizes, times, block),
        out_shape=jax.ShapeDtypeStruct((times * share, LANES), F32),
        in_specs=[whole(pltpu.SMEM), whole(), whole(), hbm, whole(), whole()],
        out_specs=whole(),
        scratch_shapes=main_scratch + [pltpu.SemaphoreType.DMA((rows,))],
        compiler_params=limit(main_scratch),
        name="sampler",
    )(index, arrived.reshape(times * block, LANES), w_time, in_hbm(mix), lines, weights)
    back = lax.all_to_all(
        result.reshape(times, share, LANES), "tm", split_axis=0, concat_axis=0, tiled=True
    )
    return pl.pallas_call(
        functools.partial(unpack_kernel, sizes),
        out_shape=jax.ShapeDtypeStruct((1,) + sizes, F32),
        in_specs=[whole()],
        out_specs=whole(),
        compiler_params=params,
        name="unpack",
    )(back.reshape(columns, LANES))


def solution(mesh):
    in_specs = (
        P("groups", None, None, None),
        P(("groups", "tm")),
        P("tm", "groups", None, None, None),
        P(),
        P(),
        P(),
        P(),
        P(),
        P(),
    )
    out_specs = P("tm", "groups", None, None, None)
    return jax.shard_map(shards, mesh=mesh, in_specs=in_specs, out_specs=out_specs, check_vma=False)
```

```python
import functools
import math

import jax
import jax.numpy as jnp
from jax import lax
from jax.experimental import pallas as pl
from jax.experimental.pallas import tpu as pltpu
from jax.sharding import PartitionSpec as P

ITERS = 2
LANES = 128
SUB = 8
HALO = 2
NOISE_SCALE = 2.0
EPS = 1e-06
AHEAD = 3
F32 = jnp.float32
BF16 = jnp.bfloat16
VMEM_ROOM = 12 * 1024 * 1024


def in_hbm(value):
    return pltpu.with_memory_space_constraint(value, pltpu.HBM)


def limit(scratch):
    held = [s for s in scratch if hasattr(s, "shape") and jnp.issubdtype(s.dtype, jnp.number)]
    size = sum(math.prod(s.shape) * jnp.dtype(s.dtype).itemsize for s in held)
    return pltpu.CompilerParams(vmem_limit_bytes=size + VMEM_ROOM)


def round_up(value, multiple):
    return (value + multiple - 1) // multiple * multiple


def whole(memory_space=pltpu.VMEM):
    return pl.BlockSpec(memory_space=memory_space)


def columns_as_rows(image, extra):
    channels, frames, rows, columns = image.shape
    parts = [image[c, f] for f in range(frames) for c in range(channels)]
    left = LANES - channels * frames * rows
    parts.append(jnp.full((left, columns), extra, F32))
    return jnp.transpose(jnp.concatenate(parts, axis=0))


def pack_kernel(shares, share, block, plan_ref, noise_ref, out_ref, padded):
    columns = noise_ref.shape[-1]
    edge = jnp.zeros((SUB, LANES), F32)
    padded[0:SUB, :] = edge
    padded[SUB + columns : 2 * SUB + columns, :] = edge
    padded[SUB : SUB + columns, :] = columns_as_rows(
        noise_ref[0], plan_ref[0].astype(F32)
    )
    for dest in range(shares):
        first = SUB - HALO + dest * share
        out_ref[dest, 0 : share + 2 * HALO, :] = padded[first : first + share + 2 * HALO, :]
        if block > share + 2 * HALO:
            out_ref[dest, share + 2 * HALO : block, :] = jnp.zeros(
                (block - share - 2 * HALO, LANES), F32
            )


def window_of(frame, frames):
    return min(max(frame - 1, 0), frames - 3)


def one_hot_fits(times, group):
    return 9 * group + 2 * times <= 2 * LANES and (2 * LANES - 2 * times) % 16 == 0


def stack_taps(state, window, group, times):
    width = 3 * group
    before, here, after = [
        pltpu.roll(s, (LANES - window * group + k * width) % LANES, 1)
        for k, s in enumerate(state)
    ]
    lane = lax.broadcasted_iota(jnp.int32, before.shape, 1)
    first = jnp.where(lane < width, before, here)
    spill = 2 * width - LANES
    code = jnp.zeros_like(before)
    if one_hot_fits(times, group):
        when = lax.rem(lax.broadcasted_iota(jnp.int32, before.shape, 0), times)
        at = lane - (LANES - 2 * times)
        code = jnp.where((at >= 0) & (lax.rem(at + times, times) == when), 1.0, 0.0)
    second = jnp.where(
        lane < spill, here, jnp.where(lane < spill + width, after, code)
    )
    return jnp.concatenate([first.astype(BF16), second.astype(BF16)], axis=-1)


class Table:
    def __init__(self, share, sizes):
        _, frames, rows, _ = sizes
        self.wide = round_up(share + 4 * HALO, SUB)
        self.taps = 0
        self.edges = 15 * SUB
        self.own = self.edges + round_up(3 * frames * rows, SUB)
        self.direct = self.own + self.wide
        self.out = self.direct + self.wide
        self.size = self.out + LANES


def weight_rows(frames):
    proj = 2 * frames * LANES
    return proj, proj + 2 * LANES, proj + 4 * LANES, proj + 6 * LANES


def exact(a, b):
    return jnp.dot(a, b, precision=lax.Precision.HIGHEST, preferred_element_type=F32)


def split(value):
    top = value.astype(BF16)
    return top, (value - top.astype(F32)).astype(BF16)


def prep_kernel(
    share, sizes, index_ref, start_hbm, lift_hbm, spatial_hbm, temporal_hbm, point_hbm, out_hbm,
    first_ref, mix_hbm, table_ref, weight_ref,
    mix_ref, start_ref, lift_ref, spatial_ref, temporal_ref, point_ref, out_w_ref, padded, sems,
):
    channels, frames, rows, columns = sizes
    group = channels * rows
    index = index_ref[0]
    table = Table(share, sizes)
    plain = mix_ref.shape[2]
    copies = [
        pltpu.make_async_copy(source, target, sems.at[k])
        for k, (source, target) in enumerate([
            (start_hbm, start_ref), (lift_hbm, lift_ref), (spatial_hbm, spatial_ref),
            (temporal_hbm, temporal_ref), (point_hbm, point_ref), (out_hbm, out_w_ref),
        ])
    ]
    for copy in copies:
        copy.start()
    padded[...] = jnp.zeros_like(padded)
    for copy in copies:
        copy.wait()
    row = lax.broadcasted_iota(jnp.int32, (SUB, LANES), 0)

    zero = jnp.zeros((SUB, LANES), F32)
    sp = [spatial_ref[k, 0:1, :] for k in range(9)]
    tm = [temporal_ref[k, 0:1, :] for k in range(3)]
    lift = [lift_ref[c : c + 1, :] for c in range(channels)]
    timed = [[l * t for t in tm] for l in lift]
    for h in range(rows):
        by_tap = []
        for tap in range(3):
            total = zero
            for a in range(3):
                if 0 <= h + a - 1 < rows:
                    total = jnp.where(row == h + a - 1, sp[3 * a + tap], total)
            by_tap.append(total)
        made = [[[t * timed[c][k] for k in range(3)] for c in range(channels)] for t in by_tap]
        only = [jnp.where(row == h, l, 0.0) for l in lift]
        for f in range(frames):
            window = window_of(f, frames)
            mixes, ups = [], []
            for tap in range(3):
                for local in range(3):
                    k = window + local - f + 1
                    for c in range(channels):
                        mixes.append(made[tap][c][k] if 0 <= k < 3 else zero)
                        ups.append(only[c] if k == 1 and tap == 1 else zero)
            mixes += [zero] * (plain // SUB - len(mixes))
            ups += [zero] * (plain // SUB - len(ups))
            target, line = (first_ref, h) if h < AHEAD else (mix_ref, h - AHEAD)
            at = f % 2 * LANES
            target[line, f // 2, :, at : at + LANES] = jnp.concatenate(mixes, axis=0).astype(BF16)
            at += 2 * LANES
            target[line, f // 2, :, at : at + LANES] = jnp.concatenate(ups, axis=0).astype(BF16)
    leaving = pltpu.make_async_copy(mix_ref, mix_hbm, sems.at[6])
    leaving.start()

    lines = []
    for a in range(3):
        g = [spatial_ref[3 * a + c, 1:2, :] for c in range(3)]
        lines += [g[0], 0.5 * (g[0] + g[1] + g[2]), 0.5 * (g[0] - g[1] + g[2]), g[2]]
    lines += [temporal_ref[k, 1:2, :] for k in range(3)]
    for k, line in enumerate(lines):
        at = table.taps + k * SUB
        table_ref[at : at + SUB, :] = jnp.broadcast_to(line, (SUB, LANES))
    for tap in range(3):
        lines = []
        for f in range(frames):
            over = functools.reduce(
                jnp.add, [tm[k] for k in range(3) if 0 <= f + k - 1 < frames]
            )
            for h in range(rows):
                lines.append(over * functools.reduce(
                    jnp.add, [sp[3 * a + tap] for a in range(3) if 0 <= h + a - 1 < rows]
                ))
        at = table.edges + tap * frames * rows
        table_ref[at : at + frames * rows, :] = jnp.concatenate(lines, axis=0)

    left = jnp.zeros((LANES - frames * group, LANES), F32)
    spread = [jnp.broadcast_to(out_w_ref[c : c + 1, :], (rows, LANES)) for c in range(channels)]
    out_lanes = jnp.transpose(jnp.concatenate(spread * frames + [left], axis=0))
    table_ref[table.out : table.out + LANES, :] = out_lanes
    lane = lax.broadcasted_iota(jnp.int32, (LANES, LANES), 1)
    line = lax.broadcasted_iota(jnp.int32, (LANES, LANES), 0)
    first = jnp.where(lax.rem(lane, rows) == 0, out_lanes, 0.0)
    for slot, b in enumerate((1, 0)):
        folded = exact(point_ref[b].astype(F32), first)
        for f in range(frames):
            here = jnp.where((lane >= f * group) & (lane < (f + 1) * group), folded, 0.0)
            at = (slot * frames + f) * LANES
            weight_ref[at : at + LANES, 0:LANES], weight_ref[at : at + LANES, LANES:] = split(here)
    lift_rows = [jnp.broadcast_to(l, (rows, LANES)) for l in lift]
    both = exact(jnp.concatenate(lift_rows * frames + [left], axis=0), out_lanes)
    same = (lax.div(lane, group) == lax.div(line, group)) & (
        lax.rem(lane, rows) == lax.rem(line, rows)
    )
    both = jnp.where(same, both, 0.0)
    proj, direct, mixing, _ = weight_rows(frames)
    hi, lo = split(both)
    nothing = jnp.zeros((LANES, LANES), BF16)
    weight_ref[proj : proj + LANES, 0:LANES] = hi
    weight_ref[proj : proj + LANES, LANES:] = lo
    weight_ref[proj + LANES : direct, 0:LANES] = hi
    weight_ref[proj + LANES : direct, LANES:] = nothing
    for at, value in ((direct, point_ref[0]), (mixing, jnp.full((LANES, LANES), 4.0 / LANES, BF16))):
        weight_ref[at : at + LANES, 0:LANES] = value
        weight_ref[at + LANES : at + 2 * LANES, LANES:] = value
        weight_ref[at : at + LANES, LANES:] = nothing
        weight_ref[at + LANES : at + 2 * LANES, 0:LANES] = nothing

    lead = 2 * HALO + SUB
    padded[lead : lead + columns, :] = columns_as_rows(start_ref[...], 0.0)
    own = padded[pl.ds(SUB + index * share, table.wide), :]
    table_ref[table.own : table.own + table.wide, :] = own
    table_ref[table.direct : table.direct + table.wide, :] = exact(own, both)
    leaving.wait()


def main_kernel(
    share, sizes, times, block, index_ref, noise_ref, time_ref, first_ref, mix_hbm, table_ref, weight_ref,
    out_ref, feats, fresh, mixed_buf, normed_buf, acc, state, left_buf, mix_ref, hot_ref, sems,
):
    channels, frames, rows, columns = sizes
    group = channels * rows
    index = index_ref[0]
    step = 1.0 / times
    table = Table(share, sizes)
    halves = times // SUB
    proj, direct, mixing, mean_end = weight_rows(frames)
    hot = one_hot_fits(times, group)

    def arrival(k):
        return pltpu.make_async_copy(mix_hbm.at[k], mix_ref.at[k], sems.at[k])

    for k in range(rows - AHEAD):
        arrival(k).start()
    for h in (0, rows + 1):
        feats[:, h] = jnp.zeros(feats.shape[:1] + feats.shape[2:], F32)

    half = LANES // 2
    planned = noise_ref[pl.ds(HALO, times, stride=block), :][:, LANES - 1 : LANES]
    lane = lax.broadcasted_iota(jnp.int32, (1, LANES), 1)
    place = jnp.where(lane < half, lane, lane - half).astype(F32)
    angles = planned * jnp.exp(place * (-math.log(1000.0) / half))
    embedded = jnp.where(lane < half, jnp.sin(angles), jnp.cos(angles))
    bias = exact(embedded, time_ref[...])
    bias_out = exact(bias, table_ref[table.out : table.out + LANES, :])

    def mean_square(pair):
        return jnp.dot(
            (pair * pair).astype(BF16), weight_ref[mixing:mean_end, :], preferred_element_type=F32
        )

    def normalise(pair, mean):
        value = pair * lax.rsqrt(mean + 4.0 * EPS)
        return (value + value * jnp.tanh(value)).astype(BF16)

    def in_pairs(values):
        return jnp.concatenate(
            [jnp.concatenate(values[f : f + 2], axis=1) for f in range(0, frames, 2)], axis=0
        )

    def by_frame(pairs, cells):
        return jnp.concatenate(
            [pairs[k * cells : (k + 1) * cells] for k in range(frames // 2)], axis=1
        )

    def bias_taps(h):
        return [
            jnp.concatenate(
                [
                    bias * table_ref[pl.ds(table.edges + (k * frames + f) * rows + h, 1), :]
                    for f in range(frames)
                ],
                axis=1,
            )
            for k in range(3)
        ]

    def receive(h):
        if not isinstance(h, int):
            arrival(h - AHEAD).wait()
        elif h >= AHEAD:
            arrival(h - AHEAD).wait()
        if hot:
            by_tap = bias_taps(h)
            every = by_tap[0] + by_tap[1] + by_tap[2]
            for p in range(frames // 2):
                here = every[:, 2 * p * LANES : 2 * (p + 1) * LANES]
                terms = jnp.concatenate([here, bias, bias], axis=1)
                hot_ref[h, p, 0:times, :], hot_ref[h, p, times:, :] = split(terms)

    def lift_weights(h, p, lanes):
        if isinstance(h, int) and h < AHEAD:
            taken = first_ref[h, p, :, lanes]
        else:
            taken = mix_ref[h - AHEAD, p, :, lanes]
        return jnp.concatenate([taken, hot_ref[h, p, :, lanes]], axis=0) if hot else taken

    def run_network(cols, first_time):
        wide = cols + 2
        cells = cols * times
        many = wide * times
        margin = (wide - share) // 2
        flags = {}
        for j in list(range(margin)) + list(range(wide - margin, wide)):
            col = index * share + j - margin
            flags[j] = jnp.where((col >= 0) & (col < columns), 1.0, 0.0).astype(F32)
        at_left = jnp.where(index == 0, 1.0, 0.0).astype(F32)
        at_right = jnp.where((index + 1) * share == columns, 1.0, 0.0).astype(F32)
        taps = [table_ref[table.taps + k * SUB : table.taps + (k + 1) * SUB, :] for k in range(15)]
        around = [state[k : k + wide].reshape(many, LANES) for k in range(3)]
        for p in range(frames // 2):
            left_buf[p, 0:many, :] = stack_taps(around, p, group, times)

        def block_one(h):
            linear = [
                jnp.dot(
                    left_buf[p, 0:many, :], lift_weights(h, p, slice(0, 2 * LANES)),
                    preferred_element_type=F32,
                )
                for p in range(frames // 2)
            ]
            yield
            by_tap = bias_taps(h)
            parts = []
            for p in range(frames // 2):
                lanes = slice(2 * p * LANES, 2 * (p + 1) * LANES)
                mixed = linear[p]
                if not hot:
                    every = by_tap[0] + by_tap[1] + by_tap[2]
                    mixed = mixed + jnp.concatenate([every[:, lanes]] * wide, axis=0)
                one, two = margin * times, (wide - margin - 1) * times
                if one == two:
                    edge = by_tap[0][:, lanes] * at_left + by_tap[2][:, lanes] * at_right
                    middle = [mixed[one : one + times] - edge]
                else:
                    middle = [
                        mixed[one : one + times] - by_tap[0][:, lanes] * at_left,
                        mixed[one + times : two],
                        mixed[two : two + times] - by_tap[2][:, lanes] * at_right,
                    ]
                parts += [mixed[:one]] + middle + [mixed[two + times :]]
            pair = jnp.concatenate([x for x in parts if x.shape[0]], axis=0)
            mean = mean_square(pair)
            yield
            normed = normalise(pair, mean)
            normed_buf[h, 0:cells, :] = by_frame(normed, many)[times : times + cells]
            updates = []
            for p in range(frames // 2):
                both = jnp.concatenate([normed[p * many : (p + 1) * many], left_buf[p, 0:many, :]], axis=1)
                onto = jnp.concatenate(
                    [weight_ref[direct:mixing, :], lift_weights(h, p, slice(2 * LANES, 4 * LANES))], axis=0
                )
                updates.append(jnp.dot(both, onto, preferred_element_type=F32))
            yield
            for p in range(frames // 2):
                fresh[p, 0:many, :] = updates[p]
            yield

        def settle(lines, line):
            for f in range(frames):
                lanes = slice(f % 2 * LANES, (f % 2 + 1) * LANES)
                new = []
                for j in range(wide):
                    value = fresh[f // 2, j * times : (j + 1) * times, lanes]
                    if not hot:
                        value = value + bias
                    value = value.reshape(halves, SUB, LANES)
                    new.append(value * flags[j] if j in flags else value)
                for q in range(cols // 2):
                    d = new[2 * q : 2 * q + 4]
                    lines[f, line, q, 0] = d[0] - d[2]
                    lines[f, line, q, 1] = d[1] + d[2]
                    lines[f, line, q, 2] = d[2] - d[1]
                    lines[f, line, q, 3] = d[1] - d[3]

        def convolve(h, lines, begin, end):
            for q in range(begin, end):
                spread = []
                for f in range(frames):
                    m = []
                    for i in range(4):
                        terms = [lines[f, a, q, i] * taps[4 * a + i] for a in range(3)]
                        m.append(terms[0] + terms[1] + terms[2])
                    spread.append((m[0] + m[1] + m[2], m[1] - m[2] - m[3]))
                for f in range(frames):
                    for side in range(2):
                        total = None
                        for k in range(3):
                            if 0 <= f + k - 1 < frames:
                                term = spread[f + k - 1][side] * taps[12 + k]
                                total = term if total is None else total + term
                        at = (2 * q + side) * times
                        mixed_buf[lax.rem(h, 2), f, at : at + times, :] = total.reshape(times, LANES)

        def finish(h, slot):
            pair = in_pairs([mixed_buf[slot, f, 0:cells, :] for f in range(frames)])
            mean = mean_square(pair)
            yield
            normed = by_frame(normalise(pair, mean), cells)
            left = jnp.concatenate([normed, normed_buf[h, 0:cells, :]], axis=1)
            out = jnp.dot(left, weight_ref[0:proj, :], preferred_element_type=F32)
            yield
            out = out[:, 0:LANES] + out[:, LANES:]
            acc[0:cells, :] += pltpu.roll(out, h, 1)
            yield

        acc[0:cells, :] = jnp.zeros((cells, LANES), F32)
        pairs = cols // 2

        def receive_next(h):
            if first_time and isinstance(h, int):
                receive(h)
            elif first_time:

                @pl.when(h < rows)
                def _():
                    receive(h)

        def steady(h, carry):
            lines = feats.at[:, pl.ds(h, 3)]
            ending, starting = finish(h - 1, lax.rem(h + 1, 2)), block_one(h + 2)
            settle(lines, 2)
            next(starting)
            next(ending)
            next(starting)
            convolve(h, lines, 0, pairs)
            next(ending)
            next(starting)
            next(ending)
            next(starting)
            receive_next(h + 3)
            return carry

        if first_time:
            receive(0)
            receive(1)
        ahead = block_one(0)
        for _ in ahead:
            pass
        settle(feats, 1)
        for _ in block_one(1):
            pass
        receive_next(2)
        settle(feats, 2)
        starting = block_one(2)
        next(starting)
        convolve(0, feats, 0, pairs)
        for _ in starting:
            pass
        receive_next(3)
        lax.fori_loop(1, rows - 2, steady, 0)
        lines = feats.at[:, pl.ds(rows - 2, 3)]
        settle(lines, 2)
        ending = finish(rows - 3, (rows - 3) % 2)
        next(ending)
        convolve(rows - 2, lines, 0, pairs)
        for _ in ending:
            pass
        ending = finish(rows - 2, (rows - 2) % 2)
        next(ending)
        convolve(rows - 1, feats.at[:, pl.ds(rows - 1, 3)], 0, pairs)
        for _ in ending:
            pass
        for _ in finish(rows - 1, (rows - 1) % 2):
            pass

    def drift(cols, skip, through):
        f = acc[0 : cols * times, :].reshape(cols, times, LANES) + through + bias_out[None]
        noise = jnp.stack(
            [noise_ref[pl.ds(skip + j, times, stride=block), :] for j in range(cols)]
        )
        return step * f + (NOISE_SCALE * math.sqrt(step)) * noise

    def running(values):
        when = lax.broadcasted_iota(jnp.int32, values.shape, 1)
        reach = 1
        while reach < times:
            values = values + jnp.where(when >= reach, pltpu.roll(values, reach, 1), 0.0)
            reach *= 2
        return values

    cols = share + 2 * HALO
    for j in range(cols + 4):
        at = table.own + j
        state[j] = jnp.broadcast_to(table_ref[at : at + 1, :], (times, LANES))
    run_network(cols, True)
    begin = table_ref[table.own + HALO : table.own + HALO + cols, :][:, None, :]
    through = table_ref[table.direct + HALO : table.direct + HALO + cols, :][:, None, :]
    moved = drift(cols, 0, through)
    col = lax.broadcasted_iota(jnp.int32, moved.shape, 0) + (index * share - HALO)
    inside = (col >= 0) & (col < columns)
    state[0:cols] = begin + jnp.where(inside, running(moved) - moved, 0.0)

    run_network(share, False)
    hi, lo = split(state[HALO : HALO + share].reshape(share * times, LANES))
    through = jnp.dot(
        jnp.concatenate([hi, lo], axis=1), weight_ref[proj:direct, :], preferred_element_type=F32
    )
    through = (through[:, 0:LANES] + through[:, LANES:]).reshape(share, times, LANES)
    own = table.own + 2 * HALO
    ended = table_ref[own : own + share, :][:, None, :] + running(drift(share, HALO, through))
    for j in range(share):
        out_ref[pl.ds(j, times, stride=share), :] = ended[j]


def unpack_kernel(sizes, in_ref, out_ref):
    channels, frames, rows, _ = sizes
    image = jnp.transpose(in_ref[...])
    for f in range(frames):
        for c in range(channels):
            at = (f * channels + c) * rows
            out_ref[0, c, f] = image[at : at + rows, :]


def shards(start_frames, plan, noise, w_lift, w_time, spatial, temporal, w_point, w_out):
    times = lax.axis_size("tm")
    sizes = start_frames.shape
    channels, frames, rows, columns = sizes
    share = columns // times
    block = round_up(share + 2 * HALO, SUB)
    cols = share + 2 * HALO
    table = Table(share, sizes)
    params = limit([])
    codes = 2 * times if one_hot_fits(times, channels * rows) else 0
    mix_shape = (rows - AHEAD, frames // 2, 2 * LANES - codes, 4 * LANES)
    prep_scratch = [pltpu.VMEM(mix_shape, BF16), pltpu.VMEM(sizes, F32)]
    main_scratch = [
        pltpu.VMEM((frames, rows + 2, cols // 2, 4, times // SUB, SUB, LANES), F32),
        pltpu.VMEM((frames // 2, (cols + 2) * times, 2 * LANES), F32),
        pltpu.VMEM((2, frames, cols * times, LANES), F32),
        pltpu.VMEM((rows, cols * times, frames * LANES), BF16),
        pltpu.VMEM((cols * times, LANES), F32),
        pltpu.VMEM((cols + 4, times, LANES), F32),
        pltpu.VMEM((frames // 2, (cols + 2) * times, 2 * LANES), BF16),
        pltpu.VMEM(mix_shape, BF16),
        pltpu.VMEM((rows, frames // 2, max(codes, 16), 4 * LANES), BF16),
    ]
    index = lax.axis_index("tm").astype(jnp.int32).reshape(1)
    hbm = whole(pltpu.HBM)

    packed = pl.pallas_call(
        functools.partial(pack_kernel, times, share, block),
        out_shape=pltpu.VMEM((times, block, LANES), F32),
        in_specs=[whole(pltpu.SMEM), whole()],
        out_specs=whole(),
        scratch_shapes=[pltpu.VMEM((columns + 2 * SUB, LANES), F32)],
        compiler_params=params,
        name="pack",
    )(plan, noise)
    arrived = lax.all_to_all(packed, "tm", split_axis=0, concat_axis=0, tiled=True)

    by_tap = (
        w_lift, jnp.transpose(spatial, (2, 0, 1)), jnp.transpose(temporal, (2, 0, 1)), w_point,
        jnp.transpose(w_out),
    )
    first, mix, lines, weights = pl.pallas_call(
        functools.partial(prep_kernel, share, sizes),
        out_shape=[
            pltpu.VMEM((AHEAD,) + mix_shape[1:], BF16),
            pltpu.HBM(mix_shape, BF16),
            pltpu.VMEM((table.size, LANES), F32),
            pltpu.VMEM((weight_rows(frames)[-1], 2 * LANES), BF16),
        ],
        in_specs=[whole(pltpu.SMEM)] + [hbm] * 6,
        out_specs=[whole(), hbm, whole(), whole()],
        scratch_shapes=prep_scratch
        + [pltpu.VMEM(a.shape, a.dtype) for a in by_tap]
        + [
            pltpu.VMEM((columns + 4 * SUB + table.wide, LANES), F32),
            pltpu.SemaphoreType.DMA((7,)),
        ],
        compiler_params=limit(prep_scratch),
        cost_estimate=pl.CostEstimate(flops=10**9, bytes_accessed=10**7, transcendentals=0),
        name="prep",
    )(index, *[in_hbm(a) for a in (start_frames,) + by_tap])

    result = pl.pallas_call(
        functools.partial(main_kernel, share, sizes, times, block),
        out_shape=jax.ShapeDtypeStruct((times * share, LANES), F32),
        in_specs=[whole(pltpu.SMEM), whole(), whole(), whole(), hbm, whole(), whole()],
        out_specs=whole(),
        scratch_shapes=main_scratch + [pltpu.SemaphoreType.DMA((rows - AHEAD,))],
        compiler_params=limit(main_scratch),
        name="sampler",
    )(index, arrived.reshape(times * block, LANES), w_time, first, in_hbm(mix), lines, weights)
    back = lax.all_to_all(
        result.reshape(times, share, LANES), "tm", split_axis=0, concat_axis=0, tiled=True
    )
    return pl.pallas_call(
        functools.partial(unpack_kernel, sizes),
        out_shape=jax.ShapeDtypeStruct((1,) + sizes, F32),
        in_specs=[whole()],
        out_specs=whole(),
        compiler_params=params,
        name="unpack",
    )(back.reshape(columns, LANES))


def solution(mesh):
    in_specs = (
        P("groups", None, None, None),
        P(("groups", "tm")),
        P("tm", "groups", None, None, None),
        P(),
        P(),
        P(),
        P(),
        P(),
        P(),
    )
    out_specs = P("tm", "groups", None, None, None)
    return jax.shard_map(shards, mesh=mesh, in_specs=in_specs, out_specs=out_specs, check_vma=False)
```

```python
import functools
import math

import jax
import jax.numpy as jnp
from jax import lax
from jax.experimental import pallas as pl
from jax.experimental.pallas import tpu as pltpu
from jax.sharding import PartitionSpec as P

ITERS = 2
LANES = 128
SUB = 8
HALO = 2
NOISE_SCALE = 2.0
EPS = 1e-06
AHEAD = 3
F32 = jnp.float32
BF16 = jnp.bfloat16
VMEM_ROOM = 12 * 1024 * 1024


def in_hbm(value):
    return pltpu.with_memory_space_constraint(value, pltpu.HBM)


def limit(scratch):
    held = [s for s in scratch if hasattr(s, "shape") and jnp.issubdtype(s.dtype, jnp.number)]
    size = sum(math.prod(s.shape) * jnp.dtype(s.dtype).itemsize for s in held)
    return pltpu.CompilerParams(vmem_limit_bytes=size + VMEM_ROOM)


def round_up(value, multiple):
    return (value + multiple - 1) // multiple * multiple


def whole(memory_space=pltpu.VMEM):
    return pl.BlockSpec(memory_space=memory_space)


def columns_as_rows(image, extra):
    channels, frames, rows, columns = image.shape
    parts = [image[c, f] for f in range(frames) for c in range(channels)]
    left = LANES - channels * frames * rows
    parts.append(jnp.full((left, columns), extra, F32))
    return jnp.transpose(jnp.concatenate(parts, axis=0))


def sent_block(share, used):
    spare = LANES - used
    if share % SUB == 0 and used % spare == 0 and used // spare * 2 * HALO < share:
        return share, used // spare
    return round_up(share + 2 * HALO, SUB), 0


def pack_kernel(shares, share, plan_ref, noise_ref, out_ref, padded, moved):
    _, channels, frames, rows, columns = noise_ref.shape
    used = channels * frames * rows
    block, pieces = sent_block(share, used)
    edge = jnp.zeros((SUB, LANES), F32)
    padded[0:SUB, :] = edge
    padded[SUB + columns : 2 * SUB + columns, :] = edge
    image = columns_as_rows(noise_ref[0], plan_ref[0].astype(F32))
    padded[SUB : SUB + columns, :] = image
    for k in range(pieces):
        moved[k, 0:SUB, :] = edge
        moved[k, SUB + columns : 2 * SUB + columns, :] = edge
        moved[k, SUB : SUB + columns, :] = pltpu.roll(image, used - k * (LANES - used), 1)
    lane = lax.broadcasted_iota(jnp.int32, (2 * HALO, LANES), 1)
    for dest in range(shares):
        first = SUB - HALO + dest * share
        if pieces:
            for k in range(pieces):
                at = 2 * HALO * k
                out_ref[dest, at : at + 2 * HALO, :] = jnp.where(
                    lane < used,
                    padded[first + at : first + at + 2 * HALO, :],
                    moved[k, first + share : first + share + 2 * HALO, :],
                )
            at = 2 * HALO * pieces
            out_ref[dest, at:share, :] = padded[first + at : first + share, :]
        else:
            out_ref[dest, 0 : share + 2 * HALO, :] = padded[first : first + share + 2 * HALO, :]
            if block > share + 2 * HALO:
                out_ref[dest, share + 2 * HALO : block, :] = jnp.zeros(
                    (block - share - 2 * HALO, LANES), F32
                )


def window_of(frame, frames):
    return min(max(frame - 1, 0), frames - 3)


def one_hot_fits(times, group):
    return 9 * group + 2 * times <= 2 * LANES and (2 * LANES - 2 * times) % 16 == 0


def stack_taps(state, window, group, times):
    width = 3 * group
    before, here, after = [
        pltpu.roll(s, (LANES - window * group + k * width) % LANES, 1)
        for k, s in enumerate(state)
    ]
    lane = lax.broadcasted_iota(jnp.int32, before.shape, 1)
    first = jnp.where(lane < width, before, here)
    spill = 2 * width - LANES
    code = jnp.zeros_like(before)
    if one_hot_fits(times, group):
        when = lax.rem(lax.broadcasted_iota(jnp.int32, before.shape, 0), times)
        at = lane - (LANES - 2 * times)
        code = jnp.where((at >= 0) & (lax.rem(at + times, times) == when), 1.0, 0.0)
    second = jnp.where(
        lane < spill, here, jnp.where(lane < spill + width, after, code)
    )
    return jnp.concatenate([first.astype(BF16), second.astype(BF16)], axis=-1)


class Table:
    def __init__(self, share, sizes):
        _, frames, rows, _ = sizes
        self.wide = round_up(share + 4 * HALO, SUB)
        self.taps = 0
        self.edges = 15 * SUB
        self.own = self.edges + round_up(3 * frames * rows, SUB)
        self.direct = self.own + self.wide
        self.out = self.direct + self.wide
        self.size = self.out + LANES


def weight_rows(frames):
    proj = 2 * frames * LANES
    return proj, proj + 2 * LANES, proj + 4 * LANES, proj + 6 * LANES


def exact(a, b):
    return jnp.dot(a, b, precision=lax.Precision.HIGHEST, preferred_element_type=F32)


def split(value):
    top = value.astype(BF16)
    return top, (value - top.astype(F32)).astype(BF16)


def prep_kernel(
    share, sizes, index_ref, start_hbm, lift_hbm, spatial_hbm, temporal_hbm, point_hbm, out_hbm,
    first_ref, mix_hbm, table_ref, weight_ref,
    mix_ref, start_ref, lift_ref, spatial_ref, temporal_ref, point_ref, out_w_ref, padded, sems,
):
    channels, frames, rows, columns = sizes
    group = channels * rows
    index = index_ref[0]
    table = Table(share, sizes)
    plain = mix_ref.shape[2]
    copies = [
        pltpu.make_async_copy(source, target, sems.at[k])
        for k, (source, target) in enumerate([
            (start_hbm, start_ref), (lift_hbm, lift_ref), (spatial_hbm, spatial_ref),
            (temporal_hbm, temporal_ref), (point_hbm, point_ref), (out_hbm, out_w_ref),
        ])
    ]
    for copy in copies:
        copy.start()
    padded[...] = jnp.zeros_like(padded)
    for copy in copies:
        copy.wait()
    row = lax.broadcasted_iota(jnp.int32, (SUB, LANES), 0)

    zero = jnp.zeros((SUB, LANES), F32)
    sp = [spatial_ref[k, 0:1, :] for k in range(9)]
    tm = [temporal_ref[k, 0:1, :] for k in range(3)]
    lift = [lift_ref[c : c + 1, :] for c in range(channels)]
    timed = [[l * t for t in tm] for l in lift]
    for h in range(rows):
        by_tap = []
        for tap in range(3):
            total = zero
            for a in range(3):
                if 0 <= h + a - 1 < rows:
                    total = jnp.where(row == h + a - 1, sp[3 * a + tap], total)
            by_tap.append(total)
        made = [[[t * timed[c][k] for k in range(3)] for c in range(channels)] for t in by_tap]
        only = [jnp.where(row == h, l, 0.0) for l in lift]
        for f in range(frames):
            window = window_of(f, frames)
            mixes, ups = [], []
            for tap in range(3):
                for local in range(3):
                    k = window + local - f + 1
                    for c in range(channels):
                        mixes.append(made[tap][c][k] if 0 <= k < 3 else zero)
                        ups.append(only[c] if k == 1 and tap == 1 else zero)
            mixes += [zero] * (plain // SUB - len(mixes))
            ups += [zero] * (plain // SUB - len(ups))
            target, line = (first_ref, h) if h < AHEAD else (mix_ref, h - AHEAD)
            at = f % 2 * LANES
            target[line, f // 2, :, at : at + LANES] = jnp.concatenate(mixes, axis=0).astype(BF16)
            at += 2 * LANES
            target[line, f // 2, :, at : at + LANES] = jnp.concatenate(ups, axis=0).astype(BF16)
    leaving = pltpu.make_async_copy(mix_ref, mix_hbm, sems.at[6])
    leaving.start()

    lines = []
    for a in range(3):
        g = [spatial_ref[3 * a + c, 1:2, :] for c in range(3)]
        lines += [g[0], 0.5 * (g[0] + g[1] + g[2]), 0.5 * (g[0] - g[1] + g[2]), g[2]]
    lines += [temporal_ref[k, 1:2, :] for k in range(3)]
    for k, line in enumerate(lines):
        at = table.taps + k * SUB
        table_ref[at : at + SUB, :] = jnp.broadcast_to(line, (SUB, LANES))
    for tap in range(3):
        lines = []
        for f in range(frames):
            over = functools.reduce(
                jnp.add, [tm[k] for k in range(3) if 0 <= f + k - 1 < frames]
            )
            for h in range(rows):
                lines.append(over * functools.reduce(
                    jnp.add, [sp[3 * a + tap] for a in range(3) if 0 <= h + a - 1 < rows]
                ))
        at = table.edges + tap * frames * rows
        table_ref[at : at + frames * rows, :] = jnp.concatenate(lines, axis=0)

    left = jnp.zeros((LANES - frames * group, LANES), F32)
    spread = [jnp.broadcast_to(out_w_ref[c : c + 1, :], (rows, LANES)) for c in range(channels)]
    out_lanes = jnp.transpose(jnp.concatenate(spread * frames + [left], axis=0))
    table_ref[table.out : table.out + LANES, :] = out_lanes
    lane = lax.broadcasted_iota(jnp.int32, (LANES, LANES), 1)
    line = lax.broadcasted_iota(jnp.int32, (LANES, LANES), 0)
    first = jnp.where(lax.rem(lane, rows) == 0, out_lanes, 0.0)
    for slot, b in enumerate((1, 0)):
        folded = exact(point_ref[b].astype(F32), first)
        for f in range(frames):
            here = jnp.where((lane >= f * group) & (lane < (f + 1) * group), folded, 0.0)
            at = (slot * frames + f) * LANES
            weight_ref[at : at + LANES, 0:LANES], weight_ref[at : at + LANES, LANES:] = split(here)
    lift_rows = [jnp.broadcast_to(l, (rows, LANES)) for l in lift]
    both = exact(jnp.concatenate(lift_rows * frames + [left], axis=0), out_lanes)
    same = (lax.div(lane, group) == lax.div(line, group)) & (
        lax.rem(lane, rows) == lax.rem(line, rows)
    )
    both = jnp.where(same, both, 0.0)
    proj, direct, mixing, _ = weight_rows(frames)
    hi, lo = split(both)
    nothing = jnp.zeros((LANES, LANES), BF16)
    weight_ref[proj : proj + LANES, 0:LANES] = hi
    weight_ref[proj : proj + LANES, LANES:] = lo
    weight_ref[proj + LANES : direct, 0:LANES] = hi
    weight_ref[proj + LANES : direct, LANES:] = nothing
    for at, value in ((direct, point_ref[0]), (mixing, jnp.full((LANES, LANES), 4.0 / LANES, BF16))):
        weight_ref[at : at + LANES, 0:LANES] = value
        weight_ref[at + LANES : at + 2 * LANES, LANES:] = value
        weight_ref[at : at + LANES, LANES:] = nothing
        weight_ref[at + LANES : at + 2 * LANES, 0:LANES] = nothing

    lead = 2 * HALO + SUB
    padded[lead : lead + columns, :] = columns_as_rows(start_ref[...], 0.0)
    own = padded[pl.ds(SUB + index * share, table.wide), :]
    table_ref[table.own : table.own + table.wide, :] = own
    table_ref[table.direct : table.direct + table.wide, :] = exact(own, both)
    leaving.wait()


def main_kernel(
    share, sizes, times, index_ref, noise_ref, time_ref, first_ref, mix_hbm, table_ref, weight_ref,
    out_ref, feats, fresh, mixed_buf, normed_buf, acc, state, left_buf, mix_ref, hot_ref, sems,
):
    channels, frames, rows, columns = sizes
    group = channels * rows
    index = index_ref[0]
    step = 1.0 / times
    table = Table(share, sizes)
    halves = times // SUB
    proj, direct, mixing, mean_end = weight_rows(frames)
    hot = one_hot_fits(times, group)
    used = frames * group
    block, pieces = sent_block(share, used)

    def arrival(k):
        return pltpu.make_async_copy(mix_hbm.at[k], mix_ref.at[k], sems.at[k])

    for k in range(rows - AHEAD):
        arrival(k).start()
    for h in (0, rows + 1):
        feats[:, h] = jnp.zeros(feats.shape[:1] + feats.shape[2:], F32)

    half = LANES // 2
    line = share - 1 if pieces else HALO
    planned = noise_ref[pl.ds(line, times, stride=block), :][:, LANES - 1 : LANES]
    lane = lax.broadcasted_iota(jnp.int32, (1, LANES), 1)
    place = jnp.where(lane < half, lane, lane - half).astype(F32)
    angles = planned * jnp.exp(place * (-math.log(1000.0) / half))
    embedded = jnp.where(lane < half, jnp.sin(angles), jnp.cos(angles))
    bias = exact(embedded, time_ref[...])
    bias_out = exact(bias, table_ref[table.out : table.out + LANES, :])

    def mean_square(pair):
        return jnp.dot(
            (pair * pair).astype(BF16), weight_ref[mixing:mean_end, :], preferred_element_type=F32
        )

    def normalise(pair, mean):
        value = pair * lax.rsqrt(mean + 4.0 * EPS)
        return (value + value * jnp.tanh(value)).astype(BF16)

    def in_pairs(values):
        return jnp.concatenate(
            [jnp.concatenate(values[f : f + 2], axis=1) for f in range(0, frames, 2)], axis=0
        )

    def by_frame(pairs, cells):
        return jnp.concatenate(
            [pairs[k * cells : (k + 1) * cells] for k in range(frames // 2)], axis=1
        )

    def bias_taps(h):
        return [
            jnp.concatenate(
                [
                    bias * table_ref[pl.ds(table.edges + (k * frames + f) * rows + h, 1), :]
                    for f in range(frames)
                ],
                axis=1,
            )
            for k in range(3)
        ]

    def receive(h):
        if not isinstance(h, int):
            arrival(h - AHEAD).wait()
        elif h >= AHEAD:
            arrival(h - AHEAD).wait()
        if hot:
            by_tap = bias_taps(h)
            every = by_tap[0] + by_tap[1] + by_tap[2]
            for p in range(frames // 2):
                here = every[:, 2 * p * LANES : 2 * (p + 1) * LANES]
                terms = jnp.concatenate([here, bias, bias], axis=1)
                hot_ref[h, p, 0:times, :], hot_ref[h, p, times:, :] = split(terms)

    def lift_weights(h, p, lanes):
        if isinstance(h, int) and h < AHEAD:
            taken = first_ref[h, p, :, lanes]
        else:
            taken = mix_ref[h - AHEAD, p, :, lanes]
        return jnp.concatenate([taken, hot_ref[h, p, :, lanes]], axis=0) if hot else taken

    def run_network(cols, first_time):
        wide = cols + 2
        cells = cols * times
        many = wide * times
        margin = (wide - share) // 2
        flags = {}
        for j in list(range(margin)) + list(range(wide - margin, wide)):
            col = index * share + j - margin
            flags[j] = jnp.where((col >= 0) & (col < columns), 1.0, 0.0).astype(F32)
        at_left = jnp.where(index == 0, 1.0, 0.0).astype(F32)
        at_right = jnp.where((index + 1) * share == columns, 1.0, 0.0).astype(F32)
        taps = [table_ref[table.taps + k * SUB : table.taps + (k + 1) * SUB, :] for k in range(15)]
        around = [state[k : k + wide].reshape(many, LANES) for k in range(3)]
        for p in range(frames // 2):
            left_buf[p, 0:many, :] = stack_taps(around, p, group, times)

        def block_one(h):
            linear = [
                jnp.dot(
                    left_buf[p, 0:many, :], lift_weights(h, p, slice(0, 2 * LANES)),
                    preferred_element_type=F32,
                )
                for p in range(frames // 2)
            ]
            yield
            by_tap = bias_taps(h)
            parts = []
            for p in range(frames // 2):
                lanes = slice(2 * p * LANES, 2 * (p + 1) * LANES)
                mixed = linear[p]
                if not hot:
                    every = by_tap[0] + by_tap[1] + by_tap[2]
                    mixed = mixed + jnp.concatenate([every[:, lanes]] * wide, axis=0)
                one, two = margin * times, (wide - margin - 1) * times
                if one == two:
                    edge = by_tap[0][:, lanes] * at_left + by_tap[2][:, lanes] * at_right
                    middle = [mixed[one : one + times] - edge]
                else:
                    middle = [
                        mixed[one : one + times] - by_tap[0][:, lanes] * at_left,
                        mixed[one + times : two],
                        mixed[two : two + times] - by_tap[2][:, lanes] * at_right,
                    ]
                parts += [mixed[:one]] + middle + [mixed[two + times :]]
            pair = jnp.concatenate([x for x in parts if x.shape[0]], axis=0)
            mean = mean_square(pair)
            yield
            normed = normalise(pair, mean)
            normed_buf[h, 0:cells, :] = by_frame(normed, many)[times : times + cells]
            updates = []
            for p in range(frames // 2):
                both = jnp.concatenate([normed[p * many : (p + 1) * many], left_buf[p, 0:many, :]], axis=1)
                onto = jnp.concatenate(
                    [weight_ref[direct:mixing, :], lift_weights(h, p, slice(2 * LANES, 4 * LANES))], axis=0
                )
                updates.append(jnp.dot(both, onto, preferred_element_type=F32))
            yield
            for p in range(frames // 2):
                fresh[p, 0:many, :] = updates[p]
            yield

        def settle(lines, line):
            for f in range(frames):
                lanes = slice(f % 2 * LANES, (f % 2 + 1) * LANES)
                new = []
                for j in range(wide):
                    value = fresh[f // 2, j * times : (j + 1) * times, lanes]
                    if not hot:
                        value = value + bias
                    value = value.reshape(halves, SUB, LANES)
                    new.append(value * flags[j] if j in flags else value)
                for q in range(cols // 2):
                    d = new[2 * q : 2 * q + 4]
                    lines[f, line, q, 0] = d[0] - d[2]
                    lines[f, line, q, 1] = d[1] + d[2]
                    lines[f, line, q, 2] = d[2] - d[1]
                    lines[f, line, q, 3] = d[1] - d[3]

        def convolve(h, lines, begin, end):
            for q in range(begin, end):
                spread = []
                for f in range(frames):
                    m = []
                    for i in range(4):
                        terms = [lines[f, a, q, i] * taps[4 * a + i] for a in range(3)]
                        m.append(terms[0] + terms[1] + terms[2])
                    spread.append((m[0] + m[1] + m[2], m[1] - m[2] - m[3]))
                for f in range(frames):
                    for side in range(2):
                        total = None
                        for k in range(3):
                            if 0 <= f + k - 1 < frames:
                                term = spread[f + k - 1][side] * taps[12 + k]
                                total = term if total is None else total + term
                        at = (2 * q + side) * times
                        mixed_buf[lax.rem(h, 2), f, at : at + times, :] = total.reshape(times, LANES)

        def finish(h, slot):
            pair = in_pairs([mixed_buf[slot, f, 0:cells, :] for f in range(frames)])
            mean = mean_square(pair)
            yield
            normed = by_frame(normalise(pair, mean), cells)
            left = jnp.concatenate([normed, normed_buf[h, 0:cells, :]], axis=1)
            out = jnp.dot(left, weight_ref[0:proj, :], preferred_element_type=F32)
            yield
            out = out[:, 0:LANES] + out[:, LANES:]
            acc[0:cells, :] += pltpu.roll(out, h, 1)
            yield

        acc[0:cells, :] = jnp.zeros((cells, LANES), F32)
        pairs = cols // 2

        def receive_next(h):
            if first_time and isinstance(h, int):
                receive(h)
            elif first_time:

                @pl.when(h < rows)
                def _():
                    receive(h)

        def steady(h, carry):
            lines = feats.at[:, pl.ds(h, 3)]
            ending, starting = finish(h - 1, lax.rem(h + 1, 2)), block_one(h + 2)
            settle(lines, 2)
            next(starting)
            next(ending)
            next(starting)
            convolve(h, lines, 0, pairs)
            next(ending)
            next(starting)
            next(ending)
            next(starting)
            receive_next(h + 3)
            return carry

        if first_time:
            receive(0)
            receive(1)
        ahead = block_one(0)
        for _ in ahead:
            pass
        settle(feats, 1)
        for _ in block_one(1):
            pass
        receive_next(2)
        settle(feats, 2)
        starting = block_one(2)
        next(starting)
        convolve(0, feats, 0, pairs)
        for _ in starting:
            pass
        receive_next(3)
        lax.fori_loop(1, rows - 2, steady, 0)
        lines = feats.at[:, pl.ds(rows - 2, 3)]
        settle(lines, 2)
        ending = finish(rows - 3, (rows - 3) % 2)
        next(ending)
        convolve(rows - 2, lines, 0, pairs)
        for _ in ending:
            pass
        ending = finish(rows - 2, (rows - 2) % 2)
        next(ending)
        convolve(rows - 1, feats.at[:, pl.ds(rows - 1, 3)], 0, pairs)
        for _ in ending:
            pass
        for _ in finish(rows - 1, (rows - 1) % 2):
            pass

    def arrived(j):
        if not pieces or j < share:
            return noise_ref[pl.ds(j, times, stride=block), :]
        spare = LANES - used
        lane = lax.broadcasted_iota(jnp.int32, (times, LANES), 1)
        total = jnp.zeros((times, LANES), F32)
        for k in range(pieces):
            piece = noise_ref[pl.ds(2 * HALO * k + j - share, times, stride=block), :]
            piece = pltpu.roll(piece, (k * spare + LANES - used) % LANES, 1)
            total = jnp.where((lane >= k * spare) & (lane < (k + 1) * spare), piece, total)
        return total

    def drift(cols, skip, through):
        f = acc[0 : cols * times, :].reshape(cols, times, LANES) + through + bias_out[None]
        noise = jnp.stack([arrived(skip + j) for j in range(cols)])
        return step * f + (NOISE_SCALE * math.sqrt(step)) * noise

    def running(values):
        when = lax.broadcasted_iota(jnp.int32, values.shape, 1)
        reach = 1
        while reach < times:
            values = values + jnp.where(when >= reach, pltpu.roll(values, reach, 1), 0.0)
            reach *= 2
        return values

    cols = share + 2 * HALO
    for j in range(cols + 4):
        at = table.own + j
        state[j] = jnp.broadcast_to(table_ref[at : at + 1, :], (times, LANES))
    run_network(cols, True)
    begin = table_ref[table.own + HALO : table.own + HALO + cols, :][:, None, :]
    through = table_ref[table.direct + HALO : table.direct + HALO + cols, :][:, None, :]
    moved = drift(cols, 0, through)
    col = lax.broadcasted_iota(jnp.int32, moved.shape, 0) + (index * share - HALO)
    inside = (col >= 0) & (col < columns)
    state[0:cols] = begin + jnp.where(inside, running(moved) - moved, 0.0)

    run_network(share, False)
    hi, lo = split(state[HALO : HALO + share].reshape(share * times, LANES))
    through = jnp.dot(
        jnp.concatenate([hi, lo], axis=1), weight_ref[proj:direct, :], preferred_element_type=F32
    )
    through = (through[:, 0:LANES] + through[:, LANES:]).reshape(share, times, LANES)
    own = table.own + 2 * HALO
    ended = table_ref[own : own + share, :][:, None, :] + running(drift(share, HALO, through))
    for j in range(share):
        out_ref[pl.ds(j, times, stride=share), :] = ended[j]


def unpack_kernel(sizes, in_ref, out_ref):
    channels, frames, rows, _ = sizes
    image = jnp.transpose(in_ref[...])
    for f in range(frames):
        for c in range(channels):
            at = (f * channels + c) * rows
            out_ref[0, c, f] = image[at : at + rows, :]


def shards(start_frames, plan, noise, w_lift, w_time, spatial, temporal, w_point, w_out):
    times = lax.axis_size("tm")
    sizes = start_frames.shape
    channels, frames, rows, columns = sizes
    share = columns // times
    block, pieces = sent_block(share, channels * frames * rows)
    cols = share + 2 * HALO
    table = Table(share, sizes)
    params = limit([])
    codes = 2 * times if one_hot_fits(times, channels * rows) else 0
    mix_shape = (rows - AHEAD, frames // 2, 2 * LANES - codes, 4 * LANES)
    prep_scratch = [pltpu.VMEM(mix_shape, BF16), pltpu.VMEM(sizes, F32)]
    main_scratch = [
        pltpu.VMEM((frames, rows + 2, cols // 2, 4, times // SUB, SUB, LANES), F32),
        pltpu.VMEM((frames // 2, (cols + 2) * times, 2 * LANES), F32),
        pltpu.VMEM((2, frames, cols * times, LANES), F32),
        pltpu.VMEM((rows, cols * times, frames * LANES), BF16),
        pltpu.VMEM((cols * times, LANES), F32),
        pltpu.VMEM((cols + 4, times, LANES), F32),
        pltpu.VMEM((frames // 2, (cols + 2) * times, 2 * LANES), BF16),
        pltpu.VMEM(mix_shape, BF16),
        pltpu.VMEM((rows, frames // 2, max(codes, 16), 4 * LANES), BF16),
    ]
    index = lax.axis_index("tm").astype(jnp.int32).reshape(1)
    hbm = whole(pltpu.HBM)

    packed = pl.pallas_call(
        functools.partial(pack_kernel, times, share),
        out_shape=pltpu.VMEM((times, block, LANES), F32),
        in_specs=[whole(pltpu.SMEM), whole()],
        out_specs=whole(),
        scratch_shapes=[
            pltpu.VMEM((columns + 2 * SUB, LANES), F32),
            pltpu.VMEM((max(pieces, 1), columns + 2 * SUB, LANES), F32),
        ],
        compiler_params=params,
        name="pack",
    )(plan, noise)
    arrived = lax.all_to_all(packed, "tm", split_axis=0, concat_axis=0, tiled=True)

    by_tap = (
        w_lift, jnp.transpose(spatial, (2, 0, 1)), jnp.transpose(temporal, (2, 0, 1)), w_point,
        jnp.transpose(w_out),
    )
    first, mix, lines, weights = pl.pallas_call(
        functools.partial(prep_kernel, share, sizes),
        out_shape=[
            pltpu.VMEM((AHEAD,) + mix_shape[1:], BF16),
            pltpu.HBM(mix_shape, BF16),
            pltpu.VMEM((table.size, LANES), F32),
            pltpu.VMEM((weight_rows(frames)[-1], 2 * LANES), BF16),
        ],
        in_specs=[whole(pltpu.SMEM)] + [hbm] * 6,
        out_specs=[whole(), hbm, whole(), whole()],
        scratch_shapes=prep_scratch
        + [pltpu.VMEM(a.shape, a.dtype) for a in by_tap]
        + [
            pltpu.VMEM((columns + 4 * SUB + table.wide, LANES), F32),
            pltpu.SemaphoreType.DMA((7,)),
        ],
        compiler_params=limit(prep_scratch),
        cost_estimate=pl.CostEstimate(flops=10**9, bytes_accessed=10**7, transcendentals=0),
        name="prep",
    )(index, *[in_hbm(a) for a in (start_frames,) + by_tap])

    result = pl.pallas_call(
        functools.partial(main_kernel, share, sizes, times),
        out_shape=jax.ShapeDtypeStruct((times * share, LANES), F32),
        in_specs=[whole(pltpu.SMEM), whole(), whole(), whole(), hbm, whole(), whole()],
        out_specs=whole(),
        scratch_shapes=main_scratch + [pltpu.SemaphoreType.DMA((rows - AHEAD,))],
        compiler_params=limit(main_scratch),
        name="sampler",
    )(index, arrived.reshape(times * block, LANES), w_time, first, in_hbm(mix), lines, weights)
    back = lax.all_to_all(
        result.reshape(times, share, LANES), "tm", split_axis=0, concat_axis=0, tiled=True
    )
    return pl.pallas_call(
        functools.partial(unpack_kernel, sizes),
        out_shape=jax.ShapeDtypeStruct((1,) + sizes, F32),
        in_specs=[whole()],
        out_specs=whole(),
        compiler_params=params,
        name="unpack",
    )(back.reshape(columns, LANES))


def solution(mesh):
    in_specs = (
        P("groups", None, None, None),
        P(("groups", "tm")),
        P("tm", "groups", None, None, None),
        P(),
        P(),
        P(),
        P(),
        P(),
        P(),
    )
    out_specs = P("tm", "groups", None, None, None)
    return jax.shard_map(shards, mesh=mesh, in_specs=in_specs, out_specs=out_specs, check_vma=False)
```

```python
import functools
import math

import jax
import jax.numpy as jnp
from jax import lax
from jax.experimental import pallas as pl
from jax.experimental.pallas import tpu as pltpu
from jax.sharding import PartitionSpec as P

ITERS = 2
LANES = 128
SUB = 8
HALO = 2
NOISE_SCALE = 2.0
EPS = 1e-06
AHEAD = 3
F32 = jnp.float32
BF16 = jnp.bfloat16
VMEM_ROOM = 12 * 1024 * 1024


def in_hbm(value):
    return pltpu.with_memory_space_constraint(value, pltpu.HBM)


def limit(scratch):
    held = [s for s in scratch if hasattr(s, "shape") and jnp.issubdtype(s.dtype, jnp.number)]
    size = sum(math.prod(s.shape) * jnp.dtype(s.dtype).itemsize for s in held)
    return pltpu.CompilerParams(vmem_limit_bytes=size + VMEM_ROOM)


def round_up(value, multiple):
    return (value + multiple - 1) // multiple * multiple


def whole(memory_space=pltpu.VMEM):
    return pl.BlockSpec(memory_space=memory_space)


def columns_as_rows(image, extra):
    channels, frames, rows, columns = image.shape
    parts = [image[c, f] for f in range(frames) for c in range(channels)]
    left = LANES - channels * frames * rows
    parts.append(jnp.full((left, columns), extra, F32))
    return jnp.transpose(jnp.concatenate(parts, axis=0))


def sent_block(share, used):
    spare = LANES - used
    if share % SUB == 0 and used % spare == 0 and used // spare * 2 * HALO < share:
        return share, used // spare
    return round_up(share + 2 * HALO, SUB), 0


def returned_block(share, used):
    pieces = sent_block(share, used)[1]
    if pieces and pieces * 2 * HALO == share - 2 * HALO:
        return (pieces, 2 * HALO, LANES), pieces
    return (share, LANES), 0


def pack_kernel(shares, share, plan_ref, noise_ref, out_ref, padded, moved):
    _, channels, frames, rows, columns = noise_ref.shape
    used = channels * frames * rows
    block, pieces = sent_block(share, used)
    edge = jnp.zeros((SUB, LANES), F32)
    padded[0:SUB, :] = edge
    padded[SUB + columns : 2 * SUB + columns, :] = edge
    image = columns_as_rows(noise_ref[0], plan_ref[0].astype(F32))
    padded[SUB : SUB + columns, :] = image
    for k in range(pieces):
        moved[k, 0:SUB, :] = edge
        moved[k, SUB + columns : 2 * SUB + columns, :] = edge
        moved[k, SUB : SUB + columns, :] = pltpu.roll(image, used - k * (LANES - used), 1)
    lane = lax.broadcasted_iota(jnp.int32, (2 * HALO, LANES), 1)
    for dest in range(shares):
        first = SUB - HALO + dest * share
        if pieces:
            for k in range(pieces):
                at = 2 * HALO * k
                out_ref[dest, at : at + 2 * HALO, :] = jnp.where(
                    lane < used,
                    padded[first + at : first + at + 2 * HALO, :],
                    moved[k, first + share : first + share + 2 * HALO, :],
                )
            at = 2 * HALO * pieces
            out_ref[dest, at:share, :] = padded[first + at : first + share, :]
        else:
            out_ref[dest, 0 : share + 2 * HALO, :] = padded[first : first + share + 2 * HALO, :]
            if block > share + 2 * HALO:
                out_ref[dest, share + 2 * HALO : block, :] = jnp.zeros(
                    (block - share - 2 * HALO, LANES), F32
                )


def window_of(frame, frames):
    return min(max(frame - 1, 0), frames - 3)


def one_hot_fits(times, group):
    return 9 * group + 2 * times <= 2 * LANES and (2 * LANES - 2 * times) % 16 == 0


def stack_taps(state, window, group, times):
    width = 3 * group
    before, here, after = [
        pltpu.roll(s, (LANES - window * group + k * width) % LANES, 1)
        for k, s in enumerate(state)
    ]
    lane = lax.broadcasted_iota(jnp.int32, before.shape, 1)
    first = jnp.where(lane < width, before, here)
    spill = 2 * width - LANES
    code = jnp.zeros_like(before)
    if one_hot_fits(times, group):
        when = lax.rem(lax.broadcasted_iota(jnp.int32, before.shape, 0), times)
        at = lane - (LANES - 2 * times)
        code = jnp.where((at >= 0) & (lax.rem(at + times, times) == when), 1.0, 0.0)
    second = jnp.where(
        lane < spill, here, jnp.where(lane < spill + width, after, code)
    )
    return jnp.concatenate([first.astype(BF16), second.astype(BF16)], axis=-1)


class Table:
    def __init__(self, share, sizes):
        _, frames, rows, _ = sizes
        self.wide = round_up(share + 4 * HALO, SUB)
        self.taps = 0
        self.edges = 15 * SUB
        self.own = self.edges + round_up(3 * frames * rows, SUB)
        self.direct = self.own + self.wide
        self.out = self.direct + self.wide
        self.size = self.out + LANES


def weight_rows(frames):
    proj = 2 * frames * LANES
    return proj, proj + 2 * LANES, proj + 4 * LANES, proj + 6 * LANES


def exact(a, b):
    return jnp.dot(a, b, precision=lax.Precision.HIGHEST, preferred_element_type=F32)


def split(value):
    top = value.astype(BF16)
    return top, (value - top.astype(F32)).astype(BF16)


def prep_kernel(
    share, sizes, index_ref, start_hbm, lift_hbm, spatial_hbm, temporal_hbm, point_hbm, out_hbm,
    first_ref, mix_hbm, table_ref, weight_ref,
    mix_ref, start_ref, lift_ref, spatial_ref, temporal_ref, point_ref, out_w_ref, padded, sems,
):
    channels, frames, rows, columns = sizes
    group = channels * rows
    index = index_ref[0]
    table = Table(share, sizes)
    plain = mix_ref.shape[2]
    copies = [
        pltpu.make_async_copy(source, target, sems.at[k])
        for k, (source, target) in enumerate([
            (start_hbm, start_ref), (lift_hbm, lift_ref), (spatial_hbm, spatial_ref),
            (temporal_hbm, temporal_ref), (point_hbm, point_ref), (out_hbm, out_w_ref),
        ])
    ]
    for copy in copies:
        copy.start()
    padded[...] = jnp.zeros_like(padded)
    for copy in copies:
        copy.wait()
    row = lax.broadcasted_iota(jnp.int32, (SUB, LANES), 0)

    zero = jnp.zeros((SUB, LANES), F32)
    sp = [spatial_ref[k, 0:1, :] for k in range(9)]
    tm = [temporal_ref[k, 0:1, :] for k in range(3)]
    lift = [lift_ref[c : c + 1, :] for c in range(channels)]
    timed = [[l * t for t in tm] for l in lift]
    for h in range(rows):
        by_tap = []
        for tap in range(3):
            total = zero
            for a in range(3):
                if 0 <= h + a - 1 < rows:
                    total = jnp.where(row == h + a - 1, sp[3 * a + tap], total)
            by_tap.append(total)
        made = [[[t * timed[c][k] for k in range(3)] for c in range(channels)] for t in by_tap]
        only = [jnp.where(row == h, l, 0.0) for l in lift]
        for f in range(frames):
            window = window_of(f, frames)
            mixes, ups = [], []
            for tap in range(3):
                for local in range(3):
                    k = window + local - f + 1
                    for c in range(channels):
                        mixes.append(made[tap][c][k] if 0 <= k < 3 else zero)
                        ups.append(only[c] if k == 1 and tap == 1 else zero)
            mixes += [zero] * (plain // SUB - len(mixes))
            ups += [zero] * (plain // SUB - len(ups))
            target, line = (first_ref, h) if h < AHEAD else (mix_ref, h - AHEAD)
            at = f % 2 * LANES
            target[line, f // 2, :, at : at + LANES] = jnp.concatenate(mixes, axis=0).astype(BF16)
            at += 2 * LANES
            target[line, f // 2, :, at : at + LANES] = jnp.concatenate(ups, axis=0).astype(BF16)
    leaving = pltpu.make_async_copy(mix_ref, mix_hbm, sems.at[6])
    leaving.start()

    lines = []
    for a in range(3):
        g = [spatial_ref[3 * a + c, 1:2, :] for c in range(3)]
        lines += [g[0], 0.5 * (g[0] + g[1] + g[2]), 0.5 * (g[0] - g[1] + g[2]), g[2]]
    lines += [temporal_ref[k, 1:2, :] for k in range(3)]
    for k, line in enumerate(lines):
        at = table.taps + k * SUB
        table_ref[at : at + SUB, :] = jnp.broadcast_to(line, (SUB, LANES))
    for tap in range(3):
        lines = []
        for f in range(frames):
            over = functools.reduce(
                jnp.add, [tm[k] for k in range(3) if 0 <= f + k - 1 < frames]
            )
            for h in range(rows):
                lines.append(over * functools.reduce(
                    jnp.add, [sp[3 * a + tap] for a in range(3) if 0 <= h + a - 1 < rows]
                ))
        at = table.edges + tap * frames * rows
        table_ref[at : at + frames * rows, :] = jnp.concatenate(lines, axis=0)

    left = jnp.zeros((LANES - frames * group, LANES), F32)
    spread = [jnp.broadcast_to(out_w_ref[c : c + 1, :], (rows, LANES)) for c in range(channels)]
    out_lanes = jnp.transpose(jnp.concatenate(spread * frames + [left], axis=0))
    table_ref[table.out : table.out + LANES, :] = out_lanes
    lane = lax.broadcasted_iota(jnp.int32, (LANES, LANES), 1)
    line = lax.broadcasted_iota(jnp.int32, (LANES, LANES), 0)
    first = jnp.where(lax.rem(lane, rows) == 0, out_lanes, 0.0)
    for slot, b in enumerate((1, 0)):
        folded = exact(point_ref[b].astype(F32), first)
        for f in range(frames):
            here = jnp.where((lane >= f * group) & (lane < (f + 1) * group), folded, 0.0)
            at = (slot * frames + f) * LANES
            weight_ref[at : at + LANES, 0:LANES], weight_ref[at : at + LANES, LANES:] = split(here)
    lift_rows = [jnp.broadcast_to(l, (rows, LANES)) for l in lift]
    both = exact(jnp.concatenate(lift_rows * frames + [left], axis=0), out_lanes)
    same = (lax.div(lane, group) == lax.div(line, group)) & (
        lax.rem(lane, rows) == lax.rem(line, rows)
    )
    both = jnp.where(same, both, 0.0)
    proj, direct, mixing, _ = weight_rows(frames)
    hi, lo = split(both)
    nothing = jnp.zeros((LANES, LANES), BF16)
    weight_ref[proj : proj + LANES, 0:LANES] = hi
    weight_ref[proj : proj + LANES, LANES:] = lo
    weight_ref[proj + LANES : direct, 0:LANES] = hi
    weight_ref[proj + LANES : direct, LANES:] = nothing
    for at, value in ((direct, point_ref[0]), (mixing, jnp.full((LANES, LANES), 4.0 / LANES, BF16))):
        weight_ref[at : at + LANES, 0:LANES] = value
        weight_ref[at + LANES : at + 2 * LANES, LANES:] = value
        weight_ref[at : at + LANES, LANES:] = nothing
        weight_ref[at + LANES : at + 2 * LANES, 0:LANES] = nothing

    lead = 2 * HALO + SUB
    padded[lead : lead + columns, :] = columns_as_rows(start_ref[...], 0.0)
    own = padded[pl.ds(SUB + index * share, table.wide), :]
    table_ref[table.own : table.own + table.wide, :] = own
    table_ref[table.direct : table.direct + table.wide, :] = exact(own, both)
    leaving.wait()


def main_kernel(
    share, sizes, times, index_ref, noise_ref, time_ref, first_ref, mix_hbm, table_ref, weight_ref,
    out_ref, feats, fresh, mixed_buf, normed_buf, acc, state, left_buf, mix_ref, hot_ref, leaving, sems,
):
    channels, frames, rows, columns = sizes
    group = channels * rows
    index = index_ref[0]
    step = 1.0 / times
    table = Table(share, sizes)
    halves = times // SUB
    proj, direct, mixing, mean_end = weight_rows(frames)
    hot = one_hot_fits(times, group)
    used = frames * group
    block, pieces = sent_block(share, used)

    def arrival(k):
        return pltpu.make_async_copy(mix_hbm.at[k], mix_ref.at[k], sems.at[k])

    for k in range(rows - AHEAD):
        arrival(k).start()

    half = LANES // 2
    line = share - 1 if pieces else HALO
    planned = noise_ref[pl.ds(line, times, stride=block), :][:, LANES - 1 : LANES]
    lane = lax.broadcasted_iota(jnp.int32, (1, LANES), 1)
    place = jnp.where(lane < half, lane, lane - half).astype(F32)
    angles = planned * jnp.exp(place * (-math.log(1000.0) / half))
    embedded = jnp.where(lane < half, jnp.sin(angles), jnp.cos(angles))
    bias = exact(embedded, time_ref[...])
    bias_out = exact(bias, table_ref[table.out : table.out + LANES, :])

    def mean_square(pair):
        return jnp.dot(
            (pair * pair).astype(BF16), weight_ref[mixing:mean_end, :], preferred_element_type=F32
        )

    def normalise(pair, mean):
        value = pair * lax.rsqrt(mean + 4.0 * EPS)
        return (value + value * jnp.tanh(value)).astype(BF16)

    def in_pairs(values):
        return jnp.concatenate(
            [jnp.concatenate(values[f : f + 2], axis=1) for f in range(0, frames, 2)], axis=0
        )

    def by_frame(pairs, cells):
        return jnp.concatenate(
            [pairs[k * cells : (k + 1) * cells] for k in range(frames // 2)], axis=1
        )

    def bias_taps(h):
        return [
            jnp.concatenate(
                [
                    bias * table_ref[pl.ds(table.edges + (k * frames + f) * rows + h, 1), :]
                    for f in range(frames)
                ],
                axis=1,
            )
            for k in range(3)
        ]

    def receive(h):
        if not isinstance(h, int):
            arrival(h - AHEAD).wait()
        elif h >= AHEAD:
            arrival(h - AHEAD).wait()
        if hot:
            by_tap = bias_taps(h)
            every = by_tap[0] + by_tap[1] + by_tap[2]
            for p in range(frames // 2):
                here = every[:, 2 * p * LANES : 2 * (p + 1) * LANES]
                terms = jnp.concatenate([here, bias, bias], axis=1)
                hot_ref[h, p, 0:times, :], hot_ref[h, p, times:, :] = split(terms)

    def lift_weights(h, p, lanes):
        if isinstance(h, int) and h < AHEAD:
            taken = first_ref[h, p, :, lanes]
        else:
            taken = mix_ref[h - AHEAD, p, :, lanes]
        return jnp.concatenate([taken, hot_ref[h, p, :, lanes]], axis=0) if hot else taken

    def run_network(cols, first_time):
        wide = cols + 2
        cells = cols * times
        many = wide * times
        margin = (wide - share) // 2
        flags = {}
        for j in list(range(margin)) + list(range(wide - margin, wide)):
            col = index * share + j - margin
            flags[j] = jnp.where((col >= 0) & (col < columns), 1.0, 0.0).astype(F32)
        at_left = jnp.where(index == 0, 1.0, 0.0).astype(F32)
        at_right = jnp.where((index + 1) * share == columns, 1.0, 0.0).astype(F32)
        taps = [table_ref[table.taps + k * SUB : table.taps + (k + 1) * SUB, :] for k in range(15)]
        around = [state[k : k + wide].reshape(many, LANES) for k in range(3)]
        for p in range(frames // 2):
            left_buf[p, 0:many, :] = stack_taps(around, p, group, times)

        def block_one(h):
            linear = [
                jnp.dot(
                    left_buf[p, 0:many, :], lift_weights(h, p, slice(0, 2 * LANES)),
                    preferred_element_type=F32,
                )
                for p in range(frames // 2)
            ]
            yield
            by_tap = bias_taps(h)
            parts = []
            for p in range(frames // 2):
                lanes = slice(2 * p * LANES, 2 * (p + 1) * LANES)
                mixed = linear[p]
                if not hot:
                    every = by_tap[0] + by_tap[1] + by_tap[2]
                    mixed = mixed + jnp.concatenate([every[:, lanes]] * wide, axis=0)
                one, two = margin * times, (wide - margin - 1) * times
                if one == two:
                    edge = by_tap[0][:, lanes] * at_left + by_tap[2][:, lanes] * at_right
                    middle = [mixed[one : one + times] - edge]
                else:
                    middle = [
                        mixed[one : one + times] - by_tap[0][:, lanes] * at_left,
                        mixed[one + times : two],
                        mixed[two : two + times] - by_tap[2][:, lanes] * at_right,
                    ]
                parts += [mixed[:one]] + middle + [mixed[two + times :]]
            pair = jnp.concatenate([x for x in parts if x.shape[0]], axis=0)
            mean = mean_square(pair)
            yield
            normed = normalise(pair, mean)
            normed_buf[h, 0:cells, :] = by_frame(normed, many)[times : times + cells]
            updates = []
            for p in range(frames // 2):
                both = jnp.concatenate([normed[p * many : (p + 1) * many], left_buf[p, 0:many, :]], axis=1)
                onto = jnp.concatenate(
                    [weight_ref[direct:mixing, :], lift_weights(h, p, slice(2 * LANES, 4 * LANES))], axis=0
                )
                updates.append(jnp.dot(both, onto, preferred_element_type=F32))
            yield
            for p in range(frames // 2):
                fresh[p, 0:many, :] = updates[p]
            yield

        def settle(lines, line):
            for f in range(frames):
                lanes = slice(f % 2 * LANES, (f % 2 + 1) * LANES)
                new = []
                for j in range(wide):
                    value = fresh[f // 2, j * times : (j + 1) * times, lanes]
                    if not hot:
                        value = value + bias
                    value = value.reshape(halves, SUB, LANES)
                    new.append(value * flags[j] if j in flags else value)
                for q in range(cols // 2):
                    d = new[2 * q : 2 * q + 4]
                    lines[f, line, q, 0] = d[0] - d[2]
                    lines[f, line, q, 1] = d[1] + d[2]
                    lines[f, line, q, 2] = d[2] - d[1]
                    lines[f, line, q, 3] = d[1] - d[3]

        def convolve(h, lines, begin, end):
            inside = range(3)
            if isinstance(h, int):
                inside = [a for a in range(3) if 0 <= h + a - 1 < rows]
            for q in range(begin, end):
                spread = []
                for f in range(frames):
                    m = []
                    for i in range(4):
                        terms = [lines[f, a, q, i] * taps[4 * a + i] for a in inside]
                        m.append(functools.reduce(jnp.add, terms))
                    spread.append((m[0] + m[1] + m[2], m[1] - m[2] - m[3]))
                for f in range(frames):
                    for side in range(2):
                        total = None
                        for k in range(3):
                            if 0 <= f + k - 1 < frames:
                                term = spread[f + k - 1][side] * taps[12 + k]
                                total = term if total is None else total + term
                        at = (2 * q + side) * times
                        mixed_buf[lax.rem(h, 2), f, at : at + times, :] = total.reshape(times, LANES)

        def finish(h, slot):
            pair = in_pairs([mixed_buf[slot, f, 0:cells, :] for f in range(frames)])
            mean = mean_square(pair)
            yield
            normed = by_frame(normalise(pair, mean), cells)
            left = jnp.concatenate([normed, normed_buf[h, 0:cells, :]], axis=1)
            out = jnp.dot(left, weight_ref[0:proj, :], preferred_element_type=F32)
            yield
            out = out[:, 0:LANES] + out[:, LANES:]
            acc[0:cells, :] += pltpu.roll(out, h, 1)
            yield

        acc[0:cells, :] = jnp.zeros((cells, LANES), F32)
        pairs = cols // 2

        def receive_next(h):
            if first_time and isinstance(h, int):
                receive(h)
            elif first_time:

                @pl.when(h < rows)
                def _():
                    receive(h)

        def steady(h, carry):
            lines = feats.at[:, pl.ds(h, 3)]
            ending, starting = finish(h - 1, lax.rem(h + 1, 2)), block_one(h + 2)
            settle(lines, 2)
            next(starting)
            next(ending)
            next(starting)
            convolve(h, lines, 0, pairs)
            next(ending)
            next(starting)
            next(ending)
            next(starting)
            receive_next(h + 3)
            return carry

        if first_time:
            receive(0)
            receive(1)
        ahead = block_one(0)
        for _ in ahead:
            pass
        settle(feats, 1)
        for _ in block_one(1):
            pass
        receive_next(2)
        settle(feats, 2)
        starting = block_one(2)
        next(starting)
        convolve(0, feats, 0, pairs)
        for _ in starting:
            pass
        receive_next(3)
        lax.fori_loop(1, rows - 2, steady, 0)
        lines = feats.at[:, pl.ds(rows - 2, 3)]
        settle(lines, 2)
        ending = finish(rows - 3, (rows - 3) % 2)
        next(ending)
        convolve(rows - 2, lines, 0, pairs)
        for _ in ending:
            pass
        ending = finish(rows - 2, (rows - 2) % 2)
        next(ending)
        convolve(rows - 1, feats.at[:, pl.ds(rows - 1, 3)], 0, pairs)
        for _ in ending:
            pass
        for _ in finish(rows - 1, (rows - 1) % 2):
            pass

    def arrived(j):
        if not pieces or j < share:
            return noise_ref[pl.ds(j, times, stride=block), :]
        spare = LANES - used
        lane = lax.broadcasted_iota(jnp.int32, (times, LANES), 1)
        total = jnp.zeros((times, LANES), F32)
        for k in range(pieces):
            piece = noise_ref[pl.ds(2 * HALO * k + j - share, times, stride=block), :]
            piece = pltpu.roll(piece, (k * spare + LANES - used) % LANES, 1)
            total = jnp.where((lane >= k * spare) & (lane < (k + 1) * spare), piece, total)
        return total

    def drift(cols, skip, through):
        f = acc[0 : cols * times, :].reshape(cols, times, LANES) + through + bias_out[None]
        noise = jnp.stack([arrived(skip + j) for j in range(cols)])
        return step * f + (NOISE_SCALE * math.sqrt(step)) * noise

    def running(values):
        when = lax.broadcasted_iota(jnp.int32, values.shape, 1)
        reach = 1
        while reach < times:
            values = values + jnp.where(when >= reach, pltpu.roll(values, reach, 1), 0.0)
            reach *= 2
        return values

    cols = share + 2 * HALO
    for j in range(cols + 4):
        at = table.own + j
        state[j] = jnp.broadcast_to(table_ref[at : at + 1, :], (times, LANES))
    run_network(cols, True)
    begin = table_ref[table.own + HALO : table.own + HALO + cols, :][:, None, :]
    through = table_ref[table.direct + HALO : table.direct + HALO + cols, :][:, None, :]
    moved = drift(cols, 0, through)
    col = lax.broadcasted_iota(jnp.int32, moved.shape, 0) + (index * share - HALO)
    inside = (col >= 0) & (col < columns)
    state[0:cols] = begin + jnp.where(inside, running(moved) - moved, 0.0)

    run_network(share, False)
    hi, lo = split(state[HALO : HALO + share].reshape(share * times, LANES))
    through = jnp.dot(
        jnp.concatenate([hi, lo], axis=1), weight_ref[proj:direct, :], preferred_element_type=F32
    )
    through = (through[:, 0:LANES] + through[:, LANES:]).reshape(share, times, LANES)
    own = table.own + 2 * HALO
    ended = table_ref[own : own + share, :][:, None, :] + running(drift(share, HALO, through))
    kept = returned_block(share, used)[1] * 2 * HALO
    if not kept:
        for j in range(share):
            out_ref[pl.ds(j, times, stride=share), :] = ended[j]
        return
    lane = lax.broadcasted_iota(jnp.int32, (times, LANES), 1)
    for j in range(kept):
        k, i = divmod(j, 2 * HALO)
        moved = pltpu.roll(ended[kept + i], used - k * (LANES - used), 1)
        leaving[pl.ds(j, times, stride=kept), :] = jnp.where(lane < used, ended[j], moved)
    for t in range(times):
        for k in range(kept // (2 * HALO)):
            at = t * kept + k * 2 * HALO
            out_ref[t, k] = leaving[at : at + 2 * HALO, :]


def unpack_kernel(share, sizes, in_ref, out_ref, lines):
    channels, frames, rows, columns = sizes
    used = channels * frames * rows
    pieces = returned_block(share, used)[1]
    if pieces:
        spare = LANES - used
        lane = lax.broadcasted_iota(jnp.int32, (2 * HALO, LANES), 1)
        for sender in range(columns // share):
            last = jnp.zeros((2 * HALO, LANES), F32)
            for k in range(pieces):
                at = sender * share + k * 2 * HALO
                block = in_ref[sender, k]
                lines[at : at + 2 * HALO, :] = block
                piece = pltpu.roll(block, (k * spare + LANES - used) % LANES, 1)
                last = jnp.where((lane >= k * spare) & (lane < (k + 1) * spare), piece, last)
            at = (sender + 1) * share - 2 * HALO
            lines[at : at + 2 * HALO, :] = last
        image = jnp.transpose(lines[...])
    else:
        image = jnp.transpose(in_ref[...])
    for f in range(frames):
        for c in range(channels):
            at = (f * channels + c) * rows
            out_ref[0, c, f] = image[at : at + rows, :]


def shards(start_frames, plan, noise, w_lift, w_time, spatial, temporal, w_point, w_out):
    times = lax.axis_size("tm")
    sizes = start_frames.shape
    channels, frames, rows, columns = sizes
    share = columns // times
    block, pieces = sent_block(share, channels * frames * rows)
    cols = share + 2 * HALO
    table = Table(share, sizes)
    params = limit([])
    codes = 2 * times if one_hot_fits(times, channels * rows) else 0
    mix_shape = (rows - AHEAD, frames // 2, 2 * LANES - codes, 4 * LANES)
    prep_scratch = [pltpu.VMEM(mix_shape, BF16), pltpu.VMEM(sizes, F32)]
    main_scratch = [
        pltpu.VMEM((frames, rows + 2, cols // 2, 4, times // SUB, SUB, LANES), F32),
        pltpu.VMEM((frames // 2, (cols + 2) * times, 2 * LANES), F32),
        pltpu.VMEM((2, frames, cols * times, LANES), F32),
        pltpu.VMEM((rows, cols * times, frames * LANES), BF16),
        pltpu.VMEM((cols * times, LANES), F32),
        pltpu.VMEM((cols + 4, times, LANES), F32),
        pltpu.VMEM((frames // 2, (cols + 2) * times, 2 * LANES), BF16),
        pltpu.VMEM(mix_shape, BF16),
        pltpu.VMEM((rows, frames // 2, max(codes, 16), 4 * LANES), BF16),
        pltpu.VMEM((times * share, LANES), F32),
    ]
    index = lax.axis_index("tm").astype(jnp.int32).reshape(1)
    hbm = whole(pltpu.HBM)

    packed = pl.pallas_call(
        functools.partial(pack_kernel, times, share),
        out_shape=pltpu.VMEM((times, block, LANES), F32),
        in_specs=[whole(pltpu.SMEM), whole()],
        out_specs=whole(),
        scratch_shapes=[
            pltpu.VMEM((columns + 2 * SUB, LANES), F32),
            pltpu.VMEM((max(pieces, 1), columns + 2 * SUB, LANES), F32),
        ],
        compiler_params=params,
        name="pack",
    )(plan, noise)
    arrived = lax.all_to_all(packed, "tm", split_axis=0, concat_axis=0, tiled=True)

    by_tap = (
        w_lift, jnp.transpose(spatial, (2, 0, 1)), jnp.transpose(temporal, (2, 0, 1)), w_point,
        jnp.transpose(w_out),
    )
    first, mix, lines, weights = pl.pallas_call(
        functools.partial(prep_kernel, share, sizes),
        out_shape=[
            pltpu.VMEM((AHEAD,) + mix_shape[1:], BF16),
            pltpu.HBM(mix_shape, BF16),
            pltpu.VMEM((table.size, LANES), F32),
            pltpu.VMEM((weight_rows(frames)[-1], 2 * LANES), BF16),
        ],
        in_specs=[whole(pltpu.SMEM)] + [hbm] * 6,
        out_specs=[whole(), hbm, whole(), whole()],
        scratch_shapes=prep_scratch
        + [pltpu.VMEM(a.shape, a.dtype) for a in by_tap]
        + [
            pltpu.VMEM((columns + 4 * SUB + table.wide, LANES), F32),
            pltpu.SemaphoreType.DMA((7,)),
        ],
        compiler_params=limit(prep_scratch),
        cost_estimate=pl.CostEstimate(flops=10**9, bytes_accessed=10**7, transcendentals=0),
        name="prep",
    )(index, *[in_hbm(a) for a in (start_frames,) + by_tap])

    shape, packed_back = returned_block(share, channels * frames * rows)
    result_shape = (times,) + shape if packed_back else (times * share, LANES)
    result = pl.pallas_call(
        functools.partial(main_kernel, share, sizes, times),
        out_shape=jax.ShapeDtypeStruct(result_shape, F32),
        in_specs=[whole(pltpu.SMEM), whole(), whole(), whole(), hbm, whole(), whole()],
        out_specs=whole(),
        scratch_shapes=main_scratch + [pltpu.SemaphoreType.DMA((rows - AHEAD,))],
        compiler_params=limit(main_scratch),
        name="sampler",
    )(index, arrived.reshape(times * block, LANES), w_time, first, in_hbm(mix), lines, weights)
    back = lax.all_to_all(
        result.reshape((times,) + shape), "tm", split_axis=0, concat_axis=0, tiled=True
    )
    return pl.pallas_call(
        functools.partial(unpack_kernel, share, sizes),
        out_shape=jax.ShapeDtypeStruct((1,) + sizes, F32),
        in_specs=[whole()],
        out_specs=whole(),
        scratch_shapes=[pltpu.VMEM((columns, LANES), F32)],
        compiler_params=params,
        name="unpack",
    )(back if packed_back else back.reshape(columns, LANES))


def solution(mesh):
    in_specs = (
        P("groups", None, None, None),
        P(("groups", "tm")),
        P("tm", "groups", None, None, None),
        P(),
        P(),
        P(),
        P(),
        P(),
        P(),
    )
    out_specs = P("tm", "groups", None, None, None)
    return jax.shard_map(shards, mesh=mesh, in_specs=in_specs, out_specs=out_specs, check_vma=False)
```

```python
import functools
import math

import jax
import jax.numpy as jnp
from jax import lax
from jax.experimental import pallas as pl
from jax.experimental.pallas import tpu as pltpu
from jax.sharding import PartitionSpec as P

ITERS = 2
LANES = 128
SUB = 8
HALO = 2
NOISE_SCALE = 2.0
EPS = 1e-06
AHEAD = 3
F32 = jnp.float32
BF16 = jnp.bfloat16
VMEM_ROOM = 12 * 1024 * 1024


def in_hbm(value):
    return pltpu.with_memory_space_constraint(value, pltpu.HBM)


def limit(scratch):
    held = [s for s in scratch if hasattr(s, "shape") and jnp.issubdtype(s.dtype, jnp.number)]
    size = sum(math.prod(s.shape) * jnp.dtype(s.dtype).itemsize for s in held)
    return pltpu.CompilerParams(vmem_limit_bytes=size + VMEM_ROOM)


def round_up(value, multiple):
    return (value + multiple - 1) // multiple * multiple


def whole(memory_space=pltpu.VMEM):
    return pl.BlockSpec(memory_space=memory_space)


def columns_as_rows(image, extra):
    channels, frames, rows, columns = image.shape
    parts = [image[c, f] for f in range(frames) for c in range(channels)]
    left = LANES - channels * frames * rows
    parts.append(jnp.full((left, columns), extra, F32))
    return jnp.transpose(jnp.concatenate(parts, axis=0))


def sent_block(share, used):
    spare = LANES - used
    if share % SUB == 0 and used % spare == 0 and used // spare * 2 * HALO < share:
        return share, used // spare
    return round_up(share + 2 * HALO, SUB), 0


def returned_block(share, used):
    pieces = sent_block(share, used)[1]
    if pieces and pieces * 2 * HALO == share - 2 * HALO:
        return (pieces, 2 * HALO, LANES), pieces
    return (share, LANES), 0


def pack_kernel(shares, share, plan_ref, noise_ref, out_ref, padded, moved):
    _, channels, frames, rows, columns = noise_ref.shape
    used = channels * frames * rows
    block, pieces = sent_block(share, used)
    edge = jnp.zeros((SUB, LANES), F32)
    padded[0:SUB, :] = edge
    padded[SUB + columns : 2 * SUB + columns, :] = edge
    image = columns_as_rows(noise_ref[0], plan_ref[0].astype(F32))
    padded[SUB : SUB + columns, :] = image
    for k in range(pieces):
        moved[k, 0:SUB, :] = edge
        moved[k, SUB + columns : 2 * SUB + columns, :] = edge
        moved[k, SUB : SUB + columns, :] = pltpu.roll(image, used - k * (LANES - used), 1)
    lane = lax.broadcasted_iota(jnp.int32, (2 * HALO, LANES), 1)
    for dest in range(shares):
        first = SUB - HALO + dest * share
        if pieces:
            for k in range(pieces):
                at = 2 * HALO * k
                out_ref[dest, at : at + 2 * HALO, :] = jnp.where(
                    lane < used,
                    padded[first + at : first + at + 2 * HALO, :],
                    moved[k, first + share : first + share + 2 * HALO, :],
                )
            at = 2 * HALO * pieces
            out_ref[dest, at:share, :] = padded[first + at : first + share, :]
        else:
            out_ref[dest, 0 : share + 2 * HALO, :] = padded[first : first + share + 2 * HALO, :]
            if block > share + 2 * HALO:
                out_ref[dest, share + 2 * HALO : block, :] = jnp.zeros(
                    (block - share - 2 * HALO, LANES), F32
                )


def window_of(frame, frames):
    return min(max(frame - 1, 0), frames - 3)


def one_hot_fits(times, group):
    return 9 * group + 2 * times <= 2 * LANES and (2 * LANES - 2 * times) % 16 == 0


def stack_taps(state, window, group, times):
    width = 3 * group
    before, here, after = [
        pltpu.roll(s, (LANES - window * group + k * width) % LANES, 1)
        for k, s in enumerate(state)
    ]
    lane = lax.broadcasted_iota(jnp.int32, before.shape, 1)
    first = jnp.where(lane < width, before, here)
    spill = 2 * width - LANES
    code = jnp.zeros_like(before)
    if one_hot_fits(times, group):
        when = lax.rem(lax.broadcasted_iota(jnp.int32, before.shape, 0), times)
        at = lane - (LANES - 2 * times)
        code = jnp.where((at >= 0) & (lax.rem(at + times, times) == when), 1.0, 0.0)
    second = jnp.where(
        lane < spill, here, jnp.where(lane < spill + width, after, code)
    )
    return jnp.concatenate([first.astype(BF16), second.astype(BF16)], axis=-1)


class Table:
    def __init__(self, share, sizes):
        _, frames, rows, _ = sizes
        self.wide = round_up(share + 4 * HALO, SUB)
        self.taps = 0
        self.edges = 15 * SUB
        self.own = self.edges + round_up(3 * frames * rows, SUB)
        self.direct = self.own + self.wide
        self.out = self.direct + self.wide
        self.size = self.out + LANES


def weight_rows(frames):
    proj = 2 * frames * LANES
    return proj, proj + 2 * LANES, proj + 4 * LANES, proj + 6 * LANES


def exact(a, b):
    return jnp.dot(a, b, precision=lax.Precision.HIGHEST, preferred_element_type=F32)


def split(value):
    top = value.astype(BF16)
    return top, (value - top.astype(F32)).astype(BF16)


def prep_kernel(
    share, sizes, index_ref, start_hbm, lift_hbm, spatial_hbm, temporal_hbm, point_hbm, out_hbm,
    first_ref, mix_hbm, table_ref, weight_ref,
    mix_ref, start_ref, lift_ref, spatial_ref, temporal_ref, point_ref, out_w_ref, padded, sems,
):
    channels, frames, rows, columns = sizes
    group = channels * rows
    index = index_ref[0]
    table = Table(share, sizes)
    plain = mix_ref.shape[2]
    copies = [
        pltpu.make_async_copy(source, target, sems.at[k])
        for k, (source, target) in enumerate([
            (start_hbm, start_ref), (lift_hbm, lift_ref), (spatial_hbm, spatial_ref),
            (temporal_hbm, temporal_ref), (point_hbm, point_ref), (out_hbm, out_w_ref),
        ])
    ]
    for copy in copies:
        copy.start()
    padded[...] = jnp.zeros_like(padded)
    for copy in copies:
        copy.wait()
    row = lax.broadcasted_iota(jnp.int32, (SUB, LANES), 0)

    zero = jnp.zeros((SUB, LANES), F32)
    sp = [spatial_ref[k, 0:1, :] for k in range(9)]
    tm = [temporal_ref[k, 0:1, :] for k in range(3)]
    lift = [lift_ref[c : c + 1, :] for c in range(channels)]
    timed = [[l * t for t in tm] for l in lift]
    for h in range(rows):
        by_tap = []
        for tap in range(3):
            total = zero
            for a in range(3):
                if 0 <= h + a - 1 < rows:
                    total = jnp.where(row == h + a - 1, sp[3 * a + tap], total)
            by_tap.append(total)
        made = [[[t * timed[c][k] for k in range(3)] for c in range(channels)] for t in by_tap]
        only = [jnp.where(row == h, l, 0.0) for l in lift]
        for f in range(frames):
            window = window_of(f, frames)
            mixes, ups = [], []
            for tap in range(3):
                for local in range(3):
                    k = window + local - f + 1
                    for c in range(channels):
                        mixes.append(made[tap][c][k] if 0 <= k < 3 else zero)
                        ups.append(only[c] if k == 1 and tap == 1 else zero)
            mixes += [zero] * (plain // SUB - len(mixes))
            ups += [zero] * (plain // SUB - len(ups))
            target, line = (first_ref, h) if h < AHEAD else (mix_ref, h - AHEAD)
            at = f % 2 * LANES
            target[line, f // 2, :, at : at + LANES] = jnp.concatenate(mixes, axis=0).astype(BF16)
            at += 2 * LANES
            target[line, f // 2, :, at : at + LANES] = jnp.concatenate(ups, axis=0).astype(BF16)
    leaving = pltpu.make_async_copy(mix_ref, mix_hbm, sems.at[6])
    leaving.start()

    lines = []
    for a in range(3):
        g = [spatial_ref[3 * a + c, 1:2, :] for c in range(3)]
        lines += [g[0], 0.5 * (g[0] + g[1] + g[2]), 0.5 * (g[0] - g[1] + g[2]), g[2]]
    lines += [temporal_ref[k, 1:2, :] for k in range(3)]
    for k, line in enumerate(lines):
        at = table.taps + k * SUB
        table_ref[at : at + SUB, :] = jnp.broadcast_to(line, (SUB, LANES))
    for tap in range(3):
        lines = []
        for f in range(frames):
            over = functools.reduce(
                jnp.add, [tm[k] for k in range(3) if 0 <= f + k - 1 < frames]
            )
            for h in range(rows):
                lines.append(over * functools.reduce(
                    jnp.add, [sp[3 * a + tap] for a in range(3) if 0 <= h + a - 1 < rows]
                ))
        at = table.edges + tap * frames * rows
        table_ref[at : at + frames * rows, :] = jnp.concatenate(lines, axis=0)

    left = jnp.zeros((LANES - frames * group, LANES), F32)
    spread = [jnp.broadcast_to(out_w_ref[c : c + 1, :], (rows, LANES)) for c in range(channels)]
    out_lanes = jnp.transpose(jnp.concatenate(spread * frames + [left], axis=0))
    table_ref[table.out : table.out + LANES, :] = out_lanes
    lane = lax.broadcasted_iota(jnp.int32, (LANES, LANES), 1)
    line = lax.broadcasted_iota(jnp.int32, (LANES, LANES), 0)
    first = jnp.where(lax.rem(lane, rows) == 0, out_lanes, 0.0)
    for slot, b in enumerate((1, 0)):
        folded = exact(point_ref[b].astype(F32), first)
        for f in range(frames):
            here = jnp.where((lane >= f * group) & (lane < (f + 1) * group), folded, 0.0)
            at = (slot * frames + f) * LANES
            weight_ref[at : at + LANES, 0:LANES], weight_ref[at : at + LANES, LANES:] = split(here)
    lift_rows = [jnp.broadcast_to(l, (rows, LANES)) for l in lift]
    both = exact(jnp.concatenate(lift_rows * frames + [left], axis=0), out_lanes)
    same = (lax.div(lane, group) == lax.div(line, group)) & (
        lax.rem(lane, rows) == lax.rem(line, rows)
    )
    both = jnp.where(same, both, 0.0)
    proj, direct, mixing, _ = weight_rows(frames)
    hi, lo = split(both)
    nothing = jnp.zeros((LANES, LANES), BF16)
    weight_ref[proj : proj + LANES, 0:LANES] = hi
    weight_ref[proj : proj + LANES, LANES:] = lo
    weight_ref[proj + LANES : direct, 0:LANES] = hi
    weight_ref[proj + LANES : direct, LANES:] = nothing
    for at, value in ((direct, point_ref[0]), (mixing, jnp.full((LANES, LANES), 4.0 / LANES, BF16))):
        weight_ref[at : at + LANES, 0:LANES] = value
        weight_ref[at + LANES : at + 2 * LANES, LANES:] = value
        weight_ref[at : at + LANES, LANES:] = nothing
        weight_ref[at + LANES : at + 2 * LANES, 0:LANES] = nothing

    lead = 2 * HALO + SUB
    padded[lead : lead + columns, :] = columns_as_rows(start_ref[...], 0.0)
    own = padded[pl.ds(SUB + index * share, table.wide), :]
    table_ref[table.own : table.own + table.wide, :] = own
    table_ref[table.direct : table.direct + table.wide, :] = exact(own, both)
    leaving.wait()


def main_kernel(
    share, sizes, times, index_ref, noise_ref, time_ref, first_ref, mix_hbm, table_ref, weight_ref,
    out_ref, feats, fresh, mixed_buf, normed_buf, acc, state, left_buf, mix_ref, hot_ref, leaving, sems,
):
    channels, frames, rows, columns = sizes
    group = channels * rows
    index = index_ref[0]
    step = 1.0 / times
    table = Table(share, sizes)
    halves = times // SUB
    proj, direct, mixing, mean_end = weight_rows(frames)
    hot = one_hot_fits(times, group)
    used = frames * group
    block, pieces = sent_block(share, used)

    def arrival(k):
        return pltpu.make_async_copy(mix_hbm.at[k], mix_ref.at[k], sems.at[k])

    for k in range(rows - AHEAD):
        arrival(k).start()

    half = LANES // 2
    line = share - 1 if pieces else HALO
    planned = noise_ref[pl.ds(line, times, stride=block), :][:, LANES - 1 : LANES]
    lane = lax.broadcasted_iota(jnp.int32, (1, LANES), 1)
    place = jnp.where(lane < half, lane, lane - half).astype(F32)
    angles = planned * jnp.exp(place * (-math.log(1000.0) / half))
    embedded = jnp.where(lane < half, jnp.sin(angles), jnp.cos(angles))
    bias = exact(embedded, time_ref[...])
    bias_out = exact(bias, table_ref[table.out : table.out + LANES, :])

    def mean_square(pair):
        return jnp.dot(
            (pair * pair).astype(BF16), weight_ref[mixing:mean_end, :], preferred_element_type=F32
        )

    def normalise(pair, mean):
        value = pair * lax.rsqrt(mean + 4.0 * EPS)
        return (value + value * jnp.tanh(value)).astype(BF16)

    def in_pairs(values):
        return jnp.concatenate(
            [jnp.concatenate(values[f : f + 2], axis=1) for f in range(0, frames, 2)], axis=0
        )

    def by_frame(pairs, cells):
        return jnp.concatenate(
            [pairs[k * cells : (k + 1) * cells] for k in range(frames // 2)], axis=1
        )

    def bias_taps(h):
        return [
            jnp.concatenate(
                [
                    bias * table_ref[pl.ds(table.edges + (k * frames + f) * rows + h, 1), :]
                    for f in range(frames)
                ],
                axis=1,
            )
            for k in range(3)
        ]

    def receive(h):
        if not isinstance(h, int):
            arrival(h - AHEAD).wait()
        elif h >= AHEAD:
            arrival(h - AHEAD).wait()
        if hot:
            by_tap = bias_taps(h)
            every = by_tap[0] + by_tap[1] + by_tap[2]
            for p in range(frames // 2):
                here = every[:, 2 * p * LANES : 2 * (p + 1) * LANES]
                terms = jnp.concatenate([here, bias, bias], axis=1)
                hot_ref[h, p, 0:times, :], hot_ref[h, p, times:, :] = split(terms)

    def lift_weights(h, p, lanes):
        if isinstance(h, int) and h < AHEAD:
            taken = first_ref[h, p, :, lanes]
        else:
            taken = mix_ref[h - AHEAD, p, :, lanes]
        return jnp.concatenate([taken, hot_ref[h, p, :, lanes]], axis=0) if hot else taken

    def run_network(cols, first_time):
        wide = cols + 2
        cells = cols * times
        many = wide * times
        margin = (wide - share) // 2
        flags = {}
        for j in list(range(margin)) + list(range(wide - margin, wide)):
            col = index * share + j - margin
            flags[j] = jnp.where((col >= 0) & (col < columns), 1.0, 0.0).astype(F32)
        first_column = {
            margin - i * share: jnp.where(index == i, 1.0, 0.0).astype(F32)
            for i in range(margin // share + 1)
        }
        last_column = {
            wide - margin - 1 + i * share: jnp.where(
                (index + 1 + i) * share == columns, 1.0, 0.0
            ).astype(F32)
            for i in range(margin // share + 1)
        }
        taps = [table_ref[table.taps + k * SUB : table.taps + (k + 1) * SUB, :] for k in range(15)]
        around = [state[k : k + wide].reshape(many, LANES) for k in range(3)]
        for p in range(frames // 2):
            left_buf[p, 0:many, :] = stack_taps(around, p, group, times)

        def block_one(h):
            linear = [
                jnp.dot(
                    left_buf[p, 0:many, :], lift_weights(h, p, slice(0, 2 * LANES)),
                    preferred_element_type=F32,
                )
                for p in range(frames // 2)
            ]
            yield
            by_tap = bias_taps(h)
            parts = []
            for p in range(frames // 2):
                lanes = slice(2 * p * LANES, 2 * (p + 1) * LANES)
                mixed = linear[p]
                if not hot:
                    every = by_tap[0] + by_tap[1] + by_tap[2]
                    mixed = mixed + jnp.concatenate([every[:, lanes]] * wide, axis=0)
                for j in range(wide):
                    value = mixed[j * times : (j + 1) * times]
                    if j in first_column:
                        value = value - by_tap[0][:, lanes] * first_column[j]
                    if j in last_column:
                        value = value - by_tap[2][:, lanes] * last_column[j]
                    parts.append(value)
            pair = jnp.concatenate(parts, axis=0)
            mean = mean_square(pair)
            yield
            normed = normalise(pair, mean)
            normed_buf[h, 0:cells, :] = by_frame(normed, many)[times : times + cells]
            updates = []
            for p in range(frames // 2):
                both = jnp.concatenate([normed[p * many : (p + 1) * many], left_buf[p, 0:many, :]], axis=1)
                onto = jnp.concatenate(
                    [weight_ref[direct:mixing, :], lift_weights(h, p, slice(2 * LANES, 4 * LANES))], axis=0
                )
                updates.append(jnp.dot(both, onto, preferred_element_type=F32))
            yield
            for p in range(frames // 2):
                fresh[p, 0:many, :] = updates[p]
            yield

        def settle(lines, line):
            for f in range(frames):
                lanes = slice(f % 2 * LANES, (f % 2 + 1) * LANES)
                new = []
                for j in range(wide):
                    value = fresh[f // 2, j * times : (j + 1) * times, lanes]
                    if not hot:
                        value = value + bias
                    value = value.reshape(halves, SUB, LANES)
                    new.append(value * flags[j] if j in flags else value)
                for q in range(cols // 2):
                    d = new[2 * q : 2 * q + 4]
                    lines[f, line, q, 0] = d[0] - d[2]
                    lines[f, line, q, 1] = d[1] + d[2]
                    lines[f, line, q, 2] = d[2] - d[1]
                    lines[f, line, q, 3] = d[1] - d[3]

        def convolve(h, lines, begin, end):
            inside = range(3)
            if isinstance(h, int):
                inside = [a for a in range(3) if 0 <= h + a - 1 < rows]
            for q in range(begin, end):
                spread = []
                for f in range(frames):
                    m = []
                    for i in range(4):
                        terms = [lines[f, a, q, i] * taps[4 * a + i] for a in inside]
                        m.append(functools.reduce(jnp.add, terms))
                    spread.append((m[0] + m[1] + m[2], m[1] - m[2] - m[3]))
                for f in range(frames):
                    for side in range(2):
                        total = None
                        for k in range(3):
                            if 0 <= f + k - 1 < frames:
                                term = spread[f + k - 1][side] * taps[12 + k]
                                total = term if total is None else total + term
                        at = (2 * q + side) * times
                        mixed_buf[lax.rem(h, 2), f, at : at + times, :] = total.reshape(times, LANES)

        def finish(h, slot):
            pair = in_pairs([mixed_buf[slot, f, 0:cells, :] for f in range(frames)])
            mean = mean_square(pair)
            yield
            normed = by_frame(normalise(pair, mean), cells)
            left = jnp.concatenate([normed, normed_buf[h, 0:cells, :]], axis=1)
            out = jnp.dot(left, weight_ref[0:proj, :], preferred_element_type=F32)
            yield
            out = out[:, 0:LANES] + out[:, LANES:]
            acc[0:cells, :] += pltpu.roll(out, h, 1)
            yield

        acc[0:cells, :] = jnp.zeros((cells, LANES), F32)
        pairs = cols // 2

        def receive_next(h):
            if first_time and isinstance(h, int):
                receive(h)
            elif first_time:

                @pl.when(h < rows)
                def _():
                    receive(h)

        def steady(h, carry):
            lines = feats.at[:, pl.ds(h, 3)]
            ending, starting = finish(h - 1, lax.rem(h + 1, 2)), block_one(h + 2)
            settle(lines, 2)
            next(starting)
            next(ending)
            next(starting)
            convolve(h, lines, 0, pairs)
            next(ending)
            next(starting)
            next(ending)
            next(starting)
            receive_next(h + 3)
            return carry

        if first_time:
            receive(0)
            receive(1)
        ahead = block_one(0)
        for _ in ahead:
            pass
        settle(feats, 1)
        for _ in block_one(1):
            pass
        receive_next(2)
        settle(feats, 2)
        starting = block_one(2)
        next(starting)
        convolve(0, feats, 0, pairs)
        for _ in starting:
            pass
        receive_next(3)
        lax.fori_loop(1, rows - 2, steady, 0)
        lines = feats.at[:, pl.ds(rows - 2, 3)]
        settle(lines, 2)
        ending = finish(rows - 3, (rows - 3) % 2)
        next(ending)
        convolve(rows - 2, lines, 0, pairs)
        for _ in ending:
            pass
        ending = finish(rows - 2, (rows - 2) % 2)
        next(ending)
        convolve(rows - 1, feats.at[:, pl.ds(rows - 1, 3)], 0, pairs)
        for _ in ending:
            pass
        for _ in finish(rows - 1, (rows - 1) % 2):
            pass

    def arrived(j):
        if not pieces or j < share:
            return noise_ref[pl.ds(j, times, stride=block), :]
        spare = LANES - used
        lane = lax.broadcasted_iota(jnp.int32, (times, LANES), 1)
        total = jnp.zeros((times, LANES), F32)
        for k in range(pieces):
            piece = noise_ref[pl.ds(2 * HALO * k + j - share, times, stride=block), :]
            piece = pltpu.roll(piece, (k * spare + LANES - used) % LANES, 1)
            total = jnp.where((lane >= k * spare) & (lane < (k + 1) * spare), piece, total)
        return total

    def drift(cols, skip, through):
        f = acc[0 : cols * times, :].reshape(cols, times, LANES) + through + bias_out[None]
        noise = jnp.stack([arrived(skip + j) for j in range(cols)])
        return step * f + (NOISE_SCALE * math.sqrt(step)) * noise

    def running(values):
        when = lax.broadcasted_iota(jnp.int32, values.shape, 1)
        reach = 1
        while reach < times:
            values = values + jnp.where(when >= reach, pltpu.roll(values, reach, 1), 0.0)
            reach *= 2
        return values

    cols = share + 2 * HALO
    for j in range(cols + 4):
        at = table.own + j
        state[j] = jnp.broadcast_to(table_ref[at : at + 1, :], (times, LANES))
    run_network(cols, True)
    begin = table_ref[table.own + HALO : table.own + HALO + cols, :][:, None, :]
    through = table_ref[table.direct + HALO : table.direct + HALO + cols, :][:, None, :]
    moved = drift(cols, 0, through)
    col = lax.broadcasted_iota(jnp.int32, moved.shape, 0) + (index * share - HALO)
    inside = (col >= 0) & (col < columns)
    state[0:cols] = begin + jnp.where(inside, running(moved) - moved, 0.0)

    run_network(share, False)
    hi, lo = split(state[HALO : HALO + share].reshape(share * times, LANES))
    through = jnp.dot(
        jnp.concatenate([hi, lo], axis=1), weight_ref[proj:direct, :], preferred_element_type=F32
    )
    through = (through[:, 0:LANES] + through[:, LANES:]).reshape(share, times, LANES)
    own = table.own + 2 * HALO
    ended = table_ref[own : own + share, :][:, None, :] + running(drift(share, HALO, through))
    kept = returned_block(share, used)[1] * 2 * HALO
    if not kept:
        for j in range(share):
            out_ref[pl.ds(j, times, stride=share), :] = ended[j]
        return
    lane = lax.broadcasted_iota(jnp.int32, (times, LANES), 1)
    for j in range(kept):
        k, i = divmod(j, 2 * HALO)
        moved = pltpu.roll(ended[kept + i], used - k * (LANES - used), 1)
        leaving[pl.ds(j, times, stride=kept), :] = jnp.where(lane < used, ended[j], moved)
    for t in range(times):
        for k in range(kept // (2 * HALO)):
            at = t * kept + k * 2 * HALO
            out_ref[t, k] = leaving[at : at + 2 * HALO, :]


def unpack_kernel(share, sizes, in_ref, out_ref, lines):
    channels, frames, rows, columns = sizes
    used = channels * frames * rows
    pieces = returned_block(share, used)[1]
    if pieces:
        spare = LANES - used
        lane = lax.broadcasted_iota(jnp.int32, (2 * HALO, LANES), 1)
        for sender in range(columns // share):
            last = jnp.zeros((2 * HALO, LANES), F32)
            for k in range(pieces):
                at = sender * share + k * 2 * HALO
                block = in_ref[sender, k]
                lines[at : at + 2 * HALO, :] = block
                piece = pltpu.roll(block, (k * spare + LANES - used) % LANES, 1)
                last = jnp.where((lane >= k * spare) & (lane < (k + 1) * spare), piece, last)
            at = (sender + 1) * share - 2 * HALO
            lines[at : at + 2 * HALO, :] = last
        image = jnp.transpose(lines[...])
    else:
        image = jnp.transpose(in_ref[...])
    for f in range(frames):
        for c in range(channels):
            at = (f * channels + c) * rows
            out_ref[0, c, f] = image[at : at + rows, :]


def shards(start_frames, plan, noise, w_lift, w_time, spatial, temporal, w_point, w_out):
    times = lax.axis_size("tm")
    sizes = start_frames.shape
    channels, frames, rows, columns = sizes
    share = columns // times
    block, pieces = sent_block(share, channels * frames * rows)
    cols = share + 2 * HALO
    table = Table(share, sizes)
    params = limit([])
    codes = 2 * times if one_hot_fits(times, channels * rows) else 0
    mix_shape = (rows - AHEAD, frames // 2, 2 * LANES - codes, 4 * LANES)
    prep_scratch = [pltpu.VMEM(mix_shape, BF16), pltpu.VMEM(sizes, F32)]
    main_scratch = [
        pltpu.VMEM((frames, rows + 2, cols // 2, 4, times // SUB, SUB, LANES), F32),
        pltpu.VMEM((frames // 2, (cols + 2) * times, 2 * LANES), F32),
        pltpu.VMEM((2, frames, cols * times, LANES), F32),
        pltpu.VMEM((rows, cols * times, frames * LANES), BF16),
        pltpu.VMEM((cols * times, LANES), F32),
        pltpu.VMEM((cols + 4, times, LANES), F32),
        pltpu.VMEM((frames // 2, (cols + 2) * times, 2 * LANES), BF16),
        pltpu.VMEM(mix_shape, BF16),
        pltpu.VMEM((rows, frames // 2, max(codes, 16), 4 * LANES), BF16),
        pltpu.VMEM((times * share, LANES), F32),
    ]
    index = lax.axis_index("tm").astype(jnp.int32).reshape(1)
    hbm = whole(pltpu.HBM)

    packed = pl.pallas_call(
        functools.partial(pack_kernel, times, share),
        out_shape=pltpu.VMEM((times, block, LANES), F32),
        in_specs=[whole(pltpu.SMEM), whole()],
        out_specs=whole(),
        scratch_shapes=[
            pltpu.VMEM((columns + 2 * SUB, LANES), F32),
            pltpu.VMEM((max(pieces, 1), columns + 2 * SUB, LANES), F32),
        ],
        compiler_params=params,
        name="pack",
    )(plan, noise)
    arrived = lax.all_to_all(packed, "tm", split_axis=0, concat_axis=0, tiled=True)

    by_tap = (
        w_lift, jnp.transpose(spatial, (2, 0, 1)), jnp.transpose(temporal, (2, 0, 1)), w_point,
        jnp.transpose(w_out),
    )
    first, mix, lines, weights = pl.pallas_call(
        functools.partial(prep_kernel, share, sizes),
        out_shape=[
            pltpu.VMEM((AHEAD,) + mix_shape[1:], BF16),
            pltpu.HBM(mix_shape, BF16),
            pltpu.VMEM((table.size, LANES), F32),
            pltpu.VMEM((weight_rows(frames)[-1], 2 * LANES), BF16),
        ],
        in_specs=[whole(pltpu.SMEM)] + [hbm] * 6,
        out_specs=[whole(), hbm, whole(), whole()],
        scratch_shapes=prep_scratch
        + [pltpu.VMEM(a.shape, a.dtype) for a in by_tap]
        + [
            pltpu.VMEM((columns + 4 * SUB + table.wide, LANES), F32),
            pltpu.SemaphoreType.DMA((7,)),
        ],
        compiler_params=limit(prep_scratch),
        cost_estimate=pl.CostEstimate(flops=10**9, bytes_accessed=10**7, transcendentals=0),
        name="prep",
    )(index, *[in_hbm(a) for a in (start_frames,) + by_tap])

    shape, packed_back = returned_block(share, channels * frames * rows)
    result_shape = (times,) + shape if packed_back else (times * share, LANES)
    result = pl.pallas_call(
        functools.partial(main_kernel, share, sizes, times),
        out_shape=jax.ShapeDtypeStruct(result_shape, F32),
        in_specs=[whole(pltpu.SMEM), whole(), whole(), whole(), hbm, whole(), whole()],
        out_specs=whole(),
        scratch_shapes=main_scratch + [pltpu.SemaphoreType.DMA((rows - AHEAD,))],
        compiler_params=limit(main_scratch),
        name="sampler",
    )(index, arrived.reshape(times * block, LANES), w_time, first, in_hbm(mix), lines, weights)
    back = lax.all_to_all(
        result.reshape((times,) + shape), "tm", split_axis=0, concat_axis=0, tiled=True
    )
    return pl.pallas_call(
        functools.partial(unpack_kernel, share, sizes),
        out_shape=jax.ShapeDtypeStruct((1,) + sizes, F32),
        in_specs=[whole()],
        out_specs=whole(),
        scratch_shapes=[pltpu.VMEM((columns, LANES), F32)],
        compiler_params=params,
        name="unpack",
    )(back if packed_back else back.reshape(columns, LANES))


def solution(mesh):
    in_specs = (
        P("groups", None, None, None),
        P(("groups", "tm")),
        P("tm", "groups", None, None, None),
        P(),
        P(),
        P(),
        P(),
        P(),
        P(),
    )
    out_specs = P("tm", "groups", None, None, None)
    return jax.shard_map(shards, mesh=mesh, in_specs=in_specs, out_specs=out_specs, check_vma=False)
```

```python
import functools
import math

import jax
import jax.numpy as jnp
from jax import lax
from jax.experimental import pallas as pl
from jax.experimental.pallas import tpu as pltpu
from jax.sharding import PartitionSpec as P

ITERS = 2
LANES = 128
SUB = 8
HALO = 2
NOISE_SCALE = 2.0
EPS = 1e-06
AHEAD = 3
F32 = jnp.float32
BF16 = jnp.bfloat16
VMEM_ROOM = 12 * 1024 * 1024


def in_hbm(value):
    return pltpu.with_memory_space_constraint(value, pltpu.HBM)


def limit(scratch):
    held = [s for s in scratch if hasattr(s, "shape") and jnp.issubdtype(s.dtype, jnp.number)]
    size = sum(math.prod(s.shape) * jnp.dtype(s.dtype).itemsize for s in held)
    return pltpu.CompilerParams(vmem_limit_bytes=size + VMEM_ROOM)


def round_up(value, multiple):
    return (value + multiple - 1) // multiple * multiple


def whole(memory_space=pltpu.VMEM):
    return pl.BlockSpec(memory_space=memory_space)


def columns_as_rows(image, extra):
    channels, frames, rows, columns = image.shape
    parts = [image[c, f] for f in range(frames) for c in range(channels)]
    left = LANES - channels * frames * rows
    parts.append(jnp.full((left, columns), extra, F32))
    return jnp.transpose(jnp.concatenate(parts, axis=0))


def sent_block(share, used):
    spare = LANES - used
    if share % SUB == 0 and used % spare == 0 and used // spare * 2 * HALO < share:
        return share, used // spare
    return round_up(share + 2 * HALO, SUB), 0


def returned_block(share, used):
    pieces = sent_block(share, used)[1]
    if pieces and pieces * 2 * HALO == share - 2 * HALO:
        return (pieces, 2 * HALO, LANES), pieces
    return (share, LANES), 0


def pack_kernel(shares, share, plan_ref, noise_ref, out_ref, padded, moved):
    _, channels, frames, rows, columns = noise_ref.shape
    used = channels * frames * rows
    block, pieces = sent_block(share, used)
    edge = jnp.zeros((SUB, LANES), F32)
    padded[0:SUB, :] = edge
    padded[SUB + columns : 2 * SUB + columns, :] = edge
    image = columns_as_rows(noise_ref[0], plan_ref[0].astype(F32))
    padded[SUB : SUB + columns, :] = image
    for k in range(pieces):
        moved[k, 0:SUB, :] = edge
        moved[k, SUB + columns : 2 * SUB + columns, :] = edge
        moved[k, SUB : SUB + columns, :] = pltpu.roll(image, used - k * (LANES - used), 1)
    lane = lax.broadcasted_iota(jnp.int32, (2 * HALO, LANES), 1)
    for dest in range(shares):
        first = SUB - HALO + dest * share
        if pieces:
            for k in range(pieces):
                at = 2 * HALO * k
                out_ref[dest, at : at + 2 * HALO, :] = jnp.where(
                    lane < used,
                    padded[first + at : first + at + 2 * HALO, :],
                    moved[k, first + share : first + share + 2 * HALO, :],
                )
            at = 2 * HALO * pieces
            out_ref[dest, at:share, :] = padded[first + at : first + share, :]
        else:
            out_ref[dest, 0 : share + 2 * HALO, :] = padded[first : first + share + 2 * HALO, :]
            if block > share + 2 * HALO:
                out_ref[dest, share + 2 * HALO : block, :] = jnp.zeros(
                    (block - share - 2 * HALO, LANES), F32
                )


def window_of(frame, frames):
    return min(max(frame - 1, 0), frames - 3)


def one_hot_fits(times, group):
    return False


def stack_taps(state, window, group, times):
    width = 3 * group
    before, here, after = [
        pltpu.roll(s, (LANES - window * group + k * width) % LANES, 1)
        for k, s in enumerate(state)
    ]
    lane = lax.broadcasted_iota(jnp.int32, before.shape, 1)
    first = jnp.where(lane < width, before, here)
    spill = 2 * width - LANES
    code = jnp.zeros_like(before)
    if one_hot_fits(times, group):
        when = lax.rem(lax.broadcasted_iota(jnp.int32, before.shape, 0), times)
        at = lane - (LANES - 2 * times)
        code = jnp.where((at >= 0) & (lax.rem(at + times, times) == when), 1.0, 0.0)
    second = jnp.where(
        lane < spill, here, jnp.where(lane < spill + width, after, code)
    )
    return jnp.concatenate([first.astype(BF16), second.astype(BF16)], axis=-1)


class Table:
    def __init__(self, share, sizes):
        _, frames, rows, _ = sizes
        self.wide = round_up(share + 4 * HALO, SUB)
        self.taps = 0
        self.edges = 15 * SUB
        self.own = self.edges + round_up(3 * frames * rows, SUB)
        self.direct = self.own + self.wide
        self.out = self.direct + self.wide
        self.size = self.out + LANES


def weight_rows(frames):
    proj = 2 * frames * LANES
    return proj, proj + 2 * LANES, proj + 4 * LANES, proj + 6 * LANES


def exact(a, b):
    return jnp.dot(a, b, precision=lax.Precision.HIGHEST, preferred_element_type=F32)


def split(value):
    top = value.astype(BF16)
    return top, (value - top.astype(F32)).astype(BF16)


def prep_kernel(
    share, sizes, index_ref, start_hbm, lift_hbm, spatial_hbm, temporal_hbm, point_hbm, out_hbm,
    first_ref, mix_hbm, table_ref, weight_ref,
    mix_ref, start_ref, lift_ref, spatial_ref, temporal_ref, point_ref, out_w_ref, padded, sems,
):
    channels, frames, rows, columns = sizes
    group = channels * rows
    index = index_ref[0]
    table = Table(share, sizes)
    plain = mix_ref.shape[2]
    copies = [
        pltpu.make_async_copy(source, target, sems.at[k])
        for k, (source, target) in enumerate([
            (start_hbm, start_ref), (lift_hbm, lift_ref), (spatial_hbm, spatial_ref),
            (temporal_hbm, temporal_ref), (point_hbm, point_ref), (out_hbm, out_w_ref),
        ])
    ]
    for copy in copies:
        copy.start()
    padded[...] = jnp.zeros_like(padded)
    for copy in copies:
        copy.wait()
    row = lax.broadcasted_iota(jnp.int32, (SUB, LANES), 0)

    zero = jnp.zeros((SUB, LANES), F32)
    sp = [spatial_ref[k, 0:1, :] for k in range(9)]
    tm = [temporal_ref[k, 0:1, :] for k in range(3)]
    lift = [lift_ref[c : c + 1, :] for c in range(channels)]
    timed = [[l * t for t in tm] for l in lift]
    for h in range(rows):
        by_tap = []
        for tap in range(3):
            total = zero
            for a in range(3):
                if 0 <= h + a - 1 < rows:
                    total = jnp.where(row == h + a - 1, sp[3 * a + tap], total)
            by_tap.append(total)
        made = [[[t * timed[c][k] for k in range(3)] for c in range(channels)] for t in by_tap]
        only = [jnp.where(row == h, l, 0.0) for l in lift]
        for f in range(frames):
            window = window_of(f, frames)
            mixes, ups = [], []
            for tap in range(3):
                for local in range(3):
                    k = window + local - f + 1
                    for c in range(channels):
                        mixes.append(made[tap][c][k] if 0 <= k < 3 else zero)
                        ups.append(only[c] if k == 1 and tap == 1 else zero)
            mixes += [zero] * (plain // SUB - len(mixes))
            ups += [zero] * (plain // SUB - len(ups))
            target, line = (first_ref, h) if h < AHEAD else (mix_ref, h - AHEAD)
            at = f % 2 * LANES
            target[line, f // 2, :, at : at + LANES] = jnp.concatenate(mixes, axis=0).astype(BF16)
            at += 2 * LANES
            target[line, f // 2, :, at : at + LANES] = jnp.concatenate(ups, axis=0).astype(BF16)
    leaving = pltpu.make_async_copy(mix_ref, mix_hbm, sems.at[6])
    leaving.start()

    lines = []
    for a in range(3):
        g = [spatial_ref[3 * a + c, 1:2, :] for c in range(3)]
        lines += [g[0], 0.5 * (g[0] + g[1] + g[2]), 0.5 * (g[0] - g[1] + g[2]), g[2]]
    lines += [temporal_ref[k, 1:2, :] for k in range(3)]
    for k, line in enumerate(lines):
        at = table.taps + k * SUB
        table_ref[at : at + SUB, :] = jnp.broadcast_to(line, (SUB, LANES))
    for tap in range(3):
        lines = []
        for f in range(frames):
            over = functools.reduce(
                jnp.add, [tm[k] for k in range(3) if 0 <= f + k - 1 < frames]
            )
            for h in range(rows):
                lines.append(over * functools.reduce(
                    jnp.add, [sp[3 * a + tap] for a in range(3) if 0 <= h + a - 1 < rows]
                ))
        at = table.edges + tap * frames * rows
        table_ref[at : at + frames * rows, :] = jnp.concatenate(lines, axis=0)

    left = jnp.zeros((LANES - frames * group, LANES), F32)
    spread = [jnp.broadcast_to(out_w_ref[c : c + 1, :], (rows, LANES)) for c in range(channels)]
    out_lanes = jnp.transpose(jnp.concatenate(spread * frames + [left], axis=0))
    table_ref[table.out : table.out + LANES, :] = out_lanes
    lane = lax.broadcasted_iota(jnp.int32, (LANES, LANES), 1)
    line = lax.broadcasted_iota(jnp.int32, (LANES, LANES), 0)
    first = jnp.where(lax.rem(lane, rows) == 0, out_lanes, 0.0)
    for slot, b in enumerate((1, 0)):
        folded = exact(point_ref[b].astype(F32), first)
        for f in range(frames):
            here = jnp.where((lane >= f * group) & (lane < (f + 1) * group), folded, 0.0)
            at = (slot * frames + f) * LANES
            weight_ref[at : at + LANES, 0:LANES], weight_ref[at : at + LANES, LANES:] = split(here)
    lift_rows = [jnp.broadcast_to(l, (rows, LANES)) for l in lift]
    both = exact(jnp.concatenate(lift_rows * frames + [left], axis=0), out_lanes)
    same = (lax.div(lane, group) == lax.div(line, group)) & (
        lax.rem(lane, rows) == lax.rem(line, rows)
    )
    both = jnp.where(same, both, 0.0)
    proj, direct, mixing, _ = weight_rows(frames)
    hi, lo = split(both)
    nothing = jnp.zeros((LANES, LANES), BF16)
    weight_ref[proj : proj + LANES, 0:LANES] = hi
    weight_ref[proj : proj + LANES, LANES:] = lo
    weight_ref[proj + LANES : direct, 0:LANES] = hi
    weight_ref[proj + LANES : direct, LANES:] = nothing
    for at, value in ((direct, point_ref[0]), (mixing, jnp.full((LANES, LANES), 4.0 / LANES, BF16))):
        weight_ref[at : at + LANES, 0:LANES] = value
        weight_ref[at + LANES : at + 2 * LANES, LANES:] = value
        weight_ref[at : at + LANES, LANES:] = nothing
        weight_ref[at + LANES : at + 2 * LANES, 0:LANES] = nothing

    lead = 2 * HALO + SUB
    padded[lead : lead + columns, :] = columns_as_rows(start_ref[...], 0.0)
    own = padded[pl.ds(SUB + index * share, table.wide), :]
    table_ref[table.own : table.own + table.wide, :] = own
    table_ref[table.direct : table.direct + table.wide, :] = exact(own, both)
    leaving.wait()


def main_kernel(
    share, sizes, times, index_ref, noise_ref, time_ref, first_ref, mix_hbm, table_ref, weight_ref,
    out_ref, feats, fresh, mixed_buf, normed_buf, acc, state, left_buf, mix_ref, hot_ref, leaving, sems,
):
    channels, frames, rows, columns = sizes
    group = channels * rows
    index = index_ref[0]
    step = 1.0 / times
    table = Table(share, sizes)
    halves = times // SUB
    proj, direct, mixing, mean_end = weight_rows(frames)
    hot = one_hot_fits(times, group)
    used = frames * group
    block, pieces = sent_block(share, used)

    def arrival(k):
        return pltpu.make_async_copy(mix_hbm.at[k], mix_ref.at[k], sems.at[k])

    for k in range(rows - AHEAD):
        arrival(k).start()

    half = LANES // 2
    line = share - 1 if pieces else HALO
    planned = noise_ref[pl.ds(line, times, stride=block), :][:, LANES - 1 : LANES]
    lane = lax.broadcasted_iota(jnp.int32, (1, LANES), 1)
    place = jnp.where(lane < half, lane, lane - half).astype(F32)
    angles = planned * jnp.exp(place * (-math.log(1000.0) / half))
    embedded = jnp.where(lane < half, jnp.sin(angles), jnp.cos(angles))
    bias = exact(embedded, time_ref[...])
    bias_out = exact(bias, table_ref[table.out : table.out + LANES, :])

    def mean_square(pair):
        return jnp.dot(
            (pair * pair).astype(BF16), weight_ref[mixing:mean_end, :], preferred_element_type=F32
        )

    def normalise(pair, mean):
        value = pair * lax.rsqrt(mean + 4.0 * EPS)
        return (value + value * jnp.tanh(value)).astype(BF16)

    def in_pairs(values):
        return jnp.concatenate(
            [jnp.concatenate(values[f : f + 2], axis=1) for f in range(0, frames, 2)], axis=0
        )

    def by_frame(pairs, cells):
        return jnp.concatenate(
            [pairs[k * cells : (k + 1) * cells] for k in range(frames // 2)], axis=1
        )

    def bias_taps(h):
        return [
            jnp.concatenate(
                [
                    bias * table_ref[pl.ds(table.edges + (k * frames + f) * rows + h, 1), :]
                    for f in range(frames)
                ],
                axis=1,
            )
            for k in range(3)
        ]

    def receive(h):
        if not isinstance(h, int):
            arrival(h - AHEAD).wait()
        elif h >= AHEAD:
            arrival(h - AHEAD).wait()
        if hot:
            by_tap = bias_taps(h)
            every = by_tap[0] + by_tap[1] + by_tap[2]
            for p in range(frames // 2):
                here = every[:, 2 * p * LANES : 2 * (p + 1) * LANES]
                terms = jnp.concatenate([here, bias, bias], axis=1)
                hot_ref[h, p, 0:times, :], hot_ref[h, p, times:, :] = split(terms)

    def lift_weights(h, p, lanes):
        if isinstance(h, int) and h < AHEAD:
            taken = first_ref[h, p, :, lanes]
        else:
            taken = mix_ref[h - AHEAD, p, :, lanes]
        return jnp.concatenate([taken, hot_ref[h, p, :, lanes]], axis=0) if hot else taken

    def run_network(cols, first_time):
        wide = cols + 2
        cells = cols * times
        many = wide * times
        margin = (wide - share) // 2
        flags = {}
        for j in list(range(margin)) + list(range(wide - margin, wide)):
            col = index * share + j - margin
            flags[j] = jnp.where((col >= 0) & (col < columns), 1.0, 0.0).astype(F32)
        first_column = {
            margin - i * share: jnp.where(index == i, 1.0, 0.0).astype(F32)
            for i in range(margin // share + 1)
        }
        last_column = {
            wide - margin - 1 + i * share: jnp.where(
                (index + 1 + i) * share == columns, 1.0, 0.0
            ).astype(F32)
            for i in range(margin // share + 1)
        }
        taps = [table_ref[table.taps + k * SUB : table.taps + (k + 1) * SUB, :] for k in range(15)]
        around = [state[k : k + wide].reshape(many, LANES) for k in range(3)]
        for p in range(frames // 2):
            left_buf[p, 0:many, :] = stack_taps(around, p, group, times)

        def block_one(h):
            linear = [
                jnp.dot(
                    left_buf[p, 0:many, :], lift_weights(h, p, slice(0, 2 * LANES)),
                    preferred_element_type=F32,
                )
                for p in range(frames // 2)
            ]
            yield
            by_tap = bias_taps(h)
            parts = []
            for p in range(frames // 2):
                lanes = slice(2 * p * LANES, 2 * (p + 1) * LANES)
                mixed = linear[p]
                if not hot:
                    every = by_tap[0] + by_tap[1] + by_tap[2]
                    mixed = mixed + jnp.concatenate([every[:, lanes]] * wide, axis=0)
                for j in range(wide):
                    value = mixed[j * times : (j + 1) * times]
                    if j in first_column:
                        value = value - by_tap[0][:, lanes] * first_column[j]
                    if j in last_column:
                        value = value - by_tap[2][:, lanes] * last_column[j]
                    parts.append(value)
            pair = jnp.concatenate(parts, axis=0)
            mean = mean_square(pair)
            yield
            normed = normalise(pair, mean)
            normed_buf[h, 0:cells, :] = by_frame(normed, many)[times : times + cells]
            updates = []
            for p in range(frames // 2):
                both = jnp.concatenate([normed[p * many : (p + 1) * many], left_buf[p, 0:many, :]], axis=1)
                onto = jnp.concatenate(
                    [weight_ref[direct:mixing, :], lift_weights(h, p, slice(2 * LANES, 4 * LANES))], axis=0
                )
                updates.append(jnp.dot(both, onto, preferred_element_type=F32))
            yield
            for p in range(frames // 2):
                fresh[p, 0:many, :] = updates[p]
            yield

        def settle(lines, line):
            for f in range(frames):
                lanes = slice(f % 2 * LANES, (f % 2 + 1) * LANES)
                new = []
                for j in range(wide):
                    value = fresh[f // 2, j * times : (j + 1) * times, lanes]
                    if not hot:
                        value = value + bias
                    value = value.reshape(halves, SUB, LANES)
                    new.append(value * flags[j] if j in flags else value)
                for q in range(cols // 2):
                    d = new[2 * q : 2 * q + 4]
                    lines[f, line, q, 0] = d[0] - d[2]
                    lines[f, line, q, 1] = d[1] + d[2]
                    lines[f, line, q, 2] = d[2] - d[1]
                    lines[f, line, q, 3] = d[1] - d[3]

        def convolve(h, lines, begin, end):
            inside = range(3)
            if isinstance(h, int):
                inside = [a for a in range(3) if 0 <= h + a - 1 < rows]
            for q in range(begin, end):
                spread = []
                for f in range(frames):
                    m = []
                    for i in range(4):
                        terms = [lines[f, a, q, i] * taps[4 * a + i] for a in inside]
                        m.append(functools.reduce(jnp.add, terms))
                    spread.append((m[0] + m[1] + m[2], m[1] - m[2] - m[3]))
                for f in range(frames):
                    for side in range(2):
                        total = None
                        for k in range(3):
                            if 0 <= f + k - 1 < frames:
                                term = spread[f + k - 1][side] * taps[12 + k]
                                total = term if total is None else total + term
                        at = (2 * q + side) * times
                        mixed_buf[lax.rem(h, 2), f, at : at + times, :] = total.reshape(times, LANES)

        def finish(h, slot):
            pair = in_pairs([mixed_buf[slot, f, 0:cells, :] for f in range(frames)])
            mean = mean_square(pair)
            yield
            normed = by_frame(normalise(pair, mean), cells)
            left = jnp.concatenate([normed, normed_buf[h, 0:cells, :]], axis=1)
            out = jnp.dot(left, weight_ref[0:proj, :], preferred_element_type=F32)
            yield
            out = out[:, 0:LANES] + out[:, LANES:]
            acc[0:cells, :] += pltpu.roll(out, h, 1)
            yield

        acc[0:cells, :] = jnp.zeros((cells, LANES), F32)
        pairs = cols // 2

        def receive_next(h):
            if first_time and isinstance(h, int):
                receive(h)
            elif first_time:

                @pl.when(h < rows)
                def _():
                    receive(h)

        def steady(h, carry):
            lines = feats.at[:, pl.ds(h, 3)]
            ending, starting = finish(h - 1, lax.rem(h + 1, 2)), block_one(h + 2)
            settle(lines, 2)
            next(starting)
            next(ending)
            next(starting)
            convolve(h, lines, 0, pairs)
            next(ending)
            next(starting)
            next(ending)
            next(starting)
            receive_next(h + 3)
            return carry

        if first_time:
            receive(0)
            receive(1)
        ahead = block_one(0)
        for _ in ahead:
            pass
        settle(feats, 1)
        for _ in block_one(1):
            pass
        receive_next(2)
        settle(feats, 2)
        starting = block_one(2)
        next(starting)
        convolve(0, feats, 0, pairs)
        for _ in starting:
            pass
        receive_next(3)
        lax.fori_loop(1, rows - 2, steady, 0)
        lines = feats.at[:, pl.ds(rows - 2, 3)]
        settle(lines, 2)
        ending = finish(rows - 3, (rows - 3) % 2)
        next(ending)
        convolve(rows - 2, lines, 0, pairs)
        for _ in ending:
            pass
        ending = finish(rows - 2, (rows - 2) % 2)
        next(ending)
        convolve(rows - 1, feats.at[:, pl.ds(rows - 1, 3)], 0, pairs)
        for _ in ending:
            pass
        for _ in finish(rows - 1, (rows - 1) % 2):
            pass

    def arrived(j):
        if not pieces or j < share:
            return noise_ref[pl.ds(j, times, stride=block), :]
        spare = LANES - used
        lane = lax.broadcasted_iota(jnp.int32, (times, LANES), 1)
        total = jnp.zeros((times, LANES), F32)
        for k in range(pieces):
            piece = noise_ref[pl.ds(2 * HALO * k + j - share, times, stride=block), :]
            piece = pltpu.roll(piece, (k * spare + LANES - used) % LANES, 1)
            total = jnp.where((lane >= k * spare) & (lane < (k + 1) * spare), piece, total)
        return total

    def drift(cols, skip, through):
        f = acc[0 : cols * times, :].reshape(cols, times, LANES) + through + bias_out[None]
        noise = jnp.stack([arrived(skip + j) for j in range(cols)])
        return step * f + (NOISE_SCALE * math.sqrt(step)) * noise

    def running(values):
        when = lax.broadcasted_iota(jnp.int32, values.shape, 1)
        reach = 1
        while reach < times:
            values = values + jnp.where(when >= reach, pltpu.roll(values, reach, 1), 0.0)
            reach *= 2
        return values

    cols = share + 2 * HALO
    for j in range(cols + 4):
        at = table.own + j
        state[j] = jnp.broadcast_to(table_ref[at : at + 1, :], (times, LANES))
    run_network(cols, True)
    begin = table_ref[table.own + HALO : table.own + HALO + cols, :][:, None, :]
    through = table_ref[table.direct + HALO : table.direct + HALO + cols, :][:, None, :]
    moved = drift(cols, 0, through)
    col = lax.broadcasted_iota(jnp.int32, moved.shape, 0) + (index * share - HALO)
    inside = (col >= 0) & (col < columns)
    state[0:cols] = begin + jnp.where(inside, running(moved) - moved, 0.0)

    run_network(share, False)
    hi, lo = split(state[HALO : HALO + share].reshape(share * times, LANES))
    through = jnp.dot(
        jnp.concatenate([hi, lo], axis=1), weight_ref[proj:direct, :], preferred_element_type=F32
    )
    through = (through[:, 0:LANES] + through[:, LANES:]).reshape(share, times, LANES)
    own = table.own + 2 * HALO
    ended = table_ref[own : own + share, :][:, None, :] + running(drift(share, HALO, through))
    kept = returned_block(share, used)[1] * 2 * HALO
    if not kept:
        for j in range(share):
            out_ref[pl.ds(j, times, stride=share), :] = ended[j]
        return
    lane = lax.broadcasted_iota(jnp.int32, (times, LANES), 1)
    for j in range(kept):
        k, i = divmod(j, 2 * HALO)
        moved = pltpu.roll(ended[kept + i], used - k * (LANES - used), 1)
        leaving[pl.ds(j, times, stride=kept), :] = jnp.where(lane < used, ended[j], moved)
    for t in range(times):
        for k in range(kept // (2 * HALO)):
            at = t * kept + k * 2 * HALO
            out_ref[t, k] = leaving[at : at + 2 * HALO, :]


def unpack_kernel(share, sizes, in_ref, out_ref, lines):
    channels, frames, rows, columns = sizes
    used = channels * frames * rows
    pieces = returned_block(share, used)[1]
    if pieces:
        spare = LANES - used
        lane = lax.broadcasted_iota(jnp.int32, (2 * HALO, LANES), 1)
        for sender in range(columns // share):
            last = jnp.zeros((2 * HALO, LANES), F32)
            for k in range(pieces):
                at = sender * share + k * 2 * HALO
                block = in_ref[sender, k]
                lines[at : at + 2 * HALO, :] = block
                piece = pltpu.roll(block, (k * spare + LANES - used) % LANES, 1)
                last = jnp.where((lane >= k * spare) & (lane < (k + 1) * spare), piece, last)
            at = (sender + 1) * share - 2 * HALO
            lines[at : at + 2 * HALO, :] = last
        image = jnp.transpose(lines[...])
    else:
        image = jnp.transpose(in_ref[...])
    for f in range(frames):
        for c in range(channels):
            at = (f * channels + c) * rows
            out_ref[0, c, f] = image[at : at + rows, :]


def shards(start_frames, plan, noise, w_lift, w_time, spatial, temporal, w_point, w_out):
    times = lax.axis_size("tm")
    sizes = start_frames.shape
    channels, frames, rows, columns = sizes
    share = columns // times
    block, pieces = sent_block(share, channels * frames * rows)
    cols = share + 2 * HALO
    table = Table(share, sizes)
    params = limit([])
    codes = 2 * times if one_hot_fits(times, channels * rows) else 0
    mix_shape = (rows - AHEAD, frames // 2, 2 * LANES - codes, 4 * LANES)
    prep_scratch = [pltpu.VMEM(mix_shape, BF16), pltpu.VMEM(sizes, F32)]
    main_scratch = [
        pltpu.VMEM((frames, rows + 2, cols // 2, 4, times // SUB, SUB, LANES), F32),
        pltpu.VMEM((frames // 2, (cols + 2) * times, 2 * LANES), F32),
        pltpu.VMEM((2, frames, cols * times, LANES), F32),
        pltpu.VMEM((rows, cols * times, frames * LANES), BF16),
        pltpu.VMEM((cols * times, LANES), F32),
        pltpu.VMEM((cols + 4, times, LANES), F32),
        pltpu.VMEM((frames // 2, (cols + 2) * times, 2 * LANES), BF16),
        pltpu.VMEM(mix_shape, BF16),
        pltpu.VMEM((rows, frames // 2, max(codes, 16), 4 * LANES), BF16),
        pltpu.VMEM((times * share, LANES), F32),
    ]
    index = lax.axis_index("tm").astype(jnp.int32).reshape(1)
    hbm = whole(pltpu.HBM)

    packed = pl.pallas_call(
        functools.partial(pack_kernel, times, share),
        out_shape=pltpu.VMEM((times, block, LANES), F32),
        in_specs=[whole(pltpu.SMEM), whole()],
        out_specs=whole(),
        scratch_shapes=[
            pltpu.VMEM((columns + 2 * SUB, LANES), F32),
            pltpu.VMEM((max(pieces, 1), columns + 2 * SUB, LANES), F32),
        ],
        compiler_params=params,
        name="pack",
    )(plan, noise)
    arrived = lax.all_to_all(packed, "tm", split_axis=0, concat_axis=0, tiled=True)

    by_tap = (
        w_lift, jnp.transpose(spatial, (2, 0, 1)), jnp.transpose(temporal, (2, 0, 1)), w_point,
        jnp.transpose(w_out),
    )
    first, mix, lines, weights = pl.pallas_call(
        functools.partial(prep_kernel, share, sizes),
        out_shape=[
            pltpu.VMEM((AHEAD,) + mix_shape[1:], BF16),
            pltpu.HBM(mix_shape, BF16),
            pltpu.VMEM((table.size, LANES), F32),
            pltpu.VMEM((weight_rows(frames)[-1], 2 * LANES), BF16),
        ],
        in_specs=[whole(pltpu.SMEM)] + [hbm] * 6,
        out_specs=[whole(), hbm, whole(), whole()],
        scratch_shapes=prep_scratch
        + [pltpu.VMEM(a.shape, a.dtype) for a in by_tap]
        + [
            pltpu.VMEM((columns + 4 * SUB + table.wide, LANES), F32),
            pltpu.SemaphoreType.DMA((7,)),
        ],
        compiler_params=limit(prep_scratch),
        cost_estimate=pl.CostEstimate(flops=10**9, bytes_accessed=10**7, transcendentals=0),
        name="prep",
    )(index, *[in_hbm(a) for a in (start_frames,) + by_tap])

    shape, packed_back = returned_block(share, channels * frames * rows)
    result_shape = (times,) + shape if packed_back else (times * share, LANES)
    result = pl.pallas_call(
        functools.partial(main_kernel, share, sizes, times),
        out_shape=jax.ShapeDtypeStruct(result_shape, F32),
        in_specs=[whole(pltpu.SMEM), whole(), whole(), whole(), hbm, whole(), whole()],
        out_specs=whole(),
        scratch_shapes=main_scratch + [pltpu.SemaphoreType.DMA((rows - AHEAD,))],
        compiler_params=limit(main_scratch),
        name="sampler",
    )(index, arrived.reshape(times * block, LANES), w_time, first, in_hbm(mix), lines, weights)
    back = lax.all_to_all(
        result.reshape((times,) + shape), "tm", split_axis=0, concat_axis=0, tiled=True
    )
    return pl.pallas_call(
        functools.partial(unpack_kernel, share, sizes),
        out_shape=jax.ShapeDtypeStruct((1,) + sizes, F32),
        in_specs=[whole()],
        out_specs=whole(),
        scratch_shapes=[pltpu.VMEM((columns, LANES), F32)],
        compiler_params=params,
        name="unpack",
    )(back if packed_back else back.reshape(columns, LANES))


def solution(mesh):
    in_specs = (
        P("groups", None, None, None),
        P(("groups", "tm")),
        P("tm", "groups", None, None, None),
        P(),
        P(),
        P(),
        P(),
        P(),
        P(),
    )
    out_specs = P("tm", "groups", None, None, None)
    return jax.shard_map(shards, mesh=mesh, in_specs=in_specs, out_specs=out_specs, check_vma=False)
```
